32 devices in a mesh: tower: 2 (over core), rows: 16 (over z, y, x).
Axes of the slice: x: 2, y: 2, z: 4, core: 2. Of those that a mesh axis runs over, the one named last changes fastest.
Arguments:
- tokens: bfloat16 [2, 32, 512, 512], P('tower', 'rows'), may hold values from -9 to 9
- segment_ids: int32 [2, 32, 512], P('tower', 'rows'), may hold values from 0 to 8, never falling along the last dimension, each value on 1 to 128 neighbouring positions
- positives: int32 [256], P('rows'), may hold values from 0 to 255, each once
- attention_gain: float32 [512], replicated, may hold values from 0.5 to 1.5
- query_weight: bfloat16 [512, 512], replicated, may hold values from -0.0625 to 0.0625
- key_weight: bfloat16 [512, 512], replicated, may hold values from -0.25 to 0.25
- value_weight: bfloat16 [512, 512], replicated, may hold values from -0.25 to 0.25
- output_weight: bfloat16 [512, 512], replicated, may hold values from -1 to 1
- position_table: float32 [32, 8], replicated, may hold values from -3 to 3
- feedforward_gain: float32 [512], replicated, may hold values from 0.5 to 1.5
- inner_weight: bfloat16 [512, 2048], replicated, may hold values from -0.25 to 0.25
- outer_weight: bfloat16 [2048, 512], replicated, may hold values from -0.1875 to 0.1875
Outputs:
- layer_output: bfloat16 [2, 32, 512, 512], P('tower', 'rows')
- token_grad: bfloat16 [2, 32, 512, 512], P('tower', 'rows')
- attention_gain_grad: float32 [512], replicated
- query_grad: float32 [512, 512], replicated
- key_grad: float32 [512, 512], replicated
- value_grad: float32 [512, 512], replicated
- output_grad: float32 [512, 512], replicated
- position_grad: float32 [32, 8], replicated
- feedforward_gain_grad: float32 [512], replicated
- inner_grad: float32 [512, 2048], replicated
- outer_grad: float32 [2048, 512], replicated
- contrastive_loss: float32 [], replicated
- root_mean_squares: float32 [3], replicated
The draws below stay inside these ranges and needn't reach their ends.
Inputs may be any that keep to these rules, and one draw needn't show every extreme that they name: `segment_ids`: within each row of 512 tokens the numbers never fall; 0 to 7 are the row's items and 8 marks the padding at its end; every number, padding included, covers 1 to 128 tokens. positives[m] is the document item paired with query item m; every document item occurs once.
All inputs are finite; a program needn't handle non-finite values.
Results may differ from the reference program's by a relative error of at most 0.028.
The reference program's roundings to bfloat16 on the way count: a program that leaves them out, or rounds other values in their place, can miss the bound.
Values sent between devices are 32-bit elements; how exact they have to be, the bound alone decides.
A program may use at most 320 MiB of HBM per device.

```python
import math
import jax
import jax.numpy as jnp
import numpy as np
from jax import lax

D = 512
HEADS = 8
HEAD_DIM = 64
FF = 2048
BUCKETS = 32
MAX_DIST = 128
SEQ = 512
ITEMS_ROW = 8
SEG_MOST = 128
INNER = 512
ROWS = 32
NITEMS = 256


def draw_tokens(key, part):
    noise_key = jax.random.fold_in(key, 11)
    shared_key = jax.random.fold_in(key, 12)
    row_place = jnp.arange(ROWS, dtype=jnp.float32) / max(ROWS - 1, 1)
    tower_scale = jnp.array([0.75, 1.5], jnp.float32)
    spread = jnp.exp(jnp.log(0.6) + jnp.log(3.0) * row_place)
    values = jnp.clip(jax.random.normal(noise_key, (2, ROWS, SEQ, D), jnp.float32), -3.0, 3.0)
    shared = jnp.clip(jax.random.normal(shared_key, (D,), jnp.float32), -3.5, 3.5) * 0.1
    scaled = values * spread[None, :, None, None] * tower_scale[:, None, None, None] + shared[None, None, None, :]
    return scaled.astype(jnp.bfloat16)


def length_profile(amount, total, limit, slope):
    portions = [(1 << 20) // math.isqrt(rank ** slope) + 1 for rank in range(2, amount + 1)]
    spare, given = total - limit - (amount - 1), [1] * (amount - 1)
    while spare > 0:
        movable = [i for i in range(amount - 1) if given[i] < limit]
        whole, remaining = sum([portions[i] for i in movable]), spare
        for i in movable:
            extra = min(limit - given[i], max(1, remaining * portions[i] // whole), spare)
            given[i] = given[i] + extra
            spare = spare - extra
    return np.array([limit] + given)


def ragged_sizes(stream_key, number_of, total, bound, skew):
    if number_of == 2:
        one = jax.random.randint(stream_key, (), max(1, total - bound), min(bound, total - 1) + 1)
        return jnp.stack([one, total - one])
    sizes = jnp.asarray(length_profile(number_of, total, bound, skew), jnp.int32)
    twos = (number_of - 1) // 2
    source_of, sink = sizes[1:1 + 2 * twos:2], sizes[2:2 + 2 * twos:2]
    margin = jnp.minimum(source_of - 1, bound - sink)
    moved = jax.random.randint(jax.random.fold_in(stream_key, 1), (twos,), 0, 1 << 20) % (margin + 1)
    sizes = sizes.at[1:1 + 2 * twos:2].set(source_of - moved).at[2:2 + 2 * twos:2].set(sink + moved)
    return sizes[jax.random.permutation(jax.random.fold_in(stream_key, 2), number_of)]


def bell_draw(stream_key, shape, scale, limit, kind=jnp.bfloat16):
    return jnp.clip(scale * jax.random.normal(stream_key, shape, jnp.float32), -limit, limit).astype(kind)


def setup_inputs(seed: int = 0) -> dict:
    arg_keys = jax.random.split(jax.random.key(seed), 13)
    return {
        "tokens": draw_tokens(jax.random.fold_in(arg_keys[12], 71), 0),
        "segment_ids": jax.vmap(lambda own: jnp.searchsorted(jnp.cumsum(ragged_sizes(own, ITEMS_ROW + 1, SEQ, SEG_MOST, 2)), jnp.arange(SEQ), side="right"))(jax.random.split(arg_keys[1], 2 * ROWS)).reshape((2, ROWS, SEQ)).astype(jnp.int32),
        "positives": jax.random.permutation(arg_keys[2], NITEMS).astype(jnp.int32),
        "attention_gain": jnp.clip(1.0 + 0.1 * jax.random.normal(arg_keys[3], (D,), jnp.float32), 0.5, 1.5),
        "query_weight": bell_draw(arg_keys[4], (D, INNER), (16 * D) ** -0.5, 0.0625),
        "key_weight": bell_draw(arg_keys[5], (D, INNER), D ** -0.5, 0.25),
        "value_weight": bell_draw(arg_keys[6], (D, INNER), D ** -0.5, 0.25),
        "output_weight": bell_draw(arg_keys[7], (INNER, D), (INNER // 16) ** -0.5, 1.0),
        "position_table": bell_draw(arg_keys[8], (BUCKETS, HEADS), 0.5, 3.0, jnp.float32),
        "feedforward_gain": jnp.clip(1.0 + 0.1 * jax.random.normal(arg_keys[9], (D,), jnp.float32), 0.5, 1.5),
        "inner_weight": bell_draw(arg_keys[10], (D, FF), D ** -0.5, 0.25),
        "outer_weight": bell_draw(arg_keys[11], (FF, D), (FF // 2) ** -0.5, 0.1875),
    }


EPSILON = 1e-06
SOFTMAX_TEMP = 0.01
LOSS_SCALE = 65536.0
MATMUL_PRECISION = lax.Precision.HIGHEST

@jax.custom_vjp
def low(v):
    return lax.optimization_barrier(v.astype(jnp.bfloat16)).astype(jnp.float32)

@jax.custom_vjp
def low_back(v):
    return v

def low_keep(v):
    return (low(v), None)

def low_pass(kept, grad):
    return (grad,)

def back_keep(v):
    return (v, None)

def back_low(kept, grad):
    return (low(grad),)
low.defvjp(low_keep, low_pass)
low_back.defvjp(back_keep, back_low)

def bucket_table(length, bucket_count, far_limit):
    half_count = bucket_count // 2
    exact_count = half_count // 2
    entries = []
    for offset in range(1 - length, length):
        distance = abs(offset)
        if distance < exact_count:
            within = distance
        else:
            within = exact_count + int(math.log(distance / exact_count) / math.log(far_limit / exact_count) * (half_count - exact_count))
            within = min(within, half_count - 1)
        entries.append(within + (half_count if offset > 0 else 0))
    by_offset = np.array(entries, dtype=np.int32)
    index_grid = np.arange(length)[None, :] - np.arange(length)[:, None] + length - 1
    return (by_offset, by_offset[index_grid])

def reference(tokens, segment_ids, positives, attention_gain, query_weight, key_weight, value_weight, output_weight, position_table, feedforward_gain, inner_weight, outer_weight):
    by_offset, bucket_index = bucket_table(SEQ, BUCKETS, MAX_DIST)
    bucket_grid = jnp.asarray(bucket_index)
    params = (attention_gain.astype(jnp.float32), query_weight.astype(jnp.float32), key_weight.astype(jnp.float32), value_weight.astype(jnp.float32), output_weight.astype(jnp.float32), position_table.astype(jnp.float32), feedforward_gain.astype(jnp.float32), inner_weight.astype(jnp.float32), outer_weight.astype(jnp.float32))
    flat_tokens = tokens.astype(jnp.float32).reshape(2 * ROWS, SEQ, D)
    flat_segments = segment_ids.reshape(2 * ROWS, SEQ)

    def objective(token_values, weights_all):
        gain_first, query_matrix, key_matrix, value_matrix, output_matrix, bucket_values, gain_second, inner_matrix, outer_matrix = weights_all

        def one_row(row_tokens, row_segments):
            scale_one = lax.rsqrt(lax.optimization_barrier(jnp.mean(row_tokens * row_tokens, axis=1, keepdims=True)) + EPSILON)
            normed_one = low(row_tokens * scale_one * gain_first)
            query_vectors = low_back(low(jnp.dot(normed_one, query_matrix, precision=MATMUL_PRECISION)))
            key_vectors = low_back(low(jnp.dot(normed_one, key_matrix, precision=MATMUL_PRECISION)))
            value_vectors = low_back(low(jnp.dot(normed_one, value_matrix, precision=MATMUL_PRECISION)))
            query_heads = query_vectors.reshape(SEQ, HEADS, HEAD_DIM)
            key_heads = key_vectors.reshape(SEQ, HEADS, HEAD_DIM)
            value_heads = value_vectors.reshape(SEQ, HEADS, HEAD_DIM)
            position_bias = jnp.take(bucket_values.T, bucket_grid, axis=1)
            scores = jnp.einsum('qhd,khd->hqk', query_heads, key_heads, precision=MATMUL_PRECISION) + position_bias
            scores = low_back(scores)
            same_item = row_segments[:, None] == row_segments[None, :]
            scores = jnp.where(same_item[None], scores, -1e+30)
            attention_probs = low(jax.nn.softmax(scores, axis=-1))
            mixed_heads = jnp.einsum('hqk,khd->qhd', attention_probs, value_heads, precision=MATMUL_PRECISION)
            mixed_rows = low_back(low(mixed_heads.reshape(SEQ, INNER)))
            branch_one = low_back(jnp.dot(mixed_rows, output_matrix, precision=MATMUL_PRECISION))
            middle = row_tokens + branch_one
            scale_two = lax.rsqrt(lax.optimization_barrier(jnp.mean(middle * middle, axis=1, keepdims=True)) + EPSILON)
            normed_two = low(middle * scale_two * gain_second)
            hidden = low(jax.nn.relu(low_back(jnp.dot(normed_two, inner_matrix, precision=MATMUL_PRECISION))))
            branch_two = low_back(jnp.dot(hidden, outer_matrix, precision=MATMUL_PRECISION))
            result = middle + branch_two
            valid_mask = (row_segments < ITEMS_ROW).astype(jnp.float32)[:, None]
            member = (row_segments[None, :] == jnp.arange(ITEMS_ROW)[:, None]).astype(jnp.float32)
            pooled = jnp.dot(member, result, precision=MATMUL_PRECISION) / lax.optimization_barrier(jnp.sum(member, axis=1, keepdims=True))
            squares = jnp.stack([jnp.sum(valid_mask * result * result), jnp.sum(valid_mask * branch_one * branch_one), jnp.sum(valid_mask * branch_two * branch_two), jnp.sum(valid_mask)])
            return (pooled, squares, result)
        checked_row = jax.checkpoint(one_row)
        pooled, squares, result = lax.map(lambda packed: checked_row(packed[0], packed[1]), (token_values, flat_segments))
        pooled = pooled.reshape(2, NITEMS, D)
        embedded_tokens = pooled * lax.rsqrt(lax.optimization_barrier(jnp.sum(pooled * pooled, axis=2, keepdims=True)) + EPSILON)
        similarity_scores = jnp.dot(embedded_tokens[0], embedded_tokens[1].T, precision=MATMUL_PRECISION) / SOFTMAX_TEMP
        highest = lax.optimization_barrier(jnp.max(similarity_scores, axis=1, keepdims=True))
        log_total = highest[:, 0] + jnp.log(lax.optimization_barrier(jnp.sum(jnp.exp(similarity_scores - highest), axis=1)))
        picked = jnp.arange(NITEMS)[None, :] == positives[:, None]
        target = lax.optimization_barrier(jnp.sum(jnp.where(picked, similarity_scores, 0.0), axis=1))
        loss_value = jnp.mean(log_total - target)
        return (loss_value, (result, squares))
    loss_value, pullback, auxiliary = jax.vjp(objective, flat_tokens, params, has_aux=True)
    token_grad, weight_grads = pullback(jnp.ones_like(loss_value) * LOSS_SCALE)
    result_all, squares_all = auxiliary
    layer_output = result_all.astype(jnp.bfloat16).reshape(2, ROWS, SEQ, D)
    totals = lax.optimization_barrier(jnp.sum(squares_all, axis=0))
    root_mean_squares = jnp.sqrt(totals[:3] / (totals[3] * D))
    return (layer_output, token_grad.astype(jnp.bfloat16).reshape(2, ROWS, SEQ, D), weight_grads[0], weight_grads[1], weight_grads[2], weight_grads[3], weight_grads[4], weight_grads[5], weight_grads[6], weight_grads[7], weight_grads[8], loss_value, root_mean_squares)
```

```python
import functools
import math

import jax
import jax.numpy as jnp
import numpy as np
from jax import lax
from jax.experimental import pallas as pl
from jax.experimental.pallas import tpu as pltpu
from jax.sharding import PartitionSpec as P

MAX_DIST = 128
ITEMS_ROW = 8


EPSILON = 1e-06
SOFTMAX_TEMP = 0.01
LOSS_SCALE = 65536.0
MATMUL_PRECISION = lax.Precision.HIGHEST


def from_partner(value, axis, apart):
    mask = 2**apart
    pairs = [(source, source ^ mask) for source in range(lax.axis_size(axis))]
    return lax.ppermute(value, axis, pairs)


def bucket_table(length, bucket_count, far_limit):
    half_count = bucket_count // 2
    exact_count = half_count // 2
    entries = []
    for offset in range(1 - length, length):
        distance = abs(offset)
        if distance < exact_count:
            within = distance
        else:
            within = exact_count + int(
                math.log(distance / exact_count)
                / math.log(far_limit / exact_count)
                * (half_count - exact_count)
            )
            within = min(within, half_count - 1)
        entries.append(within + (half_count if offset > 0 else 0))
    by_offset = np.array(entries, dtype=np.int32)
    index_grid = np.arange(length)[None, :] - np.arange(length)[:, None] + length - 1
    return (by_offset, by_offset[index_grid])


def contract_rows(left_side, right_side):
    return lax.dot_general(
        left_side, right_side, (((0,), (0,)), ((), ())), preferred_element_type=jnp.float32
    )


def times_transpose(left_side, right_side):
    return lax.dot_general(
        left_side, right_side, (((1,), (1,)), ((), ())), preferred_element_type=jnp.float32
    )


def norm_scale(values):
    return lax.rsqrt(jnp.mean(values * values, axis=1, keepdims=True) + EPSILON)


def norm_back(grad_normed, values, scale, gain):
    gained = grad_normed * gain
    return scale * (
        gained - values * scale * scale * jnp.mean(gained * values, axis=1, keepdims=True)
    )


def row_scores(query_part, key_part, segment_row, position_bias, head_count):
    length = query_part.shape[0]
    query_heads = query_part.reshape(length, head_count, -1)
    key_heads = key_part.reshape(length, head_count, -1)
    scores = (
        jnp.einsum("qhd,khd->hqk", query_heads, key_heads, preferred_element_type=jnp.float32)
        + position_bias
    )
    same_item = segment_row[:, None] == segment_row[None, :]
    return jnp.where(same_item[None], scores, -1e30)


def diagonal_sums(square):
    head_count = square.shape[0]
    length = square.shape[1]
    flipped = square[:, :, ::-1]
    padded = jnp.pad(flipped, ((0, 0), (0, 0), (0, length)))
    sheared = padded.reshape(head_count, 2 * length * length)[:, : length * (2 * length - 1)]
    sheared = sheared.reshape(head_count, length, 2 * length - 1)
    return jnp.sum(sheared, axis=1)[:, ::-1]


def shards(
    tokens,
    segment_ids,
    positives,
    attention_gain,
    query_weight,
    key_weight,
    value_weight,
    output_weight,
    position_table,
    feedforward_gain,
    inner_weight,
    outer_weight,
):
    row_count = tokens.shape[1]
    length = tokens.shape[2]
    model_width = tokens.shape[3]
    head_count = position_table.shape[1]
    inner_width = query_weight.shape[1]
    head_size = inner_width // head_count
    token_count = row_count * length
    by_offset, bucket_index = bucket_table(length, position_table.shape[0], MAX_DIST)
    position_bias = jnp.take(position_table.T, jnp.asarray(bucket_index), axis=1)
    inputs = tokens.reshape(token_count, model_width).astype(jnp.float32)
    segments = segment_ids.reshape(row_count, length)
    scale_one = norm_scale(inputs)
    normed_one = (inputs * scale_one * attention_gain).astype(jnp.bfloat16)
    query_rows = jnp.dot(normed_one, query_weight, preferred_element_type=jnp.float32).astype(
        jnp.bfloat16
    )
    key_rows = jnp.dot(normed_one, key_weight, preferred_element_type=jnp.float32).astype(
        jnp.bfloat16
    )
    value_rows = jnp.dot(normed_one, value_weight, preferred_element_type=jnp.float32).astype(
        jnp.bfloat16
    )
    query_blocks = query_rows.reshape(row_count, length, inner_width)
    key_blocks = key_rows.reshape(row_count, length, inner_width)
    value_blocks = value_rows.reshape(row_count, length, inner_width)

    def attend(packed):
        query_part, key_part, value_part, segment_row = packed
        scores = row_scores(query_part, key_part, segment_row, position_bias, head_count)
        highest = jnp.max(scores, axis=2, keepdims=True)
        exp_scores = jnp.exp(scores - highest)
        exp_total = jnp.sum(exp_scores, axis=2, keepdims=True)
        attention_probs = (exp_scores / exp_total).astype(jnp.bfloat16)
        value_heads = value_part.reshape(length, head_count, head_size)
        mixed_heads = jnp.einsum(
            "hqk,khd->qhd", attention_probs, value_heads, preferred_element_type=jnp.float32
        )
        return (
            mixed_heads.reshape(length, inner_width).astype(jnp.bfloat16),
            (highest + jnp.log(exp_total))[:, :, 0],
        )

    mixed_blocks, log_totals = lax.map(attend, (query_blocks, key_blocks, value_blocks, segments))
    mixed_rows = mixed_blocks.reshape(token_count, inner_width)
    branch_one = jnp.dot(mixed_rows, output_weight, preferred_element_type=jnp.float32)
    middle = inputs + branch_one
    scale_two = norm_scale(middle)
    normed_two = (middle * scale_two * feedforward_gain).astype(jnp.bfloat16)
    hidden = jax.nn.relu(
        jnp.dot(normed_two, inner_weight, preferred_element_type=jnp.float32)
    ).astype(jnp.bfloat16)
    branch_two = jnp.dot(hidden, outer_weight, preferred_element_type=jnp.float32)
    result = middle + branch_two
    valid_mask = (segments < ITEMS_ROW).astype(jnp.float32).reshape(token_count, 1)
    stat_terms = jnp.stack(
        [
            jnp.sum(valid_mask * result * result),
            jnp.sum(valid_mask * branch_one * branch_one),
            jnp.sum(valid_mask * branch_two * branch_two),
            jnp.sum(valid_mask),
        ]
    )
    stat_totals = lax.psum(stat_terms, ("tower", "rows"))
    member = (segments[:, None, :] == jnp.arange(ITEMS_ROW)[None, :, None]).astype(jnp.float32)
    item_sizes = jnp.sum(member, axis=2, keepdims=True)
    result_blocks = result.reshape(row_count, length, model_width)
    pooled = (
        jnp.einsum("ris,rsd->rid", member, result_blocks, precision=MATMUL_PRECISION) / item_sizes
    )
    items_here = row_count * ITEMS_ROW
    pooled = pooled.reshape(items_here, model_width)
    inverse_norm = lax.rsqrt(jnp.sum(pooled * pooled, axis=1, keepdims=True) + EPSILON)
    embedded_tokens = pooled * inverse_norm
    tower_index = lax.axis_index("tower")
    is_query = tower_index == 0
    partner = from_partner(embedded_tokens, "tower", 0)
    query_vectors = jnp.where(is_query, embedded_tokens, partner)
    document_vectors = jnp.where(is_query, partner, embedded_tokens)
    gathered_documents = lax.all_gather(document_vectors, "rows", axis=0, tiled=True)
    item_total = gathered_documents.shape[0]
    half_items = items_here // 2
    my_queries = lax.dynamic_slice_in_dim(query_vectors, tower_index * half_items, half_items, 0)
    my_targets = lax.dynamic_slice_in_dim(positives, tower_index * half_items, half_items, 0)
    similarity_scores = (
        lax.dot_general(
            my_queries,
            gathered_documents,
            (((1,), (1,)), ((), ())),
            precision=MATMUL_PRECISION,
            preferred_element_type=jnp.float32,
        )
        / SOFTMAX_TEMP
    )
    highest = jnp.max(similarity_scores, axis=1, keepdims=True)
    exp_logits = jnp.exp(similarity_scores - highest)
    exp_total = jnp.sum(exp_logits, axis=1, keepdims=True)
    log_total = highest[:, 0] + jnp.log(exp_total[:, 0])
    is_target = jnp.arange(item_total)[None, :] == my_targets[:, None]
    target = jnp.sum(jnp.where(is_target, similarity_scores, 0.0), axis=1)
    loss_part = jnp.sum(log_total - target)
    similarity_gradient = (exp_logits / exp_total - is_target.astype(jnp.float32)) * (
        LOSS_SCALE / item_total
    )
    local_gradient = (
        jnp.dot(similarity_gradient, gathered_documents, precision=MATMUL_PRECISION) / SOFTMAX_TEMP
    )
    grad_documents = lax.psum_scatter(
        lax.dot_general(
            similarity_gradient,
            my_queries,
            (((0,), (0,)), ((), ())),
            precision=MATMUL_PRECISION,
            preferred_element_type=jnp.float32,
        )
        / SOFTMAX_TEMP,
        "rows",
        scatter_dimension=0,
        tiled=True,
    )
    partner_mine, partner_documents = from_partner((local_gradient, grad_documents), "tower", 0)
    query_side = jnp.where(
        is_query,
        jnp.concatenate([local_gradient, partner_mine], 0),
        jnp.concatenate([partner_mine, local_gradient], 0),
    )
    own_grad = jnp.where(is_query, query_side, grad_documents + partner_documents)
    inner_along = jnp.sum(own_grad * embedded_tokens, axis=1, keepdims=True)
    grad_pooled = inverse_norm * (own_grad - embedded_tokens * inner_along)
    per_token = grad_pooled.reshape(row_count, ITEMS_ROW, model_width) / item_sizes
    grad_result = jnp.einsum("ris,rid->rsd", member, per_token, precision=MATMUL_PRECISION).reshape(
        token_count, model_width
    )
    grad_branch_two = grad_result.astype(jnp.bfloat16)
    outer_grad = contract_rows(hidden, grad_branch_two)
    grad_hidden = times_transpose(grad_branch_two, outer_weight)
    grad_pre = jnp.where(hidden > 0, grad_hidden, 0.0).astype(jnp.bfloat16)
    inner_grad = contract_rows(normed_two, grad_pre)
    grad_normed_two = times_transpose(grad_pre, inner_weight)
    feedforward_gain_grad = jnp.sum(grad_normed_two * middle * scale_two, axis=0)
    grad_middle = grad_result + norm_back(grad_normed_two, middle, scale_two, feedforward_gain)
    grad_branch_one = grad_middle.astype(jnp.bfloat16)
    output_grad = contract_rows(mixed_rows, grad_branch_one)
    grad_mixed = times_transpose(grad_branch_one, output_weight).astype(jnp.bfloat16)
    grad_mixed_blocks = grad_mixed.reshape(row_count, length, inner_width)

    def attend_back(running, packed):
        query_part, key_part, value_part, segment_row, row_log_total, grad_part = packed
        scores = row_scores(query_part, key_part, segment_row, position_bias, head_count)
        attention_probs = jnp.exp(scores - row_log_total[:, :, None])
        query_heads = query_part.reshape(length, head_count, head_size)
        key_heads = key_part.reshape(length, head_count, head_size)
        value_heads = value_part.reshape(length, head_count, head_size)
        grad_heads = grad_part.reshape(length, head_count, head_size)
        grad_value = jnp.einsum(
            "hqk,qhd->khd",
            attention_probs.astype(jnp.bfloat16),
            grad_heads,
            preferred_element_type=jnp.float32,
        )
        grad_probs = jnp.einsum(
            "qhd,khd->hqk", grad_heads, value_heads, preferred_element_type=jnp.float32
        )
        row_dot = jnp.sum(attention_probs * grad_probs, axis=2, keepdims=True)
        grad_scores = (attention_probs * (grad_probs - row_dot)).astype(jnp.bfloat16)
        grad_query = jnp.einsum(
            "hqk,khd->qhd", grad_scores, key_heads, preferred_element_type=jnp.float32
        )
        grad_key = jnp.einsum(
            "hqk,qhd->khd", grad_scores, query_heads, preferred_element_type=jnp.float32
        )
        outputs = (
            grad_query.reshape(length, inner_width).astype(jnp.bfloat16),
            grad_key.reshape(length, inner_width).astype(jnp.bfloat16),
            grad_value.reshape(length, inner_width).astype(jnp.bfloat16),
        )
        return (running + grad_scores.astype(jnp.float32), outputs)

    score_sum, grad_rows = lax.scan(
        attend_back,
        jnp.zeros((head_count, length, length), jnp.float32),
        (query_blocks, key_blocks, value_blocks, segments, log_totals, grad_mixed_blocks),
    )
    grad_queries = grad_rows[0].reshape(token_count, inner_width)
    grad_keys = grad_rows[1].reshape(token_count, inner_width)
    grad_values = grad_rows[2].reshape(token_count, inner_width)
    query_grad = contract_rows(normed_one, grad_queries)
    key_grad = contract_rows(normed_one, grad_keys)
    value_grad = contract_rows(normed_one, grad_values)
    grad_normed_one = (
        times_transpose(grad_queries, query_weight)
        + times_transpose(grad_keys, key_weight)
        + times_transpose(grad_values, value_weight)
    )
    attention_gain_grad = jnp.sum(grad_normed_one * inputs * scale_one, axis=0)
    token_grad = grad_middle + norm_back(grad_normed_one, inputs, scale_one, attention_gain)
    offset_onehot = jnp.asarray(
        (by_offset[:, None] == np.arange(position_table.shape[0])[None, :]).astype(np.float32)
    )
    position_grad = jnp.dot(diagonal_sums(score_sum), offset_onehot, precision=MATMUL_PRECISION).T
    closing_terms = loss_part[None]
    summed = lax.psum(
        (
            attention_gain_grad,
            query_grad,
            key_grad,
            value_grad,
            output_grad,
            position_grad,
            feedforward_gain_grad,
            inner_grad,
            outer_grad,
            closing_terms,
        ),
        ("tower", "rows"),
    )
    (
        attention_gain_grad,
        query_grad,
        key_grad,
        value_grad,
        output_grad,
        position_grad,
        feedforward_gain_grad,
        inner_grad,
        outer_grad,
        closing_totals,
    ) = summed
    contrastive_loss = closing_totals[0] / item_total
    root_mean_squares = jnp.sqrt(stat_totals[:3] / (stat_totals[3] * model_width))
    block_shape = (1, row_count, length, model_width)
    return (
        result.reshape(block_shape).astype(jnp.bfloat16),
        token_grad.reshape(block_shape).astype(jnp.bfloat16),
        attention_gain_grad,
        query_grad,
        key_grad,
        value_grad,
        output_grad,
        position_grad,
        feedforward_gain_grad,
        inner_grad,
        outer_grad,
        contrastive_loss,
        root_mean_squares,
    )


F32 = jnp.float32
BF = jnp.bfloat16
MESH = pl.DeviceIdType.MESH
NN = (((1,), (0,)), ((), ()))
NT = (((1,), (1,)), ((), ()))
TN = (((0,), (0,)), ((), ()))
UNITS = 16
HALVES = (256, 128, 64, 32, 16)
OFFSETS = (0, 256, 384, 448, 480)
FAR = 768
NEAR = 640


def dot(a, b, dims=NN):
    return lax.dot_general(a, b, dims, preferred_element_type=F32)


def exact_dot(a, b, dims=NN):
    return lax.dot_general(
        a, b, dims, precision=lax.Precision.HIGHEST, preferred_element_type=F32
    )


def tile(index, size):
    return pl.ds(pl.multiple_of(index * size, size), size)


def far_limits(bucket_count, far_limit):
    half_count = bucket_count // 2
    exact_count = half_count // 2
    limits = []
    reached = exact_count
    for distance in range(exact_count, 512):
        within = exact_count + int(
            math.log(distance / exact_count)
            / math.log(far_limit / exact_count)
            * (half_count - exact_count)
        )
        within = min(within, half_count - 1)
        while reached < within:
            limits.append(distance)
            reached += 1
    return limits


def bucket_onehot(offset):
    distance = jnp.abs(offset)
    far = jnp.full_like(distance, 8)
    for limit in far_limits(32, MAX_DIST):
        far = far + jnp.where(distance >= limit, 1, 0)
    bucket = jnp.where(distance < 8, distance, far) + jnp.where(offset > 0, 16, 0)
    same = bucket == lax.broadcasted_iota(jnp.int32, (32, FAR), 0)
    return jnp.where(same, 1.0, 0.0).astype(F32)


def split_three(value):
    high = value.astype(BF)
    rest = value - high.astype(F32)
    middle = rest.astype(BF)
    return high, middle, (rest - middle.astype(F32)).astype(BF)


class Place:
    def __init__(self):
        self.tower = lax.axis_index("tower")
        self.rows = lax.axis_index("rows")
        self.flat = lax.rem(self.rows, 4)
        self.deep = lax.div(self.rows, 4)
        bits = {
            "x": lax.rem(self.rows, 2),
            "y": lax.rem(lax.div(self.rows, 2), 2),
            "z": lax.rem(lax.div(self.rows, 4), 2),
            "w": lax.div(self.rows, 8),
        }
        steps = {"x": 1, "y": 2, "z": 4, "w": 8}
        self.bit = {"c": self.tower, **bits}
        self.to = {"c": self.device(1 - self.tower, self.rows)}
        for name, step in steps.items():
            self.to[name] = self.device(self.tower, self.rows + step * (1 - 2 * bits[name]))

    def device(self, tower, rows):
        return {"tower": tower, "rows": rows}

    def along_deep(self, step):
        return self.device(self.tower, lax.rem(self.deep + step, 4) * 4 + self.flat)

    def along_flat(self, step):
        return self.device(self.tower, self.deep * 4 + lax.rem(self.flat + step, 4))


class Sums:
    ORDERS = (("c", "x", "z", "y", "w"), ("c", "y", "z", "x", "w"))

    def __init__(self, place, total, landed, out, send_sem, recv_sem, out_sem):
        self.place, self.total, self.landed, self.out = place, total, landed, out
        self.send_sem, self.recv_sem, self.out_sem = send_sem, recv_sem, out_sem
        self.bases = []
        for order in self.ORDERS:
            base, bases = 0, [0]
            for name, half in zip(order, HALVES):
                base = base + place.bit[name] * half
                bases.append(base)
            self.bases.append(bases)
        self.active = []

    def halve(self, k, unit):
        order, bases, half = self.ORDERS[unit % 2], self.bases[unit % 2], HALVES[k]
        name = order[k]
        start = pl.multiple_of(bases[k] + (1 - self.place.bit[name]) * half, half)
        return pltpu.make_async_remote_copy(
            src_ref=self.total.at[unit, pl.ds(start, half)],
            dst_ref=self.landed.at[unit, pl.ds(OFFSETS[k], half)],
            send_sem=self.send_sem.at[k, unit],
            recv_sem=self.recv_sem.at[k, unit],
            device_id=self.place.to[name],
            device_id_type=MESH,
        )

    def own(self, k, unit):
        return pl.ds(pl.multiple_of(self.bases[unit % 2][k + 1], HALVES[k]), HALVES[k])

    def double(self, k, unit):
        rows = self.own(k, unit)
        source = self.total if k == 4 else self.out
        return pltpu.make_async_remote_copy(
            src_ref=source.at[unit, rows],
            dst_ref=self.out.at[unit, rows],
            send_sem=self.send_sem.at[9 - k, unit],
            recv_sem=self.recv_sem.at[9 - k, unit],
            device_id=self.place.to[self.ORDERS[unit % 2][k]],
            device_id_type=MESH,
        )

    def keep(self, unit):
        rows = self.own(4, unit)
        return pltpu.make_async_copy(
            self.total.at[unit, rows], self.out.at[unit, rows], self.out_sem.at[unit]
        )

    def step(self, stage, unit):
        if 1 <= stage <= 5:
            k = stage - 1
            self.halve(k, unit).wait()
            self.total[unit, self.own(k, unit), :] += self.landed[
                unit, pl.ds(OFFSETS[k], HALVES[k]), :
            ]
        elif stage >= 6:
            self.double(10 - stage, unit).wait()
        if stage <= 4:
            self.halve(stage, unit).start()
        elif stage <= 9:
            if stage == 6:
                self.keep(unit).wait()
            self.double(9 - stage, unit).start()
            if stage == 5:
                self.keep(unit).start()

    def start(self, *units):
        for unit in units:
            self.step(0, unit)
        self.active.append([units, 1])

    def tick(self):
        for entry in self.active:
            for unit in entry[0]:
                self.step(entry[1], unit)
            entry[1] += 1
        self.active = [entry for entry in self.active if entry[1] <= 10]

    def finish(self):
        while self.active:
            self.tick()


class Spread:
    def __init__(self, place, blocks, send_sem, recv_sem):
        self.place, self.blocks = place, blocks
        self.send_sem, self.recv_sem = send_sem, recv_sem

    def copy(self, row, index, where, device):
        ref = self.blocks.at[where]
        return pltpu.make_async_remote_copy(
            src_ref=ref,
            dst_ref=ref,
            send_sem=self.send_sem.at[row, index],
            recv_sem=self.recv_sem.at[row, index],
            device_id=device,
            device_id_type=MESH,
        )

    def copies(self, row, stage):
        place = self.place
        if stage == 0:
            where = (row, place.tower, place.deep, place.flat)
            return [self.copy(row, i, where, place.along_deep(i + 1)) for i in range(3)]
        if stage == 1:
            where = (row, place.tower, slice(None), place.flat)
            return [self.copy(row, 3 + i, where, place.along_flat(i + 1)) for i in range(3)]
        return [self.copy(row, 6, (row, place.tower), place.to["c"])]

    def start(self, row, stage):
        for copy in self.copies(row, stage):
            copy.start()

    def wait(self, row, stage):
        for copy in self.copies(row, stage):
            copy.wait()


def layer_kernel(
    tokens_hbm,
    segment_ref,
    positive_ref,
    gain_one_ref,
    query_hbm,
    key_hbm,
    value_hbm,
    output_hbm,
    table_ref,
    gain_two_ref,
    inner_hbm,
    outer_hbm,
    layer_hbm,
    token_grad_hbm,
    sums_hbm,
    hidden_sum_hbm,
    rows_grad_hbm,
    small_ref,
    tokens,
    query_w,
    key_w,
    value_w,
    output_w,
    inner_w,
    outer_w,
    normed_one,
    queries,
    keys,
    values,
    probs,
    mixed,
    middle,
    normed_two,
    hidden,
    bias,
    segment_column,
    segment_row,
    pooled_all,
    hidden_sum,
    normed_one_t,
    normed_two_t,
    mixed_t,
    grad_mixed,
    grad_query,
    grad_key,
    grad_value,
    key_total,
    value_total,
    total,
    landed,
    expand,
    rounded_grads,
    small_landed,
    load_sem,
    store_sem,
    sum_send,
    sum_recv,
    sum_out,
    pool_send,
    pool_recv,
    hidden_send,
    hidden_recv,
    small_send,
    small_recv,
):
    place = Place()
    barrier = pltpu.get_barrier_semaphore()
    partners = [place.to["c"]]
    partners += [place.along_deep(i) for i in (1, 2, 3)]
    partners += [place.along_flat(i) for i in (1, 2, 3)]
    for partner in partners:
        pl.semaphore_signal(barrier, inc=1, device_id=partner, device_id_type=MESH)

    loads = [
        pltpu.make_async_copy(source, target, load_sem.at[i])
        for i, (source, target) in enumerate(
            (
                (tokens_hbm, tokens),
                (query_hbm, query_w),
                (key_hbm, key_w),
                (value_hbm, value_w),
                (output_hbm, output_w),
                (inner_hbm, inner_w),
                (outer_hbm, outer_w),
            )
        )
    ]
    for load in loads:
        load.start()

    segment_row[...] = segment_ref[...].astype(F32)
    for i in range(8):
        row = segment_row[i // 4 : i // 4 + 1, (i % 4) * 128 : (i % 4) * 128 + 128]
        segment_column[i * 128 : (i + 1) * 128, :] = jnp.broadcast_to(row, (128, 128)).T
    place_row = lax.broadcasted_iota(jnp.int32, (32, FAR), 1)
    offsets = jnp.where(place_row >= NEAR, place_row - FAR, place_row) - 256
    by_place = exact_dot(table_ref[...], bucket_onehot(offsets), TN)
    for h in range(8):
        spread = jnp.broadcast_to(by_place[h : h + 1], (128, FAR))
        bias[h] = pltpu.roll(spread, 0, 1, stride=1, stride_axis=0)[:, :NEAR]
    lane = lax.broadcasted_iota(jnp.int32, (1, 128), 1)
    item = segment_column[...] + jnp.where(
        lax.broadcasted_iota(jnp.int32, (1024, 128), 0) >= 512, 8.0, 0.0
    )
    item = jnp.where(segment_column[...] < ITEMS_ROW, item, -1.0)
    slot = jnp.where(lane < 48, lax.rem(lane, 16), -2).astype(F32)
    expand[...] = jnp.where(item == slot, 1.0, 0.0).astype(BF)

    pooling = Spread(place, pooled_all, pool_send, pool_recv)
    hiddens = Spread(place, hidden_sum_hbm, hidden_send, hidden_recv)
    sums = Sums(place, total, landed, sums_hbm, sum_send, sum_recv, sum_out)

    def save_hidden(row):
        return pltpu.make_async_copy(
            hidden_sum.at[row],
            hidden_sum_hbm.at[row, place.tower, place.deep, place.flat],
            store_sem.at[row],
        )

    def spread_hidden(row):
        for i in range(3):
            yield pltpu.make_async_remote_copy(
                src_ref=hidden_sum.at[row],
                dst_ref=hidden_sum_hbm.at[row, place.tower, place.deep, place.flat],
                send_sem=hidden_send.at[row, i],
                recv_sem=hidden_recv.at[row, i],
                device_id=place.along_deep(i + 1),
                device_id_type=MESH,
            )

    head_lane = lax.broadcasted_iota(jnp.int32, (1, 256), 1) // 64
    head_mask = [jnp.where(head_lane == h, 1.0, 0.0) for h in range(4)]
    head_mask_low = [mask.astype(BF) for mask in head_mask]

    def stack_heads(part):
        return jnp.concatenate([part * mask for mask in head_mask_low], 0)

    def pick_heads(part):
        return sum(part[h * 128 : (h + 1) * 128] * head_mask[h] for h in range(4))

    def project(i, carry):
        rows = tile(i, 256)
        x = tokens[rows, :].astype(F32)
        scale = lax.rsqrt(jnp.mean(x * x, axis=1, keepdims=True) + EPSILON)
        normed = (x * scale * gain_one_ref[...]).astype(BF)
        normed_one[rows, :] = normed
        queries[rows, :] = dot(normed, query_w[...]).astype(BF)
        keys[rows, :] = dot(normed, key_w[...]).astype(BF)
        values[rows, :] = dot(normed, value_w[...]).astype(BF)
        return carry

    def window(unit):
        r, b = lax.div(unit, 4), lax.rem(unit, 4)
        start = lax.div(b, 2) * 128
        own = pl.ds(pl.multiple_of(r * 512 + b * 128, 128), 128)
        near = pl.ds(pl.multiple_of(r * 512 + start, 128), 384)
        offset = pl.ds(pl.multiple_of(start - 128 * b + 256, 128), 384)
        return r, own, near, pl.ds(pl.multiple_of(start, 128), 384), offset

    def attend(unit, carry):
        r, own, near, near_row, offset = window(unit)
        column = segment_column[own, :]
        same = jnp.concatenate([column] * 3, 1) == segment_row[pl.ds(r, 1), near_row]
        for g in range(2):
            lanes = slice(g * 256, (g + 1) * 256)
            scores = dot(stack_heads(queries[own, lanes]), keys[near, lanes], NT)
            parts = []
            for h in range(4):
                part = scores[h * 128 : (h + 1) * 128] + bias[g * 4 + h, :, offset]
                part = jnp.where(same, part, -1e30)
                highest = jnp.max(part, axis=1, keepdims=True)
                exp_part = jnp.exp(part - highest)
                exp_total = jnp.sum(exp_part, axis=1, keepdims=True)
                parts.append((exp_part * (1.0 / exp_total)).astype(BF))
            stacked = jnp.concatenate(parts, 0)
            probs[unit, g] = stacked
            mixed[own, lanes] = pick_heads(dot(stacked, values[near, lanes])).astype(BF)
        return carry

    def feed(i, carry):
        rows = tile(i, 256)
        branch = dot(mixed[rows, :], output_w[...])
        mid = tokens[rows, :].astype(F32) + branch
        middle[rows, :] = mid
        scale = lax.rsqrt(jnp.mean(mid * mid, axis=1, keepdims=True) + EPSILON)
        normed = (mid * scale * gain_two_ref[...]).astype(BF)
        normed_two[rows, :] = normed
        for c in range(4):
            lanes = slice(c * 512, (c + 1) * 512)
            hidden[rows, lanes] = jnp.maximum(dot(normed, inner_w[:, lanes]), 0.0).astype(BF)
        valid = jnp.where(segment_column[rows, 0:1] < ITEMS_ROW, 1.0, 0.0)
        small_ref[3:4, :] += jnp.sum(valid * branch * branch, axis=0, keepdims=True)
        small_ref[5:6, :] += jnp.sum(valid * jnp.ones_like(branch), axis=0, keepdims=True)
        return carry

    def pool(r):
        rows = slice(r * 512, (r + 1) * 512)
        number = lax.broadcasted_iota(jnp.int32, (8, 512), 0).astype(F32)
        member = jnp.where(segment_row[r : r + 1, :] == number, 1.0, 0.0)
        member_low = jnp.concatenate([member, jnp.zeros_like(member)], 0).astype(BF)
        count = jnp.sum(member, axis=1, keepdims=True)
        hidden_part = dot(member_low, hidden[rows, :])[:8]
        hidden_sum[r] = hidden_part
        middle_part = exact_dot(member, middle[rows, :])
        pieces = split_three(hidden_part)
        stacked = jnp.concatenate([*pieces, jnp.zeros_like(pieces[0])], 0)
        branch = dot(stacked, outer_w[...])
        pooled = (middle_part + (branch[0:8] + branch[8:16] + branch[16:24])) / count
        sublane = lax.broadcasted_iota(jnp.int32, (8, 128), 0)
        ids = jnp.zeros((8, 128), F32)
        for s in range(8):
            ids = jnp.where(sublane == s, positive_ref[r * 8 + s].astype(F32), ids)
        lanes = lax.broadcasted_iota(jnp.int32, (8, 128), 1)
        extra = jnp.where(lanes == 0, ids, count)
        pooled_all[r, place.tower, place.deep, place.flat] = jnp.concatenate([pooled, extra], 1)

    small_ref[...] = jnp.zeros_like(small_ref)
    for i in range(4):
        loads[i].wait()
    lax.fori_loop(0, 2, project, 0)
    lax.fori_loop(0, 4, attend, 0)
    for i in (4, 5):
        loads[i].wait()
    lax.fori_loop(0, 2, feed, 0)
    loads[6].wait()
    pool(0)
    pl.semaphore_wait(barrier, len(partners))
    pooling.start(0, 0)
    save_hidden(0).start()
    for copy in spread_hidden(0):
        copy.start()
    lax.fori_loop(2, 4, project, 0)
    pooling.wait(0, 0)
    pooling.start(0, 1)
    save_hidden(0).wait()
    for copy in spread_hidden(0):
        copy.wait()
    hiddens.start(0, 1)
    lax.fori_loop(4, 6, attend, 0)
    pooling.wait(0, 1)
    pooling.start(0, 2)
    lax.fori_loop(6, 8, attend, 0)
    lax.fori_loop(2, 4, feed, 0)
    hiddens.wait(0, 1)
    hiddens.start(0, 2)
    pool(1)
    pooling.start(1, 0)
    save_hidden(1).start()

    def store_rows(source, target, i, index):
        rows = tile(i, 256)
        return pltpu.make_async_copy(source.at[rows], target.at[rows], store_sem.at[index])

    def close(i, carry):
        rows = tile(i, 256)
        branch = dot(hidden[rows, :], outer_w[...])
        result = middle[rows, :] + branch
        grad_query[rows, :] = result.astype(BF)
        valid = jnp.where(segment_column[rows, 0:1] < ITEMS_ROW, 1.0, 0.0)
        small_ref[2:3, :] += jnp.sum(valid * result * result, axis=0, keepdims=True)
        small_ref[4:5, :] += jnp.sum(valid * branch * branch, axis=0, keepdims=True)
        return carry

    def turn(i, carry):
        rows = tile(i, 128)
        normed_two_t[:, rows] = normed_two[rows, :].T
        mixed_t[:, rows] = mixed[rows, :].T
        normed_one_t[:, rows] = normed_one[rows, :].T
        return carry

    lax.fori_loop(0, 4, close, 0)
    pooling.wait(1, 0)
    pooling.start(1, 1)
    save_hidden(1).wait()
    for copy in spread_hidden(1):
        copy.start()
    for i in range(4):
        store_rows(grad_query, layer_hbm, i, 2 + i).start()
    lax.fori_loop(0, 8, turn, 0)
    pooling.wait(1, 1)
    pooling.start(1, 2)
    for copy in spread_hidden(1):
        copy.wait()
    hiddens.start(1, 1)
    pooling.wait(0, 2)
    pooling.wait(1, 2)

    gathered = [
        jnp.concatenate([pooled_all[r, t].reshape(128, 640) for r in range(2)], 0)
        for t in range(2)
    ]
    vectors, inverse, counts, embedded = [], [], [], []
    for t in range(2):
        vector = gathered[t][:, :512]
        scale = lax.rsqrt(jnp.sum(vector * vector, axis=1, keepdims=True) + EPSILON)
        vectors.append(vector)
        inverse.append(scale)
        embedded.append(vector * scale)
        counts.append(gathered[t][:, 513:514])
    logits = exact_dot(embedded[0], embedded[1], NT) / SOFTMAX_TEMP
    highest = jnp.max(logits, axis=1, keepdims=True)
    exp_logits = jnp.exp(logits - highest)
    exp_total = jnp.sum(exp_logits, axis=1, keepdims=True)
    position = lax.broadcasted_iota(jnp.int32, (256, 256), 1)
    number = lax.rem(lax.div(position, 8), 16) * 16 + lax.div(position, 128) * 8
    number = (number + lax.rem(position, 8)).astype(F32)
    is_target = gathered[0][:, 512:513] == number
    target = jnp.sum(jnp.where(is_target, logits, 0.0), axis=1, keepdims=True)
    losses = highest + jnp.log(exp_total) - target
    loss = jnp.sum(losses, axis=0, keepdims=True) / 256
    grad_logits = (exp_logits / exp_total - jnp.where(is_target, 1.0, 0.0)) * (LOSS_SCALE / 256)
    grads = (
        exact_dot(grad_logits, embedded[1]) / SOFTMAX_TEMP,
        exact_dot(grad_logits, embedded[0], TN) / SOFTMAX_TEMP,
    )
    for t in range(2):
        along = jnp.sum(grads[t] * embedded[t], axis=1, keepdims=True)
        per_token = inverse[t] * (grads[t] - embedded[t] * along) / counts[t]
        for r in range(2):
            part = per_token[r * 128 : (r + 1) * 128]
            total[12 + 2 * r + t, 0:128] = part[:, :256]
            total[12 + 2 * r + t, 128:256] = part[:, 256:]
            rounded_grads[r, t] = per_token[r * 128 : (r + 1) * 128].astype(BF)
    save_grads = pltpu.make_async_copy(rounded_grads, rows_grad_hbm, store_sem.at[6])
    save_grads.start()
    own_parts = []
    for r in range(2):
        spot = 12 + 2 * r + place.tower
        left, right = tile(place.rows, 8), tile(place.rows + 16, 8)
        own_parts.append(jnp.concatenate([total[spot, left], total[spot, right]], 1))
    own = jnp.concatenate(own_parts, 0)
    pieces = split_three(own)
    own_low = pieces[0]
    own_split = jnp.concatenate([*pieces, jnp.zeros((80, 512), BF)], 0)

    def back_hidden(c):
        lanes = slice(c * 512, (c + 1) * 512)
        row_part = dot(own_low, outer_w[lanes, :], NT).astype(BF)
        row_part = jnp.concatenate([row_part, jnp.zeros((112, 512), BF)], 0)

        def mask(i, carry):
            rows = tile(i, 256)
            spread = dot(expand[rows, :], row_part)
            hidden[rows, lanes] = jnp.where(hidden[rows, lanes] > 0, spread, 0.0).astype(BF)
            return carry

        lax.fori_loop(0, 4, mask, 0)
        for half in range(2):
            unit = 2 * c + half
            total[unit] = dot(normed_two_t[...], hidden[:, unit * 256 : (unit + 1) * 256])
        sums.start(2 * c, 2 * c + 1)

    def back_middle(i, carry):
        rows = tile(i, 256)
        grad_normed = dot(hidden[rows, :], inner_w[...], NT)
        mid = middle[rows, :]
        scale = lax.rsqrt(jnp.mean(mid * mid, axis=1, keepdims=True) + EPSILON)
        small_ref[1:2, :] += jnp.sum(grad_normed * mid * scale, axis=0, keepdims=True)
        gained = grad_normed * gain_two_ref[...]
        mean = jnp.mean(gained * mid, axis=1, keepdims=True)
        grad_mid = dot(expand[rows, :], own_split) + scale * (gained - mid * scale * scale * mean)
        middle[rows, :] = grad_mid
        rounded = grad_mid.astype(BF)
        mixed[rows, :] = rounded
        grad_mixed[rows, :] = dot(rounded, output_w[...], NT).astype(BF)
        return carry

    back_hidden(0)
    back_hidden(1)
    sums.tick()
    back_hidden(2)
    back_hidden(3)
    sums.tick()
    lax.fori_loop(0, 4, back_middle, 0)
    for half in range(2):
        total[8 + half] = dot(mixed_t[...], mixed[:, half * 256 : (half + 1) * 256])
    sums.start(8, 9)
    sums.tick()
    hiddens.wait(1, 1)
    hiddens.start(1, 2)

    for i in range(4):
        store_rows(grad_query, layer_hbm, i, 2 + i).wait()
    bias[...] = jnp.zeros_like(bias)

    def attend_back(g, unit, carry):
        r, own, near, near_row, offset = window(unit)
        lanes = slice(g * 256, (g + 1) * 256)
        grad_stack = stack_heads(grad_mixed[own, lanes])
        grad_soft = dot(grad_stack, values[near, lanes], NT)
        soft = probs[unit, g]
        parts = []
        for h in range(4):
            rows = slice(h * 128, (h + 1) * 128)
            soft_part = soft[rows].astype(F32)
            grad_part = grad_soft[rows]
            along = jnp.sum(soft_part * grad_part, axis=1, keepdims=True)
            part = (soft_part * (grad_part - along)).astype(BF)
            bias[g * 4 + h, :, offset] += part.astype(F32)
            parts.append(part)
        stacked = jnp.concatenate(parts, 0)
        grad_query[own, lanes] = pick_heads(dot(stacked, keys[near, lanes])).astype(BF)
        key_total[near, :] += dot(stacked, stack_heads(queries[own, lanes]), TN)
        value_total[near, :] += dot(soft, grad_stack, TN)
        return carry

    for g in range(2):
        lanes = slice(g * 256, (g + 1) * 256)
        key_total[...] = jnp.zeros_like(key_total)
        value_total[...] = jnp.zeros_like(value_total)
        for quarter in range(4):
            lax.fori_loop(2 * quarter, 2 * quarter + 2, functools.partial(attend_back, g), 0)
            sums.tick()
        grad_key[:, lanes] = key_total[...].astype(BF)
        grad_value[:, lanes] = value_total[...].astype(BF)
        total[10 + 3 * g] = dot(normed_one_t[...], grad_query[:, lanes])
        total[11 + 3 * g] = dot(normed_one_t[...], grad_key[:, lanes])
        total[12 + 3 * g] = dot(normed_one_t[...], grad_value[:, lanes])
        sums.start(10 + 3 * g, 11 + 3 * g, 12 + 3 * g)

    def back_tokens(i, carry):
        rows = tile(i, 256)
        grad_normed = (
            dot(grad_query[rows, :], query_w[...], NT)
            + dot(grad_key[rows, :], key_w[...], NT)
            + dot(grad_value[rows, :], value_w[...], NT)
        )
        x = tokens[rows, :].astype(F32)
        scale = lax.rsqrt(jnp.mean(x * x, axis=1, keepdims=True) + EPSILON)
        small_ref[0:1, :] += jnp.sum(grad_normed * x * scale, axis=0, keepdims=True)
        gained = grad_normed * gain_one_ref[...]
        mean = jnp.mean(gained * x, axis=1, keepdims=True)
        grad = middle[rows, :] + scale * (gained - x * scale * scale * mean)
        normed_one[rows, :] = grad.astype(BF)
        return carry

    lax.fori_loop(0, 4, back_tokens, 0)
    for i in range(4):
        store_rows(normed_one, token_grad_hbm, i, 2 + i).start()
    mirror = (
        lax.broadcasted_iota(jnp.int32, (128, 128), 0)
        + lax.broadcasted_iota(jnp.int32, (128, 128), 1)
    )
    mirror = jnp.where(mirror == 127, 1.0, 0.0)
    diagonals = []
    for h in range(8):
        turned = exact_dot(mirror, bias[h])
        wide = jnp.concatenate([turned, jnp.zeros((128, FAR - NEAR), F32)], 1)
        wide = pltpu.roll(wide, 0, 1, stride=1, stride_axis=0)
        diagonals.append(jnp.sum(wide, axis=0, keepdims=True))
    buckets = exact_dot(jnp.concatenate(diagonals, 0), bucket_onehot(place_row - 383), NT)
    small_ref[8:16, :] = jnp.concatenate([buckets, jnp.zeros((8, 480), F32)], 1)
    for i, name in enumerate("cxyzw"):
        copy = pltpu.make_async_remote_copy(
            src_ref=small_ref,
            dst_ref=small_landed.at[i],
            send_sem=small_send.at[i],
            recv_sem=small_recv.at[i],
            device_id=place.to[name],
            device_id_type=MESH,
        )
        copy.start()
        copy.wait()
        small_ref[...] += small_landed[i]
        sums.tick()
    small_ref[6:7, :] = jnp.broadcast_to(loss, (1, 512))
    hiddens.wait(0, 2)
    hiddens.wait(1, 2)
    save_grads.wait()
    sums.finish()
    for i in range(4):
        store_rows(normed_one, token_grad_hbm, i, 2 + i).wait()


def closing_kernel(
    layer_hbm,
    token_grad_hbm,
    sums_hbm,
    hidden_sum_hbm,
    rows_grad_ref,
    small_ref,
    layer_out,
    token_out,
    gain_one_out,
    query_out,
    key_out,
    value_out,
    output_out,
    position_out,
    gain_two_out,
    inner_out,
    outer_out,
    loss_out,
    square_out,
    hidden_sum,
    hidden_low,
    outer_part,
    load_sem,
    copy_sem,
    store_sem,
):
    load = pltpu.make_async_copy(hidden_sum_hbm, hidden_sum, load_sem)
    load.start()
    pairs = [(layer_hbm, layer_out), (token_grad_hbm, token_out)]
    for unit in range(8):
        pairs.append((sums_hbm.at[unit], inner_out.at[:, pl.ds(unit * 256, 256)]))
    places = [(output_out, 0), (output_out, 1)]
    places += [(ref, g) for g in range(2) for ref in (query_out, key_out, value_out)]
    for unit, (ref, g) in enumerate(places):
        pairs.append((sums_hbm.at[8 + unit], ref.at[:, pl.ds(g * 256, 256)]))
    copies = [
        pltpu.make_async_copy(source, target, copy_sem.at[i])
        for i, (source, target) in enumerate(pairs)
    ]
    for copy in copies:
        copy.start()
    gain_one_out[...] = small_ref[0, :]
    gain_two_out[...] = small_ref[1, :]
    eye = jnp.where(
        lax.broadcasted_iota(jnp.int32, (32, 32), 0) == lax.broadcasted_iota(jnp.int32, (32, 32), 1),
        1.0,
        0.0,
    )
    position_out[...] = exact_dot(eye, small_ref[8:16, 0:32], NT)
    loss_out[0] = jnp.max(small_ref[6:7, :])
    squares = jnp.sum(small_ref[2:5, :], axis=1, keepdims=True)
    valid = jnp.sum(small_ref[5:6, :], axis=1, keepdims=True)
    roots = jnp.sqrt(squares / valid)
    for i in range(3):
        square_out[i] = jnp.max(roots[i : i + 1, :])
    load.wait()
    hidden_low[...] = hidden_sum[...].reshape(512, 2048).astype(BF)
    grads = rows_grad_ref[...].reshape(512, 512)
    stores = []
    for c in range(4):
        if c >= 2:
            stores[c - 2].wait()
        outer_part[c % 2] = dot(hidden_low[:, c * 512 : (c + 1) * 512], grads, TN)
        store = pltpu.make_async_copy(
            outer_part.at[c % 2], outer_out.at[pl.ds(c * 512, 512)], store_sem.at[c % 2]
        )
        store.start()
        stores.append(store)
    stores[2].wait()
    stores[3].wait()
    for copy in copies:
        copy.wait()


def fast_shards(
    tokens,
    segment_ids,
    positives,
    attention_gain,
    query_weight,
    key_weight,
    value_weight,
    output_weight,
    position_table,
    feedforward_gain,
    inner_weight,
    outer_weight,
):
    block_shape = tokens.shape
    anywhere = pl.BlockSpec(memory_space=pl.ANY)
    vmem = pl.BlockSpec(memory_space=pltpu.VMEM)
    smem = pl.BlockSpec(memory_space=pltpu.SMEM)
    shape = jax.ShapeDtypeStruct
    dma = pltpu.SemaphoreType.DMA
    low = functools.partial(pltpu.VMEM, dtype=BF)
    full = functools.partial(pltpu.VMEM, dtype=F32)
    outs = pl.pallas_call(
        layer_kernel,
        out_shape=[
            shape((1024, 512), BF),
            shape((1024, 512), BF),
            shape((UNITS, 512, 256), F32),
            shape((2, 2, 4, 4, 8, 2048), F32),
            shape((2, 2, 128, 512), BF),
            shape((16, 512), F32),
        ],
        in_specs=[anywhere, vmem, smem, vmem]
        + [anywhere] * 4
        + [vmem, vmem, anywhere, anywhere],
        out_specs=[anywhere] * 5 + [vmem],
        scratch_shapes=[
            low((1024, 512)),
            low((512, 512)),
            low((512, 512)),
            low((512, 512)),
            low((512, 512)),
            low((512, 2048)),
            low((2048, 512)),
            low((1024, 512)),
            low((1024, 512)),
            low((1024, 512)),
            low((1024, 512)),
            low((8, 2, 512, 384)),
            low((1024, 512)),
            full((1024, 512)),
            low((1024, 512)),
            low((1024, 2048)),
            full((8, 128, NEAR)),
            full((1024, 128)),
            full((2, 512)),
            full((2, 2, 4, 4, 8, 640)),
            full((2, 8, 2048)),
            low((512, 1024)),
            low((512, 1024)),
            low((512, 1024)),
            low((1024, 512)),
            low((1024, 512)),
            low((1024, 512)),
            low((1024, 512)),
            full((1024, 256)),
            full((1024, 256)),
            full((UNITS, 512, 256)),
            full((UNITS, 496, 256)),
            low((1024, 128)),
            low((2, 2, 128, 512)),
            full((5, 16, 512)),
            dma((7,)),
            dma((7,)),
            dma((10, UNITS)),
            dma((10, UNITS)),
            dma((UNITS,)),
            dma((2, 7)),
            dma((2, 7)),
            dma((2, 7)),
            dma((2, 7)),
            dma((5,)),
            dma((5,)),
        ],
        compiler_params=pltpu.CompilerParams(
            collective_id=0, has_side_effects=True, vmem_limit_bytes=63 * 2**20
        ),
    )(
        tokens.reshape(1024, 512),
        segment_ids.reshape(2, 512),
        positives,
        attention_gain.reshape(1, 512),
        query_weight,
        key_weight,
        value_weight,
        output_weight,
        position_table,
        feedforward_gain.reshape(1, 512),
        inner_weight,
        outer_weight,
    )
    results = pl.pallas_call(
        closing_kernel,
        out_shape=[
            shape((1024, 512), BF),
            shape((1024, 512), BF),
            shape((512,), F32),
            shape((512, 512), F32),
            shape((512, 512), F32),
            shape((512, 512), F32),
            shape((512, 512), F32),
            shape((32, 8), F32),
            shape((512,), F32),
            shape((512, 2048), F32),
            shape((2048, 512), F32),
            shape((1,), F32),
            shape((3,), F32),
        ],
        in_specs=[anywhere] * 4 + [vmem, vmem],
        out_specs=[anywhere, anywhere, vmem]
        + [anywhere] * 4
        + [vmem, vmem, anywhere, anywhere, smem, smem],
        scratch_shapes=[
            full((2, 2, 4, 4, 8, 2048)),
            low((512, 2048)),
            full((2, 512, 512)),
            dma(()),
            dma((18,)),
            dma((2,)),
        ],
        compiler_params=pltpu.CompilerParams(vmem_limit_bytes=24 * 2**20),
    )(*outs)
    layer, token_grad, *rest = results
    return (
        layer.reshape(block_shape),
        token_grad.reshape(block_shape),
        *rest[:9],
        rest[9].reshape(()),
        rest[10],
    )


def solution(mesh):
    fast = mesh.shape["tower"] == 2 and mesh.shape["rows"] == 16
    return jax.shard_map(
        fast_shards if fast else shards,
        mesh=mesh,
        in_specs=(
            P("tower", "rows", None, None),
            P("tower", "rows", None),
            P("rows"),
            P(),
            P(),
            P(),
            P(),
            P(),
            P(),
            P(),
            P(),
            P(),
        ),
        out_specs=(
            P("tower", "rows", None, None),
            P("tower", "rows", None, None),
            P(),
            P(),
            P(),
            P(),
            P(),
            P(),
            P(),
            P(),
            P(),
            P(),
            P(),
        ),
        check_vma=False,
    )
```

```python
import functools
import math

import jax
import jax.numpy as jnp
import numpy as np
from jax import lax
from jax.experimental import pallas as pl
from jax.experimental.pallas import tpu as pltpu
from jax.sharding import PartitionSpec as P

MAX_DIST = 128
ITEMS_ROW = 8


EPSILON = 1e-06
SOFTMAX_TEMP = 0.01
LOSS_SCALE = 65536.0
MATMUL_PRECISION = lax.Precision.HIGHEST


def from_partner(value, axis, apart):
    mask = 2**apart
    pairs = [(source, source ^ mask) for source in range(lax.axis_size(axis))]
    return lax.ppermute(value, axis, pairs)


def bucket_table(length, bucket_count, far_limit):
    half_count = bucket_count // 2
    exact_count = half_count // 2
    entries = []
    for offset in range(1 - length, length):
        distance = abs(offset)
        if distance < exact_count:
            within = distance
        else:
            within = exact_count + int(
                math.log(distance / exact_count)
                / math.log(far_limit / exact_count)
                * (half_count - exact_count)
            )
            within = min(within, half_count - 1)
        entries.append(within + (half_count if offset > 0 else 0))
    by_offset = np.array(entries, dtype=np.int32)
    index_grid = np.arange(length)[None, :] - np.arange(length)[:, None] + length - 1
    return (by_offset, by_offset[index_grid])


def contract_rows(left_side, right_side):
    return lax.dot_general(
        left_side, right_side, (((0,), (0,)), ((), ())), preferred_element_type=jnp.float32
    )


def times_transpose(left_side, right_side):
    return lax.dot_general(
        left_side, right_side, (((1,), (1,)), ((), ())), preferred_element_type=jnp.float32
    )


def norm_scale(values):
    return lax.rsqrt(jnp.mean(values * values, axis=1, keepdims=True) + EPSILON)


def norm_back(grad_normed, values, scale, gain):
    gained = grad_normed * gain
    return scale * (
        gained - values * scale * scale * jnp.mean(gained * values, axis=1, keepdims=True)
    )


def row_scores(query_part, key_part, segment_row, position_bias, head_count):
    length = query_part.shape[0]
    query_heads = query_part.reshape(length, head_count, -1)
    key_heads = key_part.reshape(length, head_count, -1)
    scores = (
        jnp.einsum("qhd,khd->hqk", query_heads, key_heads, preferred_element_type=jnp.float32)
        + position_bias
    )
    same_item = segment_row[:, None] == segment_row[None, :]
    return jnp.where(same_item[None], scores, -1e30)


def diagonal_sums(square):
    head_count = square.shape[0]
    length = square.shape[1]
    flipped = square[:, :, ::-1]
    padded = jnp.pad(flipped, ((0, 0), (0, 0), (0, length)))
    sheared = padded.reshape(head_count, 2 * length * length)[:, : length * (2 * length - 1)]
    sheared = sheared.reshape(head_count, length, 2 * length - 1)
    return jnp.sum(sheared, axis=1)[:, ::-1]


def shards(
    tokens,
    segment_ids,
    positives,
    attention_gain,
    query_weight,
    key_weight,
    value_weight,
    output_weight,
    position_table,
    feedforward_gain,
    inner_weight,
    outer_weight,
):
    row_count = tokens.shape[1]
    length = tokens.shape[2]
    model_width = tokens.shape[3]
    head_count = position_table.shape[1]
    inner_width = query_weight.shape[1]
    head_size = inner_width // head_count
    token_count = row_count * length
    by_offset, bucket_index = bucket_table(length, position_table.shape[0], MAX_DIST)
    position_bias = jnp.take(position_table.T, jnp.asarray(bucket_index), axis=1)
    inputs = tokens.reshape(token_count, model_width).astype(jnp.float32)
    segments = segment_ids.reshape(row_count, length)
    scale_one = norm_scale(inputs)
    normed_one = (inputs * scale_one * attention_gain).astype(jnp.bfloat16)
    query_rows = jnp.dot(normed_one, query_weight, preferred_element_type=jnp.float32).astype(
        jnp.bfloat16
    )
    key_rows = jnp.dot(normed_one, key_weight, preferred_element_type=jnp.float32).astype(
        jnp.bfloat16
    )
    value_rows = jnp.dot(normed_one, value_weight, preferred_element_type=jnp.float32).astype(
        jnp.bfloat16
    )
    query_blocks = query_rows.reshape(row_count, length, inner_width)
    key_blocks = key_rows.reshape(row_count, length, inner_width)
    value_blocks = value_rows.reshape(row_count, length, inner_width)

    def attend(packed):
        query_part, key_part, value_part, segment_row = packed
        scores = row_scores(query_part, key_part, segment_row, position_bias, head_count)
        highest = jnp.max(scores, axis=2, keepdims=True)
        exp_scores = jnp.exp(scores - highest)
        exp_total = jnp.sum(exp_scores, axis=2, keepdims=True)
        attention_probs = (exp_scores / exp_total).astype(jnp.bfloat16)
        value_heads = value_part.reshape(length, head_count, head_size)
        mixed_heads = jnp.einsum(
            "hqk,khd->qhd", attention_probs, value_heads, preferred_element_type=jnp.float32
        )
        return (
            mixed_heads.reshape(length, inner_width).astype(jnp.bfloat16),
            (highest + jnp.log(exp_total))[:, :, 0],
        )

    mixed_blocks, log_totals = lax.map(attend, (query_blocks, key_blocks, value_blocks, segments))
    mixed_rows = mixed_blocks.reshape(token_count, inner_width)
    branch_one = jnp.dot(mixed_rows, output_weight, preferred_element_type=jnp.float32)
    middle = inputs + branch_one
    scale_two = norm_scale(middle)
    normed_two = (middle * scale_two * feedforward_gain).astype(jnp.bfloat16)
    hidden = jax.nn.relu(
        jnp.dot(normed_two, inner_weight, preferred_element_type=jnp.float32)
    ).astype(jnp.bfloat16)
    branch_two = jnp.dot(hidden, outer_weight, preferred_element_type=jnp.float32)
    result = middle + branch_two
    valid_mask = (segments < ITEMS_ROW).astype(jnp.float32).reshape(token_count, 1)
    stat_terms = jnp.stack(
        [
            jnp.sum(valid_mask * result * result),
            jnp.sum(valid_mask * branch_one * branch_one),
            jnp.sum(valid_mask * branch_two * branch_two),
            jnp.sum(valid_mask),
        ]
    )
    stat_totals = lax.psum(stat_terms, ("tower", "rows"))
    member = (segments[:, None, :] == jnp.arange(ITEMS_ROW)[None, :, None]).astype(jnp.float32)
    item_sizes = jnp.sum(member, axis=2, keepdims=True)
    result_blocks = result.reshape(row_count, length, model_width)
    pooled = (
        jnp.einsum("ris,rsd->rid", member, result_blocks, precision=MATMUL_PRECISION) / item_sizes
    )
    items_here = row_count * ITEMS_ROW
    pooled = pooled.reshape(items_here, model_width)
    inverse_norm = lax.rsqrt(jnp.sum(pooled * pooled, axis=1, keepdims=True) + EPSILON)
    embedded_tokens = pooled * inverse_norm
    tower_index = lax.axis_index("tower")
    is_query = tower_index == 0
    partner = from_partner(embedded_tokens, "tower", 0)
    query_vectors = jnp.where(is_query, embedded_tokens, partner)
    document_vectors = jnp.where(is_query, partner, embedded_tokens)
    gathered_documents = lax.all_gather(document_vectors, "rows", axis=0, tiled=True)
    item_total = gathered_documents.shape[0]
    half_items = items_here // 2
    my_queries = lax.dynamic_slice_in_dim(query_vectors, tower_index * half_items, half_items, 0)
    my_targets = lax.dynamic_slice_in_dim(positives, tower_index * half_items, half_items, 0)
    similarity_scores = (
        lax.dot_general(
            my_queries,
            gathered_documents,
            (((1,), (1,)), ((), ())),
            precision=MATMUL_PRECISION,
            preferred_element_type=jnp.float32,
        )
        / SOFTMAX_TEMP
    )
    highest = jnp.max(similarity_scores, axis=1, keepdims=True)
    exp_logits = jnp.exp(similarity_scores - highest)
    exp_total = jnp.sum(exp_logits, axis=1, keepdims=True)
    log_total = highest[:, 0] + jnp.log(exp_total[:, 0])
    is_target = jnp.arange(item_total)[None, :] == my_targets[:, None]
    target = jnp.sum(jnp.where(is_target, similarity_scores, 0.0), axis=1)
    loss_part = jnp.sum(log_total - target)
    similarity_gradient = (exp_logits / exp_total - is_target.astype(jnp.float32)) * (
        LOSS_SCALE / item_total
    )
    local_gradient = (
        jnp.dot(similarity_gradient, gathered_documents, precision=MATMUL_PRECISION) / SOFTMAX_TEMP
    )
    grad_documents = lax.psum_scatter(
        lax.dot_general(
            similarity_gradient,
            my_queries,
            (((0,), (0,)), ((), ())),
            precision=MATMUL_PRECISION,
            preferred_element_type=jnp.float32,
        )
        / SOFTMAX_TEMP,
        "rows",
        scatter_dimension=0,
        tiled=True,
    )
    partner_mine, partner_documents = from_partner((local_gradient, grad_documents), "tower", 0)
    query_side = jnp.where(
        is_query,
        jnp.concatenate([local_gradient, partner_mine], 0),
        jnp.concatenate([partner_mine, local_gradient], 0),
    )
    own_grad = jnp.where(is_query, query_side, grad_documents + partner_documents)
    inner_along = jnp.sum(own_grad * embedded_tokens, axis=1, keepdims=True)
    grad_pooled = inverse_norm * (own_grad - embedded_tokens * inner_along)
    per_token = grad_pooled.reshape(row_count, ITEMS_ROW, model_width) / item_sizes
    grad_result = jnp.einsum("ris,rid->rsd", member, per_token, precision=MATMUL_PRECISION).reshape(
        token_count, model_width
    )
    grad_branch_two = grad_result.astype(jnp.bfloat16)
    outer_grad = contract_rows(hidden, grad_branch_two)
    grad_hidden = times_transpose(grad_branch_two, outer_weight)
    grad_pre = jnp.where(hidden > 0, grad_hidden, 0.0).astype(jnp.bfloat16)
    inner_grad = contract_rows(normed_two, grad_pre)
    grad_normed_two = times_transpose(grad_pre, inner_weight)
    feedforward_gain_grad = jnp.sum(grad_normed_two * middle * scale_two, axis=0)
    grad_middle = grad_result + norm_back(grad_normed_two, middle, scale_two, feedforward_gain)
    grad_branch_one = grad_middle.astype(jnp.bfloat16)
    output_grad = contract_rows(mixed_rows, grad_branch_one)
    grad_mixed = times_transpose(grad_branch_one, output_weight).astype(jnp.bfloat16)
    grad_mixed_blocks = grad_mixed.reshape(row_count, length, inner_width)

    def attend_back(running, packed):
        query_part, key_part, value_part, segment_row, row_log_total, grad_part = packed
        scores = row_scores(query_part, key_part, segment_row, position_bias, head_count)
        attention_probs = jnp.exp(scores - row_log_total[:, :, None])
        query_heads = query_part.reshape(length, head_count, head_size)
        key_heads = key_part.reshape(length, head_count, head_size)
        value_heads = value_part.reshape(length, head_count, head_size)
        grad_heads = grad_part.reshape(length, head_count, head_size)
        grad_value = jnp.einsum(
            "hqk,qhd->khd",
            attention_probs.astype(jnp.bfloat16),
            grad_heads,
            preferred_element_type=jnp.float32,
        )
        grad_probs = jnp.einsum(
            "qhd,khd->hqk", grad_heads, value_heads, preferred_element_type=jnp.float32
        )
        row_dot = jnp.sum(attention_probs * grad_probs, axis=2, keepdims=True)
        grad_scores = (attention_probs * (grad_probs - row_dot)).astype(jnp.bfloat16)
        grad_query = jnp.einsum(
            "hqk,khd->qhd", grad_scores, key_heads, preferred_element_type=jnp.float32
        )
        grad_key = jnp.einsum(
            "hqk,qhd->khd", grad_scores, query_heads, preferred_element_type=jnp.float32
        )
        outputs = (
            grad_query.reshape(length, inner_width).astype(jnp.bfloat16),
            grad_key.reshape(length, inner_width).astype(jnp.bfloat16),
            grad_value.reshape(length, inner_width).astype(jnp.bfloat16),
        )
        return (running + grad_scores.astype(jnp.float32), outputs)

    score_sum, grad_rows = lax.scan(
        attend_back,
        jnp.zeros((head_count, length, length), jnp.float32),
        (query_blocks, key_blocks, value_blocks, segments, log_totals, grad_mixed_blocks),
    )
    grad_queries = grad_rows[0].reshape(token_count, inner_width)
    grad_keys = grad_rows[1].reshape(token_count, inner_width)
    grad_values = grad_rows[2].reshape(token_count, inner_width)
    query_grad = contract_rows(normed_one, grad_queries)
    key_grad = contract_rows(normed_one, grad_keys)
    value_grad = contract_rows(normed_one, grad_values)
    grad_normed_one = (
        times_transpose(grad_queries, query_weight)
        + times_transpose(grad_keys, key_weight)
        + times_transpose(grad_values, value_weight)
    )
    attention_gain_grad = jnp.sum(grad_normed_one * inputs * scale_one, axis=0)
    token_grad = grad_middle + norm_back(grad_normed_one, inputs, scale_one, attention_gain)
    offset_onehot = jnp.asarray(
        (by_offset[:, None] == np.arange(position_table.shape[0])[None, :]).astype(np.float32)
    )
    position_grad = jnp.dot(diagonal_sums(score_sum), offset_onehot, precision=MATMUL_PRECISION).T
    closing_terms = loss_part[None]
    summed = lax.psum(
        (
            attention_gain_grad,
            query_grad,
            key_grad,
            value_grad,
            output_grad,
            position_grad,
            feedforward_gain_grad,
            inner_grad,
            outer_grad,
            closing_terms,
        ),
        ("tower", "rows"),
    )
    (
        attention_gain_grad,
        query_grad,
        key_grad,
        value_grad,
        output_grad,
        position_grad,
        feedforward_gain_grad,
        inner_grad,
        outer_grad,
        closing_totals,
    ) = summed
    contrastive_loss = closing_totals[0] / item_total
    root_mean_squares = jnp.sqrt(stat_totals[:3] / (stat_totals[3] * model_width))
    block_shape = (1, row_count, length, model_width)
    return (
        result.reshape(block_shape).astype(jnp.bfloat16),
        token_grad.reshape(block_shape).astype(jnp.bfloat16),
        attention_gain_grad,
        query_grad,
        key_grad,
        value_grad,
        output_grad,
        position_grad,
        feedforward_gain_grad,
        inner_grad,
        outer_grad,
        contrastive_loss,
        root_mean_squares,
    )


F32 = jnp.float32
BF = jnp.bfloat16
MESH = pl.DeviceIdType.MESH
NN = (((1,), (0,)), ((), ()))
NT = (((1,), (1,)), ((), ()))
TN = (((0,), (0,)), ((), ()))
UNITS = 16
HALVES = (256, 128, 64)
OFFSETS = (0, 256, 384, 448)
SMALL = 16
STEPS_AFTER = (
    (),
    (0, 1,),
    (2, 3,),
    (4, 5,),
    (6, 7, 0, 1,),
    (2, 3,),
    (),
    (4, 5,),
    (),
    (8, 9, 6, 7, 0, 1,),
    (2, 3, 4, 5,),
    (8, 9, 0, 1,),
    (6, 7, 2, 3, 8, 9, 4,),
    (),
    (5,),
    (10, 0, 11,),
    (12, 1, 6,),
    (10, 7, 0, 2,),
    (11, 12, 8, 3, 10, 1,),
    (9, 4, 2, 12, 0, 5,),
    (11,),
    (6, 0, 13, 3, 7, 14, 1, 4,),
    (8,),
    (10, 15, 5, 6, 2, 9, 1, 7,),
    (13, 12, 2, 11,),
    (14, 10, 3,),
    (8, 12, 4, 3,),
    (15, 11, 6, 9, 16, 5, 4, 13, 6, 5, 7, 8, 14, 7, 13, 15, 8, 10, 11, 12, 16, 14, 13, 9, 15, 10, 9, 14, 11, 10, 16, 12, 11, 15, 13, 12, 14, 16, 15, 16, 13, 14, 13, 14, 15, 15,),
)
FAR = 768
NEAR = 640


def dot(a, b, dims=NN):
    return lax.dot_general(a, b, dims, preferred_element_type=F32)


def exact_dot(a, b, dims=NN):
    return lax.dot_general(
        a, b, dims, precision=lax.Precision.HIGHEST, preferred_element_type=F32
    )


def tile(index, size):
    if isinstance(index, int):
        return pl.ds(index * size, size)
    return pl.ds(pl.multiple_of(index * size, size), size)


def far_limits(bucket_count, far_limit):
    half_count = bucket_count // 2
    exact_count = half_count // 2
    limits = []
    reached = exact_count
    for distance in range(exact_count, 512):
        within = exact_count + int(
            math.log(distance / exact_count)
            / math.log(far_limit / exact_count)
            * (half_count - exact_count)
        )
        within = min(within, half_count - 1)
        while reached < within:
            limits.append(distance)
            reached += 1
    return limits


def bucket_onehot(offset):
    distance = jnp.abs(offset)
    far = jnp.full_like(distance, 8)
    for limit in far_limits(32, MAX_DIST):
        far = far + jnp.where(distance >= limit, 1, 0)
    bucket = jnp.where(distance < 8, distance, far) + jnp.where(offset > 0, 16, 0)
    same = bucket == lax.broadcasted_iota(jnp.int32, (32, FAR), 0)
    return jnp.where(same, 1.0, 0.0).astype(F32)


def split_three(value):
    high = value.astype(BF)
    rest = value - high.astype(F32)
    middle = rest.astype(BF)
    return high, middle, (rest - middle.astype(F32)).astype(BF)


class Place:
    def __init__(self):
        self.tower = lax.axis_index("tower")
        self.rows = lax.axis_index("rows")
        self.flat = lax.rem(self.rows, 4)
        self.deep = lax.div(self.rows, 4)
        bits = {
            "x": lax.rem(self.rows, 2),
            "y": lax.rem(lax.div(self.rows, 2), 2),
            "z": lax.rem(lax.div(self.rows, 4), 2),
            "w": lax.div(self.rows, 8),
        }
        steps = {"x": 1, "y": 2, "z": 4, "w": 8}
        self.bit = {"c": self.tower, **bits}
        self.to = {"c": self.device(1 - self.tower, self.rows)}
        for name, step in steps.items():
            self.to[name] = self.device(self.tower, self.rows + step * (1 - 2 * bits[name]))

    def device(self, tower, rows):
        return {"tower": tower, "rows": rows}

    def along_deep(self, step):
        return self.device(self.tower, lax.rem(self.deep + step, 4) * 4 + self.flat)

    def along_flat(self, step):
        return self.device(self.tower, self.deep * 4 + lax.rem(self.flat + step, 4))


class Sums:
    ORDERS = (("c", "x", "y"), ("c", "y", "x"))

    def __init__(self, place, total, landed, out, small, small_landed, sems):
        self.place, self.total, self.landed, self.out = place, total, landed, out
        self.small, self.small_landed = small, small_landed
        self.send_sem, self.recv_sem, self.out_sem, self.small_send, self.small_recv = sems
        self.bases = []
        for order in self.ORDERS:
            base, bases = 0, [0]
            for name, half in zip(order, HALVES):
                base = base + place.bit[name] * half
                bases.append(base)
            self.bases.append(bases)
        self.stage = {}

    def remote(self, source, target, index, unit, device):
        return pltpu.make_async_remote_copy(
            src_ref=source,
            dst_ref=target,
            send_sem=self.send_sem.at[index, unit],
            recv_sem=self.recv_sem.at[index, unit],
            device_id=device,
            device_id_type=MESH,
        )

    def halve(self, k, unit):
        order, bases, half = self.ORDERS[unit % 2], self.bases[unit % 2], HALVES[k]
        name = order[k]
        start = pl.multiple_of(bases[k] + (1 - self.place.bit[name]) * half, half)
        return [
            self.remote(
                self.total.at[unit, pl.ds(start, half)],
                self.landed.at[unit, pl.ds(OFFSETS[k], half)],
                k,
                unit,
                self.place.to[name],
            )
        ]

    def piece(self, unit, deep):
        return pl.ds(pl.multiple_of(self.bases[unit % 2][3] + deep * 16, 16), 16)

    def share(self, unit):
        return [
            self.remote(
                self.total.at[unit, self.piece(unit, lax.rem(self.place.deep + i, 4))],
                self.landed.at[unit, pl.ds(OFFSETS[3] + 16 * (i - 1), 16)],
                2 + i,
                unit,
                self.place.along_deep(i),
            )
            for i in (1, 2, 3)
        ]

    def collect(self, unit):
        rows = self.piece(unit, self.place.deep)
        return [
            self.remote(
                self.total.at[unit, rows],
                self.out.at[unit, rows],
                5 + i,
                unit,
                self.place.along_deep(i),
            )
            for i in (1, 2, 3)
        ]

    def own(self, k, unit):
        return pl.ds(pl.multiple_of(self.bases[unit % 2][k + 1], HALVES[k]), HALVES[k])

    def double(self, k, unit):
        rows = self.out.at[unit, self.own(k, unit)]
        name = self.ORDERS[unit % 2][k]
        return [self.remote(rows, rows, 11 - k, unit, self.place.to[name])]

    def keep(self, unit):
        rows = self.piece(unit, self.place.deep)
        return pltpu.make_async_copy(
            self.total.at[unit, rows], self.out.at[unit, rows], self.out_sem.at[unit]
        )

    def copies(self, stage, unit):
        if unit == SMALL:
            return [
                pltpu.make_async_remote_copy(
                    src_ref=self.small,
                    dst_ref=self.small_landed.at[stage],
                    send_sem=self.small_send.at[stage],
                    recv_sem=self.small_recv.at[stage],
                    device_id=self.place.to["cxyzw"[stage]],
                    device_id_type=MESH,
                )
            ]
        if stage < 3:
            return self.halve(stage, unit)
        if stage == 3:
            return self.share(unit)
        if stage == 4:
            return self.collect(unit)
        return self.double(7 - stage, unit)

    def step(self, unit):
        stage = self.stage.get(unit, -1)
        if stage >= 0:
            for copy in self.copies(stage, unit):
                copy.wait()
            if unit == SMALL:
                self.small[...] += self.small_landed[stage]
            elif stage < 3:
                self.total[unit, self.own(stage, unit), :] += self.landed[
                    unit, pl.ds(OFFSETS[stage], HALVES[stage]), :
                ]
            elif stage == 3:
                parts = [self.landed[unit, pl.ds(OFFSETS[3] + 16 * i, 16), :] for i in range(3)]
                rows = self.piece(unit, self.place.deep)
                self.total[unit, rows, :] += parts[0] + parts[1] + parts[2]
            elif stage == 4:
                self.keep(unit).wait()
        stage += 1
        self.stage[unit] = stage
        if stage < (5 if unit == SMALL else 8):
            for copy in self.copies(stage, unit):
                copy.start()
            if stage == 4 and unit != SMALL:
                self.keep(unit).start()

    def after(self, piece, *units):
        for unit in units:
            self.step(unit)
        for unit in STEPS_AFTER[piece]:
            self.step(unit)


class Spread:
    def __init__(self, place, blocks, send_sem, recv_sem):
        self.place, self.blocks = place, blocks
        self.send_sem, self.recv_sem = send_sem, recv_sem

    def copy(self, row, index, where, device):
        ref = self.blocks.at[where]
        return pltpu.make_async_remote_copy(
            src_ref=ref,
            dst_ref=ref,
            send_sem=self.send_sem.at[row, index],
            recv_sem=self.recv_sem.at[row, index],
            device_id=device,
            device_id_type=MESH,
        )

    def copies(self, row, stage):
        place = self.place
        if stage == 0:
            where = (row, place.tower, place.deep, place.flat)
            return [self.copy(row, i, where, place.along_deep(i + 1)) for i in range(3)]
        if stage == 1:
            where = (row, place.tower, slice(None), place.flat)
            return [self.copy(row, 3 + i, where, place.along_flat(i + 1)) for i in range(3)]
        return [self.copy(row, 6, (row, place.tower), place.to["c"])]

    def start(self, row, stage):
        for copy in self.copies(row, stage):
            copy.start()

    def wait(self, row, stage):
        for copy in self.copies(row, stage):
            copy.wait()


def layer_kernel(
    tokens_hbm,
    segment_ref,
    positive_ref,
    gain_one_ref,
    query_hbm,
    key_hbm,
    value_hbm,
    output_hbm,
    table_ref,
    gain_two_ref,
    inner_hbm,
    outer_hbm,
    layer_hbm,
    token_grad_hbm,
    sums_hbm,
    hidden_sum_hbm,
    rows_grad_hbm,
    small_ref,
    tokens,
    query_w,
    key_w,
    value_w,
    output_w,
    inner_w,
    outer_w,
    normed_one,
    queries,
    keys,
    values,
    probs,
    mixed,
    middle,
    normed_two,
    hidden,
    bias,
    segment_column,
    segment_row,
    pooled_all,
    hidden_sum,
    normed_one_t,
    normed_two_t,
    mixed_t,
    grad_mixed,
    grad_query,
    grad_key,
    grad_value,
    key_total,
    value_total,
    total,
    landed,
    expand,
    rounded_grads,
    small_landed,
    load_sem,
    store_sem,
    sum_send,
    sum_recv,
    sum_out,
    pool_send,
    pool_recv,
    hidden_send,
    hidden_recv,
    small_send,
    small_recv,
):
    place = Place()
    barrier = pltpu.get_barrier_semaphore()
    partners = [place.to["c"]]
    partners += [place.along_deep(i) for i in (1, 2, 3)]
    partners += [place.along_flat(i) for i in (1, 2, 3)]
    for partner in partners:
        pl.semaphore_signal(barrier, inc=1, device_id=partner, device_id_type=MESH)

    loads = [
        pltpu.make_async_copy(source, target, load_sem.at[i])
        for i, (source, target) in enumerate(
            (
                (tokens_hbm, tokens),
                (query_hbm, query_w),
                (key_hbm, key_w),
                (value_hbm, value_w),
                (output_hbm, output_w),
                (inner_hbm, inner_w),
                (outer_hbm, outer_w),
            )
        )
    ]
    for load in loads:
        load.start()

    segment_row[...] = segment_ref[...].astype(F32)
    for i in range(8):
        row = segment_row[i // 4 : i // 4 + 1, (i % 4) * 128 : (i % 4) * 128 + 128]
        segment_column[i * 128 : (i + 1) * 128, :] = jnp.broadcast_to(row, (128, 128)).T
    place_row = lax.broadcasted_iota(jnp.int32, (32, FAR), 1)
    offsets = jnp.where(place_row >= NEAR, place_row - FAR, place_row) - 256
    by_place = exact_dot(table_ref[...], bucket_onehot(offsets))
    for h in range(8):
        spread = jnp.broadcast_to(by_place[h : h + 1], (128, FAR))
        bias[h] = pltpu.roll(spread, 0, 1, stride=1, stride_axis=0)[:, :NEAR]
    lane = lax.broadcasted_iota(jnp.int32, (1, 128), 1)
    item = segment_column[...] + jnp.where(
        lax.broadcasted_iota(jnp.int32, (1024, 128), 0) >= 512, 8.0, 0.0
    )
    item = jnp.where(segment_column[...] < ITEMS_ROW, item, -1.0)
    slot = jnp.where(lane < 48, lax.rem(lane, 16), -2).astype(F32)
    expand[...] = jnp.where(item == slot, 1.0, 0.0).astype(BF)

    pooling = Spread(place, pooled_all, pool_send, pool_recv)
    hiddens = Spread(place, hidden_sum_hbm, hidden_send, hidden_recv)
    sums = Sums(
        place,
        total,
        landed,
        sums_hbm,
        small_ref,
        small_landed,
        (sum_send, sum_recv, sum_out, small_send, small_recv),
    )

    def save_hidden(row):
        return pltpu.make_async_copy(
            hidden_sum.at[row],
            hidden_sum_hbm.at[row, place.tower, place.deep, place.flat],
            store_sem.at[row],
        )

    def spread_hidden(row):
        along = (place.along_deep, place.along_flat)[row]
        for i in range(3):
            yield pltpu.make_async_remote_copy(
                src_ref=hidden_sum.at[row],
                dst_ref=hidden_sum_hbm.at[row, place.tower, place.deep, place.flat],
                send_sem=hidden_send.at[row, i],
                recv_sem=hidden_recv.at[row, i],
                device_id=along(i + 1),
                device_id_type=MESH,
            )

    def deepen_hidden():
        ref = hidden_sum_hbm.at[1, place.tower, place.deep]
        for i in range(3):
            yield pltpu.make_async_remote_copy(
                src_ref=ref,
                dst_ref=ref,
                send_sem=hidden_send.at[1, 3 + i],
                recv_sem=hidden_recv.at[1, 3 + i],
                device_id=place.along_deep(i + 1),
                device_id_type=MESH,
            )

    head_lane = lax.broadcasted_iota(jnp.int32, (1, 256), 1) // 64
    head_mask = [jnp.where(head_lane == h, 1.0, 0.0) for h in range(4)]
    head_mask_low = [mask.astype(BF) for mask in head_mask]

    def stack_heads(part):
        return jnp.concatenate([part * mask for mask in head_mask_low], 0)

    def pick_heads(part):
        return sum(part[h * 128 : (h + 1) * 128] * head_mask[h] for h in range(4))

    def project(i, carry):
        rows = tile(i, 256)
        x = tokens[rows, :].astype(F32)
        scale = lax.rsqrt(jnp.mean(x * x, axis=1, keepdims=True) + EPSILON)
        normed = (x * scale * gain_one_ref[...]).astype(BF)
        normed_one[rows, :] = normed
        queries[rows, :] = dot(normed, query_w[...]).astype(BF)
        keys[rows, :] = dot(normed, key_w[...]).astype(BF)
        values[rows, :] = dot(normed, value_w[...]).astype(BF)
        return carry

    def window(unit):
        r, b = lax.div(unit, 4), lax.rem(unit, 4)
        start = lax.div(b, 2) * 128
        own = pl.ds(pl.multiple_of(r * 512 + b * 128, 128), 128)
        near = pl.ds(pl.multiple_of(r * 512 + start, 128), 384)
        offset = pl.ds(pl.multiple_of(start - 128 * b + 256, 128), 384)
        return r, own, near, pl.ds(pl.multiple_of(start, 128), 384), offset

    def attend(unit, carry):
        r, own, near, near_row, offset = window(unit)
        column = segment_column[own, :]
        same = jnp.concatenate([column] * 3, 1) == segment_row[pl.ds(r, 1), near_row]
        for g in range(2):
            lanes = slice(g * 256, (g + 1) * 256)
            scores = dot(stack_heads(queries[own, lanes]), keys[near, lanes], NT)
            parts = []
            for h in range(4):
                part = scores[h * 128 : (h + 1) * 128] + bias[g * 4 + h, :, offset]
                part = jnp.where(same, part, -1e30)
                highest = jnp.max(part, axis=1, keepdims=True)
                exp_part = jnp.exp(part - highest)
                exp_total = jnp.sum(exp_part, axis=1, keepdims=True)
                parts.append((exp_part * (1.0 / exp_total)).astype(BF))
            stacked = jnp.concatenate(parts, 0)
            probs[unit, g] = stacked
            mixed[own, lanes] = pick_heads(dot(stacked, values[near, lanes])).astype(BF)
        return carry

    def feed(i, carry):
        rows = tile(i, 256)
        branch = dot(mixed[rows, :], output_w[...])
        mid = tokens[rows, :].astype(F32) + branch
        middle[rows, :] = mid
        scale = lax.rsqrt(jnp.mean(mid * mid, axis=1, keepdims=True) + EPSILON)
        normed = (mid * scale * gain_two_ref[...]).astype(BF)
        normed_two[rows, :] = normed
        for c in range(4):
            lanes = slice(c * 512, (c + 1) * 512)
            hidden[rows, lanes] = jnp.maximum(dot(normed, inner_w[:, lanes]), 0.0).astype(BF)
        valid = jnp.where(segment_column[rows, 0:1] < ITEMS_ROW, 1.0, 0.0)
        small_ref[3:4, :] += jnp.sum(valid * branch * branch, axis=0, keepdims=True)
        small_ref[5:6, :] += jnp.sum(valid * jnp.ones_like(branch), axis=0, keepdims=True)
        return carry

    def pool(r):
        rows = slice(r * 512, (r + 1) * 512)
        number = lax.broadcasted_iota(jnp.int32, (8, 512), 0).astype(F32)
        member = jnp.where(segment_row[r : r + 1, :] == number, 1.0, 0.0)
        member_low = jnp.concatenate([member, jnp.zeros_like(member)], 0).astype(BF)
        count = jnp.sum(member, axis=1, keepdims=True)
        hidden_part = dot(member_low, hidden[rows, :])[:8]
        hidden_sum[r] = hidden_part
        middle_part = exact_dot(member, middle[rows, :])
        pieces = split_three(hidden_part)
        stacked = jnp.concatenate([*pieces, jnp.zeros_like(pieces[0])], 0)
        branch = dot(stacked, outer_w[...])
        pooled = (middle_part + (branch[0:8] + branch[8:16] + branch[16:24])) / count
        sublane = lax.broadcasted_iota(jnp.int32, (8, 128), 0)
        ids = jnp.zeros((8, 128), F32)
        for s in range(8):
            ids = jnp.where(sublane == s, positive_ref[r * 8 + s].astype(F32), ids)
        lanes = lax.broadcasted_iota(jnp.int32, (8, 128), 1)
        extra = jnp.where(lanes == 0, ids, count)
        pooled_all[r, place.tower, place.deep, place.flat] = jnp.concatenate([pooled, extra], 1)

    small_ref[...] = jnp.zeros_like(small_ref)
    for i in range(4):
        loads[i].wait()
    lax.fori_loop(0, 2, project, 0)
    lax.fori_loop(0, 4, attend, 0)
    for i in (4, 5):
        loads[i].wait()
    lax.fori_loop(0, 2, feed, 0)
    loads[6].wait()
    pool(0)
    pl.semaphore_wait(barrier, len(partners))
    pooling.start(0, 0)
    save_hidden(0).start()
    for copy in spread_hidden(0):
        copy.start()
    lax.fori_loop(2, 4, project, 0)
    pooling.wait(0, 0)
    pooling.start(0, 1)
    save_hidden(0).wait()
    for copy in spread_hidden(0):
        copy.wait()
    hiddens.start(0, 1)
    lax.fori_loop(4, 6, attend, 0)
    pooling.wait(0, 1)
    pooling.start(0, 2)
    lax.fori_loop(6, 8, attend, 0)
    lax.fori_loop(2, 4, feed, 0)
    hiddens.wait(0, 1)
    hiddens.start(0, 2)
    pool(1)
    pooling.start(1, 0)
    save_hidden(1).start()
    for copy in spread_hidden(1):
        copy.start()

    def store_rows(source, target, i, index):
        rows = tile(i, 256)
        return pltpu.make_async_copy(source.at[rows], target.at[rows], store_sem.at[index])

    def close(i, carry):
        rows = tile(i, 256)
        branch = dot(hidden[rows, :], outer_w[...])
        result = middle[rows, :] + branch
        grad_query[rows, :] = result.astype(BF)
        valid = jnp.where(segment_column[rows, 0:1] < ITEMS_ROW, 1.0, 0.0)
        small_ref[2:3, :] += jnp.sum(valid * result * result, axis=0, keepdims=True)
        small_ref[4:5, :] += jnp.sum(valid * branch * branch, axis=0, keepdims=True)
        return carry

    def turn(i, carry):
        rows = tile(i, 128)
        normed_two_t[:, rows] = normed_two[rows, :].T
        mixed_t[:, rows] = mixed[rows, :].T
        normed_one_t[:, rows] = normed_one[rows, :].T
        return carry

    lax.fori_loop(0, 4, close, 0)
    for i in range(4):
        store_rows(grad_query, layer_hbm, i, 2 + i).start()
    pooling.wait(1, 0)
    pooling.start(1, 1)
    save_hidden(1).wait()
    for copy in spread_hidden(1):
        copy.wait()
    for copy in deepen_hidden():
        copy.start()
    lax.fori_loop(0, 8, turn, 0)
    pooling.wait(1, 1)
    pooling.start(1, 2)
    pooling.wait(0, 2)
    pooling.wait(1, 2)

    gathered = [
        jnp.concatenate([pooled_all[r, t].reshape(128, 640) for r in range(2)], 0)
        for t in range(2)
    ]
    vectors, inverse, counts, embedded = [], [], [], []
    for t in range(2):
        vector = gathered[t][:, :512]
        scale = lax.rsqrt(jnp.sum(vector * vector, axis=1, keepdims=True) + EPSILON)
        vectors.append(vector)
        inverse.append(scale)
        embedded.append(vector * scale)
        counts.append(gathered[t][:, 513:514])
    logits = exact_dot(embedded[0], embedded[1], NT) / SOFTMAX_TEMP
    highest = jnp.max(logits, axis=1, keepdims=True)
    exp_logits = jnp.exp(logits - highest)
    exp_total = jnp.sum(exp_logits, axis=1, keepdims=True)
    position = lax.broadcasted_iota(jnp.int32, (256, 256), 1)
    number = lax.rem(lax.div(position, 8), 16) * 16 + lax.div(position, 128) * 8
    number = (number + lax.rem(position, 8)).astype(F32)
    is_target = gathered[0][:, 512:513] == number
    target = jnp.sum(jnp.where(is_target, logits, 0.0), axis=1, keepdims=True)
    losses = highest + jnp.log(exp_total) - target
    loss = jnp.sum(losses, axis=0, keepdims=True) / 256
    grad_logits = (exp_logits / exp_total - jnp.where(is_target, 1.0, 0.0)) * (LOSS_SCALE / 256)
    grads = (
        exact_dot(grad_logits, embedded[1]) / SOFTMAX_TEMP,
        exact_dot(grad_logits, embedded[0], TN) / SOFTMAX_TEMP,
    )
    for t in range(2):
        along = jnp.sum(grads[t] * embedded[t], axis=1, keepdims=True)
        per_token = inverse[t] * (grads[t] - embedded[t] * along) / counts[t]
        for r in range(2):
            part = per_token[r * 128 : (r + 1) * 128]
            total[12 + 2 * r + t, 0:128] = part[:, :256]
            total[12 + 2 * r + t, 128:256] = part[:, 256:]
            rounded_grads[r, t] = per_token[r * 128 : (r + 1) * 128].astype(BF)
    save_grads = pltpu.make_async_copy(rounded_grads, rows_grad_hbm, store_sem.at[6])
    save_grads.start()
    own_parts = []
    for r in range(2):
        spot = 12 + 2 * r + place.tower
        left, right = tile(place.rows, 8), tile(place.rows + 16, 8)
        own_parts.append(jnp.concatenate([total[spot, left], total[spot, right]], 1))
    own = jnp.concatenate(own_parts, 0)
    pieces = split_three(own)
    own_low = pieces[0]
    own_split = jnp.concatenate([*pieces, jnp.zeros((80, 512), BF)], 0)

    def back_hidden(c):
        lanes = slice(c * 512, (c + 1) * 512)
        row_part = dot(own_low, outer_w[lanes, :], NT).astype(BF)
        row_part = jnp.concatenate([row_part, jnp.zeros((112, 512), BF)], 0)

        def mask(i, carry):
            rows = tile(i, 256)
            spread = dot(expand[rows, :], row_part)
            hidden[rows, lanes] = jnp.where(hidden[rows, lanes] > 0, spread, 0.0).astype(BF)
            return carry

        lax.fori_loop(0, 4, mask, 0)
        for half in range(2):
            unit = 2 * c + half
            total[unit] = dot(normed_two_t[...], hidden[:, unit * 256 : (unit + 1) * 256])
        sums.after(c, 2 * c, 2 * c + 1)

    def back_middle(i, carry):
        rows = tile(i, 256)
        grad_normed = dot(hidden[rows, :], inner_w[...], NT)
        mid = middle[rows, :]
        scale = lax.rsqrt(jnp.mean(mid * mid, axis=1, keepdims=True) + EPSILON)
        small_ref[1:2, :] += jnp.sum(grad_normed * mid * scale, axis=0, keepdims=True)
        gained = grad_normed * gain_two_ref[...]
        mean = jnp.mean(gained * mid, axis=1, keepdims=True)
        grad_mid = dot(expand[rows, :], own_split) + scale * (gained - mid * scale * scale * mean)
        middle[rows, :] = grad_mid
        rounded = grad_mid.astype(BF)
        mixed[rows, :] = rounded
        grad_mixed[rows, :] = dot(rounded, output_w[...], NT).astype(BF)
        return carry

    for c in range(4):
        back_hidden(c)
    for i in range(4):
        lax.fori_loop(i, i + 1, back_middle, 0)
        sums.after(4 + i)
    for half in range(2):
        total[8 + half] = dot(mixed_t[...], mixed[:, half * 256 : (half + 1) * 256])
    sums.after(8, 8, 9)

    for i in range(4):
        store_rows(grad_query, layer_hbm, i, 2 + i).wait()
    bias[...] = jnp.zeros_like(bias)

    def attend_back(g, unit, carry):
        r, own, near, near_row, offset = window(unit)
        lanes = slice(g * 256, (g + 1) * 256)
        grad_stack = stack_heads(grad_mixed[own, lanes])
        grad_soft = dot(grad_stack, values[near, lanes], NT)
        soft = probs[unit, g]
        parts = []
        for h in range(4):
            rows = slice(h * 128, (h + 1) * 128)
            soft_part = soft[rows].astype(F32)
            grad_part = grad_soft[rows]
            along = jnp.sum(soft_part * grad_part, axis=1, keepdims=True)
            part = (soft_part * (grad_part - along)).astype(BF)
            bias[g * 4 + h, :, offset] += part.astype(F32)
            parts.append(part)
        stacked = jnp.concatenate(parts, 0)
        grad_query[own, lanes] = pick_heads(dot(stacked, keys[near, lanes])).astype(BF)
        key_total[near, :] += dot(stacked, stack_heads(queries[own, lanes]), TN)
        value_total[near, :] += dot(soft, grad_stack, TN)
        return carry

    for g in range(2):
        lanes = slice(g * 256, (g + 1) * 256)
        key_total[...] = jnp.zeros_like(key_total)
        value_total[...] = jnp.zeros_like(value_total)
        for quarter in range(4):
            lax.fori_loop(2 * quarter, 2 * quarter + 2, functools.partial(attend_back, g), 0)
            sums.after(9 + 7 * g + quarter)
        unit, piece = 10 + 3 * g, 13 + 7 * g
        total[unit] = dot(normed_one_t[...], grad_query[:, lanes])
        sums.after(piece, unit)
        grad_key[:, lanes] = key_total[...].astype(BF)
        total[unit + 1] = dot(normed_one_t[...], grad_key[:, lanes])
        sums.after(piece + 1, unit + 1)
        grad_value[:, lanes] = value_total[...].astype(BF)
        total[unit + 2] = dot(normed_one_t[...], grad_value[:, lanes])
        sums.after(piece + 2, unit + 2)
    for copy in deepen_hidden():
        copy.wait()
    hiddens.start(1, 2)

    def back_tokens(i, carry):
        rows = tile(i, 256)
        grad_normed = (
            dot(grad_query[rows, :], query_w[...], NT)
            + dot(grad_key[rows, :], key_w[...], NT)
            + dot(grad_value[rows, :], value_w[...], NT)
        )
        x = tokens[rows, :].astype(F32)
        scale = lax.rsqrt(jnp.mean(x * x, axis=1, keepdims=True) + EPSILON)
        small_ref[0:1, :] += jnp.sum(grad_normed * x * scale, axis=0, keepdims=True)
        gained = grad_normed * gain_one_ref[...]
        mean = jnp.mean(gained * x, axis=1, keepdims=True)
        grad = middle[rows, :] + scale * (gained - x * scale * scale * mean)
        normed_one[rows, :] = grad.astype(BF)
        return carry

    for i in range(4):
        lax.fori_loop(i, i + 1, back_tokens, 0)
        store_rows(normed_one, token_grad_hbm, i, 2 + i).start()
        sums.after(23 + i)
    mirror = (
        lax.broadcasted_iota(jnp.int32, (128, 128), 0)
        + lax.broadcasted_iota(jnp.int32, (128, 128), 1)
    )
    mirror = jnp.where(mirror == 127, 1.0, 0.0)
    diagonals = []
    for h in range(8):
        turned = exact_dot(mirror, bias[h])
        wide = jnp.concatenate([turned, jnp.zeros((128, FAR - NEAR), F32)], 1)
        wide = pltpu.roll(wide, 0, 1, stride=1, stride_axis=0)
        diagonals.append(jnp.sum(wide, axis=0, keepdims=True))
    buckets = exact_dot(jnp.concatenate(diagonals, 0), bucket_onehot(place_row - 383), NT)
    small_ref[8:16, :] = jnp.concatenate([buckets, jnp.zeros((8, 480), F32)], 1)
    sums.after(27, SMALL)
    small_ref[6:7, :] = jnp.broadcast_to(loss, (1, 512))
    hiddens.wait(0, 2)
    hiddens.wait(1, 2)
    save_grads.wait()
    for i in range(4):
        store_rows(normed_one, token_grad_hbm, i, 2 + i).wait()


def closing_kernel(
    layer_hbm,
    token_grad_hbm,
    sums_hbm,
    hidden_sum_hbm,
    rows_grad_hbm,
    small_ref,
    layer_out,
    token_out,
    gain_one_out,
    query_out,
    key_out,
    value_out,
    output_out,
    position_out,
    gain_two_out,
    inner_out,
    outer_out,
    loss_out,
    square_out,
    hidden_sum,
    rows_grad,
    hidden_low,
    outer_part,
    rows_part,
    units_part,
    load_sem,
    copy_sem,
    store_sem,
):
    pairs = []
    for unit in range(8):
        pairs.append((units_part.at[unit], inner_out.at[:, pl.ds(unit * 256, 256)]))
    places = [(output_out, 0), (output_out, 1)]
    places += [(ref, g) for g in range(2) for ref in (query_out, key_out, value_out)]
    for unit, (ref, g) in enumerate(places):
        pairs.append((units_part.at[8 + unit], ref.at[:, pl.ds(g * 256, 256)]))
    pairs += [(rows_part.at[0], layer_out), (rows_part.at[1], token_out)]
    copies = [
        pltpu.make_async_copy(source, target, copy_sem.at[i])
        for i, (source, target) in enumerate(pairs)
    ]
    pairs = [(rows_grad_hbm, rows_grad), (hidden_sum_hbm, hidden_sum)]
    pairs += [(sums_hbm.at[unit], units_part.at[unit]) for unit in range(UNITS)]
    pairs += [(layer_hbm, rows_part.at[0]), (token_grad_hbm, rows_part.at[1])]
    loads = [
        pltpu.make_async_copy(source, target, load_sem.at[i])
        for i, (source, target) in enumerate(pairs)
    ]
    for load in loads:
        load.start()
    gain_one_out[...] = small_ref[0, :]
    gain_two_out[...] = small_ref[1, :]
    position_out[...] = small_ref[8:16, 0:32]
    loss_out[0] = jnp.max(small_ref[6:7, :])
    squares = jnp.sum(small_ref[2:5, :], axis=1, keepdims=True)
    valid = jnp.sum(small_ref[5:6, :], axis=1, keepdims=True)
    roots = jnp.sqrt(squares / valid)
    for i in range(3):
        square_out[i] = jnp.max(roots[i : i + 1, :])
    loads[0].wait()
    loads[1].wait()
    hidden_low[...] = hidden_sum[...].reshape(512, 2048).astype(BF)
    grads = rows_grad[...].reshape(512, 512)
    stores = []
    for c in range(4):
        rows = pl.ds(c * 512, 512)
        outer_part[rows] = dot(hidden_low[:, c * 512 : (c + 1) * 512], grads, TN)
        store = pltpu.make_async_copy(outer_part.at[rows], outer_out.at[rows], store_sem.at[c])
        store.start()
        stores.append(store)
        for i in range(4 * c, 4 * c + 4):
            loads[2 + i].wait()
            copies[i].start()
    for i in (16, 17):
        loads[2 + i].wait()
        copies[i].start()
    for copy in copies + stores:
        copy.wait()


def fast_shards(
    tokens,
    segment_ids,
    positives,
    attention_gain,
    query_weight,
    key_weight,
    value_weight,
    output_weight,
    position_table,
    feedforward_gain,
    inner_weight,
    outer_weight,
):
    block_shape = tokens.shape
    anywhere = pl.BlockSpec(memory_space=pl.ANY)
    vmem = pl.BlockSpec(memory_space=pltpu.VMEM)
    smem = pl.BlockSpec(memory_space=pltpu.SMEM)
    shape = jax.ShapeDtypeStruct
    dma = pltpu.SemaphoreType.DMA
    low = functools.partial(pltpu.VMEM, dtype=BF)
    full = functools.partial(pltpu.VMEM, dtype=F32)
    outs = pl.pallas_call(
        layer_kernel,
        out_shape=[
            shape((1024, 512), BF),
            shape((1024, 512), BF),
            shape((UNITS, 512, 256), F32),
            shape((2, 2, 4, 4, 8, 2048), F32),
            shape((2, 2, 128, 512), BF),
            shape((16, 512), F32),
        ],
        in_specs=[anywhere, vmem, smem, vmem]
        + [anywhere] * 4
        + [vmem, vmem, anywhere, anywhere],
        out_specs=[anywhere] * 5 + [vmem],
        scratch_shapes=[
            low((1024, 512)),
            low((512, 512)),
            low((512, 512)),
            low((512, 512)),
            low((512, 512)),
            low((512, 2048)),
            low((2048, 512)),
            low((1024, 512)),
            low((1024, 512)),
            low((1024, 512)),
            low((1024, 512)),
            low((8, 2, 512, 384)),
            low((1024, 512)),
            full((1024, 512)),
            low((1024, 512)),
            low((1024, 2048)),
            full((8, 128, NEAR)),
            full((1024, 128)),
            full((2, 512)),
            full((2, 2, 4, 4, 8, 640)),
            full((2, 8, 2048)),
            low((512, 1024)),
            low((512, 1024)),
            low((512, 1024)),
            low((1024, 512)),
            low((1024, 512)),
            low((1024, 512)),
            low((1024, 512)),
            full((1024, 256)),
            full((1024, 256)),
            full((UNITS, 512, 256)),
            full((UNITS, 496, 256)),
            low((1024, 128)),
            low((2, 2, 128, 512)),
            full((5, 16, 512)),
            dma((7,)),
            dma((7,)),
            dma((12, UNITS)),
            dma((12, UNITS)),
            dma((UNITS,)),
            dma((2, 7)),
            dma((2, 7)),
            dma((2, 7)),
            dma((2, 7)),
            dma((5,)),
            dma((5,)),
        ],
        compiler_params=pltpu.CompilerParams(
            collective_id=0, has_side_effects=True, vmem_limit_bytes=63 * 2**20
        ),
    )(
        tokens.reshape(1024, 512),
        segment_ids.reshape(2, 512),
        positives,
        attention_gain.reshape(1, 512),
        query_weight,
        key_weight,
        value_weight,
        output_weight,
        position_table.T,
        feedforward_gain.reshape(1, 512),
        inner_weight,
        outer_weight,
    )
    results = pl.pallas_call(
        closing_kernel,
        out_shape=[
            shape((1024, 512), BF),
            shape((1024, 512), BF),
            shape((512,), F32),
            shape((512, 512), F32),
            shape((512, 512), F32),
            shape((512, 512), F32),
            shape((512, 512), F32),
            shape((8, 32), F32),
            shape((512,), F32),
            shape((512, 2048), F32),
            shape((2048, 512), F32),
            shape((1,), F32),
            shape((3,), F32),
        ],
        in_specs=[anywhere] * 5 + [vmem],
        out_specs=[anywhere, anywhere, vmem]
        + [anywhere] * 4
        + [vmem, vmem, anywhere, anywhere, smem, smem],
        scratch_shapes=[
            full((2, 2, 4, 4, 8, 2048)),
            low((2, 2, 128, 512)),
            low((512, 2048)),
            full((2048, 512)),
            low((2, 1024, 512)),
            full((UNITS, 512, 256)),
            dma((20,)),
            dma((18,)),
            dma((4,)),
        ],
        compiler_params=pltpu.CompilerParams(vmem_limit_bytes=60 * 2**20),
    )(*outs)
    layer, token_grad, *rest = results
    return (
        layer.reshape(block_shape),
        token_grad.reshape(block_shape),
        *rest[:5],
        rest[5].T,
        *rest[6:9],
        rest[9].reshape(()),
        rest[10],
    )


def solution(mesh):
    fast = mesh.shape["tower"] == 2 and mesh.shape["rows"] == 16
    return jax.shard_map(
        fast_shards if fast else shards,
        mesh=mesh,
        in_specs=(
            P("tower", "rows", None, None),
            P("tower", "rows", None),
            P("rows"),
            P(),
            P(),
            P(),
            P(),
            P(),
            P(),
            P(),
            P(),
            P(),
        ),
        out_specs=(
            P("tower", "rows", None, None),
            P("tower", "rows", None, None),
            P(),
            P(),
            P(),
            P(),
            P(),
            P(),
            P(),
            P(),
            P(),
            P(),
            P(),
        ),
        check_vma=False,
    )
```

```python
import functools
import math

import jax
import jax.numpy as jnp
import numpy as np
from jax import lax
from jax.experimental import pallas as pl
from jax.experimental.pallas import tpu as pltpu
from jax.sharding import PartitionSpec as P

MAX_DIST = 128
ITEMS_ROW = 8


EPSILON = 1e-06
SOFTMAX_TEMP = 0.01
LOSS_SCALE = 65536.0
MATMUL_PRECISION = lax.Precision.HIGHEST


def from_partner(value, axis, apart):
    mask = 2**apart
    pairs = [(source, source ^ mask) for source in range(lax.axis_size(axis))]
    return lax.ppermute(value, axis, pairs)


def bucket_table(length, bucket_count, far_limit):
    half_count = bucket_count // 2
    exact_count = half_count // 2
    entries = []
    for offset in range(1 - length, length):
        distance = abs(offset)
        if distance < exact_count:
            within = distance
        else:
            within = exact_count + int(
                math.log(distance / exact_count)
                / math.log(far_limit / exact_count)
                * (half_count - exact_count)
            )
            within = min(within, half_count - 1)
        entries.append(within + (half_count if offset > 0 else 0))
    by_offset = np.array(entries, dtype=np.int32)
    index_grid = np.arange(length)[None, :] - np.arange(length)[:, None] + length - 1
    return (by_offset, by_offset[index_grid])


def contract_rows(left_side, right_side):
    return lax.dot_general(
        left_side, right_side, (((0,), (0,)), ((), ())), preferred_element_type=jnp.float32
    )


def times_transpose(left_side, right_side):
    return lax.dot_general(
        left_side, right_side, (((1,), (1,)), ((), ())), preferred_element_type=jnp.float32
    )


def norm_scale(values):
    return lax.rsqrt(jnp.mean(values * values, axis=1, keepdims=True) + EPSILON)


def norm_back(grad_normed, values, scale, gain):
    gained = grad_normed * gain
    return scale * (
        gained - values * scale * scale * jnp.mean(gained * values, axis=1, keepdims=True)
    )


def row_scores(query_part, key_part, segment_row, position_bias, head_count):
    length = query_part.shape[0]
    query_heads = query_part.reshape(length, head_count, -1)
    key_heads = key_part.reshape(length, head_count, -1)
    scores = (
        jnp.einsum("qhd,khd->hqk", query_heads, key_heads, preferred_element_type=jnp.float32)
        + position_bias
    )
    same_item = segment_row[:, None] == segment_row[None, :]
    return jnp.where(same_item[None], scores, -1e30)


def diagonal_sums(square):
    head_count = square.shape[0]
    length = square.shape[1]
    flipped = square[:, :, ::-1]
    padded = jnp.pad(flipped, ((0, 0), (0, 0), (0, length)))
    sheared = padded.reshape(head_count, 2 * length * length)[:, : length * (2 * length - 1)]
    sheared = sheared.reshape(head_count, length, 2 * length - 1)
    return jnp.sum(sheared, axis=1)[:, ::-1]


def shards(
    tokens,
    segment_ids,
    positives,
    attention_gain,
    query_weight,
    key_weight,
    value_weight,
    output_weight,
    position_table,
    feedforward_gain,
    inner_weight,
    outer_weight,
):
    row_count = tokens.shape[1]
    length = tokens.shape[2]
    model_width = tokens.shape[3]
    head_count = position_table.shape[1]
    inner_width = query_weight.shape[1]
    head_size = inner_width // head_count
    token_count = row_count * length
    by_offset, bucket_index = bucket_table(length, position_table.shape[0], MAX_DIST)
    position_bias = jnp.take(position_table.T, jnp.asarray(bucket_index), axis=1)
    inputs = tokens.reshape(token_count, model_width).astype(jnp.float32)
    segments = segment_ids.reshape(row_count, length)
    scale_one = norm_scale(inputs)
    normed_one = (inputs * scale_one * attention_gain).astype(jnp.bfloat16)
    query_rows = jnp.dot(normed_one, query_weight, preferred_element_type=jnp.float32).astype(
        jnp.bfloat16
    )
    key_rows = jnp.dot(normed_one, key_weight, preferred_element_type=jnp.float32).astype(
        jnp.bfloat16
    )
    value_rows = jnp.dot(normed_one, value_weight, preferred_element_type=jnp.float32).astype(
        jnp.bfloat16
    )
    query_blocks = query_rows.reshape(row_count, length, inner_width)
    key_blocks = key_rows.reshape(row_count, length, inner_width)
    value_blocks = value_rows.reshape(row_count, length, inner_width)

    def attend(packed):
        query_part, key_part, value_part, segment_row = packed
        scores = row_scores(query_part, key_part, segment_row, position_bias, head_count)
        highest = jnp.max(scores, axis=2, keepdims=True)
        exp_scores = jnp.exp(scores - highest)
        exp_total = jnp.sum(exp_scores, axis=2, keepdims=True)
        attention_probs = (exp_scores / exp_total).astype(jnp.bfloat16)
        value_heads = value_part.reshape(length, head_count, head_size)
        mixed_heads = jnp.einsum(
            "hqk,khd->qhd", attention_probs, value_heads, preferred_element_type=jnp.float32
        )
        return (
            mixed_heads.reshape(length, inner_width).astype(jnp.bfloat16),
            (highest + jnp.log(exp_total))[:, :, 0],
        )

    mixed_blocks, log_totals = lax.map(attend, (query_blocks, key_blocks, value_blocks, segments))
    mixed_rows = mixed_blocks.reshape(token_count, inner_width)
    branch_one = jnp.dot(mixed_rows, output_weight, preferred_element_type=jnp.float32)
    middle = inputs + branch_one
    scale_two = norm_scale(middle)
    normed_two = (middle * scale_two * feedforward_gain).astype(jnp.bfloat16)
    hidden = jax.nn.relu(
        jnp.dot(normed_two, inner_weight, preferred_element_type=jnp.float32)
    ).astype(jnp.bfloat16)
    branch_two = jnp.dot(hidden, outer_weight, preferred_element_type=jnp.float32)
    result = middle + branch_two
    valid_mask = (segments < ITEMS_ROW).astype(jnp.float32).reshape(token_count, 1)
    stat_terms = jnp.stack(
        [
            jnp.sum(valid_mask * result * result),
            jnp.sum(valid_mask * branch_one * branch_one),
            jnp.sum(valid_mask * branch_two * branch_two),
            jnp.sum(valid_mask),
        ]
    )
    stat_totals = lax.psum(stat_terms, ("tower", "rows"))
    member = (segments[:, None, :] == jnp.arange(ITEMS_ROW)[None, :, None]).astype(jnp.float32)
    item_sizes = jnp.sum(member, axis=2, keepdims=True)
    result_blocks = result.reshape(row_count, length, model_width)
    pooled = (
        jnp.einsum("ris,rsd->rid", member, result_blocks, precision=MATMUL_PRECISION) / item_sizes
    )
    items_here = row_count * ITEMS_ROW
    pooled = pooled.reshape(items_here, model_width)
    inverse_norm = lax.rsqrt(jnp.sum(pooled * pooled, axis=1, keepdims=True) + EPSILON)
    embedded_tokens = pooled * inverse_norm
    tower_index = lax.axis_index("tower")
    is_query = tower_index == 0
    partner = from_partner(embedded_tokens, "tower", 0)
    query_vectors = jnp.where(is_query, embedded_tokens, partner)
    document_vectors = jnp.where(is_query, partner, embedded_tokens)
    gathered_documents = lax.all_gather(document_vectors, "rows", axis=0, tiled=True)
    item_total = gathered_documents.shape[0]
    half_items = items_here // 2
    my_queries = lax.dynamic_slice_in_dim(query_vectors, tower_index * half_items, half_items, 0)
    my_targets = lax.dynamic_slice_in_dim(positives, tower_index * half_items, half_items, 0)
    similarity_scores = (
        lax.dot_general(
            my_queries,
            gathered_documents,
            (((1,), (1,)), ((), ())),
            precision=MATMUL_PRECISION,
            preferred_element_type=jnp.float32,
        )
        / SOFTMAX_TEMP
    )
    highest = jnp.max(similarity_scores, axis=1, keepdims=True)
    exp_logits = jnp.exp(similarity_scores - highest)
    exp_total = jnp.sum(exp_logits, axis=1, keepdims=True)
    log_total = highest[:, 0] + jnp.log(exp_total[:, 0])
    is_target = jnp.arange(item_total)[None, :] == my_targets[:, None]
    target = jnp.sum(jnp.where(is_target, similarity_scores, 0.0), axis=1)
    loss_part = jnp.sum(log_total - target)
    similarity_gradient = (exp_logits / exp_total - is_target.astype(jnp.float32)) * (
        LOSS_SCALE / item_total
    )
    local_gradient = (
        jnp.dot(similarity_gradient, gathered_documents, precision=MATMUL_PRECISION) / SOFTMAX_TEMP
    )
    grad_documents = lax.psum_scatter(
        lax.dot_general(
            similarity_gradient,
            my_queries,
            (((0,), (0,)), ((), ())),
            precision=MATMUL_PRECISION,
            preferred_element_type=jnp.float32,
        )
        / SOFTMAX_TEMP,
        "rows",
        scatter_dimension=0,
        tiled=True,
    )
    partner_mine, partner_documents = from_partner((local_gradient, grad_documents), "tower", 0)
    query_side = jnp.where(
        is_query,
        jnp.concatenate([local_gradient, partner_mine], 0),
        jnp.concatenate([partner_mine, local_gradient], 0),
    )
    own_grad = jnp.where(is_query, query_side, grad_documents + partner_documents)
    inner_along = jnp.sum(own_grad * embedded_tokens, axis=1, keepdims=True)
    grad_pooled = inverse_norm * (own_grad - embedded_tokens * inner_along)
    per_token = grad_pooled.reshape(row_count, ITEMS_ROW, model_width) / item_sizes
    grad_result = jnp.einsum("ris,rid->rsd", member, per_token, precision=MATMUL_PRECISION).reshape(
        token_count, model_width
    )
    grad_branch_two = grad_result.astype(jnp.bfloat16)
    outer_grad = contract_rows(hidden, grad_branch_two)
    grad_hidden = times_transpose(grad_branch_two, outer_weight)
    grad_pre = jnp.where(hidden > 0, grad_hidden, 0.0).astype(jnp.bfloat16)
    inner_grad = contract_rows(normed_two, grad_pre)
    grad_normed_two = times_transpose(grad_pre, inner_weight)
    feedforward_gain_grad = jnp.sum(grad_normed_two * middle * scale_two, axis=0)
    grad_middle = grad_result + norm_back(grad_normed_two, middle, scale_two, feedforward_gain)
    grad_branch_one = grad_middle.astype(jnp.bfloat16)
    output_grad = contract_rows(mixed_rows, grad_branch_one)
    grad_mixed = times_transpose(grad_branch_one, output_weight).astype(jnp.bfloat16)
    grad_mixed_blocks = grad_mixed.reshape(row_count, length, inner_width)

    def attend_back(running, packed):
        query_part, key_part, value_part, segment_row, row_log_total, grad_part = packed
        scores = row_scores(query_part, key_part, segment_row, position_bias, head_count)
        attention_probs = jnp.exp(scores - row_log_total[:, :, None])
        query_heads = query_part.reshape(length, head_count, head_size)
        key_heads = key_part.reshape(length, head_count, head_size)
        value_heads = value_part.reshape(length, head_count, head_size)
        grad_heads = grad_part.reshape(length, head_count, head_size)
        grad_value = jnp.einsum(
            "hqk,qhd->khd",
            attention_probs.astype(jnp.bfloat16),
            grad_heads,
            preferred_element_type=jnp.float32,
        )
        grad_probs = jnp.einsum(
            "qhd,khd->hqk", grad_heads, value_heads, preferred_element_type=jnp.float32
        )
        row_dot = jnp.sum(attention_probs * grad_probs, axis=2, keepdims=True)
        grad_scores = (attention_probs * (grad_probs - row_dot)).astype(jnp.bfloat16)
        grad_query = jnp.einsum(
            "hqk,khd->qhd", grad_scores, key_heads, preferred_element_type=jnp.float32
        )
        grad_key = jnp.einsum(
            "hqk,qhd->khd", grad_scores, query_heads, preferred_element_type=jnp.float32
        )
        outputs = (
            grad_query.reshape(length, inner_width).astype(jnp.bfloat16),
            grad_key.reshape(length, inner_width).astype(jnp.bfloat16),
            grad_value.reshape(length, inner_width).astype(jnp.bfloat16),
        )
        return (running + grad_scores.astype(jnp.float32), outputs)

    score_sum, grad_rows = lax.scan(
        attend_back,
        jnp.zeros((head_count, length, length), jnp.float32),
        (query_blocks, key_blocks, value_blocks, segments, log_totals, grad_mixed_blocks),
    )
    grad_queries = grad_rows[0].reshape(token_count, inner_width)
    grad_keys = grad_rows[1].reshape(token_count, inner_width)
    grad_values = grad_rows[2].reshape(token_count, inner_width)
    query_grad = contract_rows(normed_one, grad_queries)
    key_grad = contract_rows(normed_one, grad_keys)
    value_grad = contract_rows(normed_one, grad_values)
    grad_normed_one = (
        times_transpose(grad_queries, query_weight)
        + times_transpose(grad_keys, key_weight)
        + times_transpose(grad_values, value_weight)
    )
    attention_gain_grad = jnp.sum(grad_normed_one * inputs * scale_one, axis=0)
    token_grad = grad_middle + norm_back(grad_normed_one, inputs, scale_one, attention_gain)
    offset_onehot = jnp.asarray(
        (by_offset[:, None] == np.arange(position_table.shape[0])[None, :]).astype(np.float32)
    )
    position_grad = jnp.dot(diagonal_sums(score_sum), offset_onehot, precision=MATMUL_PRECISION).T
    closing_terms = loss_part[None]
    summed = lax.psum(
        (
            attention_gain_grad,
            query_grad,
            key_grad,
            value_grad,
            output_grad,
            position_grad,
            feedforward_gain_grad,
            inner_grad,
            outer_grad,
            closing_terms,
        ),
        ("tower", "rows"),
    )
    (
        attention_gain_grad,
        query_grad,
        key_grad,
        value_grad,
        output_grad,
        position_grad,
        feedforward_gain_grad,
        inner_grad,
        outer_grad,
        closing_totals,
    ) = summed
    contrastive_loss = closing_totals[0] / item_total
    root_mean_squares = jnp.sqrt(stat_totals[:3] / (stat_totals[3] * model_width))
    block_shape = (1, row_count, length, model_width)
    return (
        result.reshape(block_shape).astype(jnp.bfloat16),
        token_grad.reshape(block_shape).astype(jnp.bfloat16),
        attention_gain_grad,
        query_grad,
        key_grad,
        value_grad,
        output_grad,
        position_grad,
        feedforward_gain_grad,
        inner_grad,
        outer_grad,
        contrastive_loss,
        root_mean_squares,
    )


F32 = jnp.float32
BF = jnp.bfloat16
MESH = pl.DeviceIdType.MESH
NN = (((1,), (0,)), ((), ()))
NT = (((1,), (1,)), ((), ()))
TN = (((0,), (0,)), ((), ()))
WIDE = 128
UNITS = 4096 // WIDE
PER_PART = 256 // WIDE
STEPS_AFTER = (
    (),
    (0, 1, 2, 3,),
    (4, 5, 6, 7,),
    (8, 9, 10, 11, 0, 1,),
    (12, 13, 14, 15, 2, 3,),
    (),
    (4, 5, 0, 1,),
    (6, 7, 2, 3,),
    (8, 9,),
    (10, 11, 4, 5, 16, 17, 18, 19,),
    (12, 13, 14, 15, 6, 7, 8,),
    (9, 10, 0, 1, 2, 3,),
    (11, 12,),
    (13,),
    (14,),
    (15, 20, 21,),
    (22, 23, 24, 25, 4, 5, 0, 1, 2, 3,),
    (16, 17,),
    (6, 7, 8, 9, 11, 10, 18, 19, 4, 5, 13, 12, 0,),
    (14, 15, 1, 2, 20, 21, 3,),
    (),
    (6, 7,),
    (26, 27, 22, 23, 8, 9, 11, 28,),
    (29, 30, 31, 24, 25, 10, 13, 16, 17, 4, 5,),
    (12, 14, 15, 18, 19, 6, 21, 0, 7, 1, 2,),
    (20, 8, 9, 11, 10, 3,),
    (26, 27, 22, 23, 13, 16,),
    (28, 29, 12, 14, 15, 17, 0, 18, 30, 31, 1, 32, 19, 25, 24, 5, 4, 2, 21, 7, 6, 9, 8, 11, 10, 20, 3, 27, 26, 13, 22, 28, 29, 12, 23, 15, 14, 16, 30, 17, 18, 0, 19, 31, 1, 0, 32, 25, 5, 1, 24, 3, 4, 2, 16, 3, 21, 17, 18, 7, 2, 32, 19, 6, 9, 8, 5, 4, 11, 5, 10, 4, 17, 16, 20, 21, 17, 16, 27, 7, 26, 13, 18, 7, 19, 22, 18, 28, 6, 19, 29, 9, 12, 6, 8, 9, 23, 15, 11, 14, 20, 8, 10, 11, 30, 10, 21, 31, 12, 25, 23, 32, 24, 21, 13, 12, 22, 27, 13, 14, 26, 28, 15, 14, 20, 29, 32, 30, 25, 15, 23, 20, 31, 24, 22, 23, 26, 27, 28, 22, 29, 30, 31, 25, 24, 25, 27, 24, 26, 27, 29, 26, 28, 29, 31, 28, 30, 31, 30,),
)
SMALL = UNITS
PIECES = len(STEPS_AFTER)
FAR = 512
NEAR = 384
WINDOWS = ((0, 256, 128), (0, 384, 0), (128, 384, 0), (256, 256, 0))


def dot(a, b, dims=NN):
    return lax.dot_general(a, b, dims, preferred_element_type=F32)


def exact_dot(a, b, dims=NN):
    return lax.dot_general(
        a, b, dims, precision=lax.Precision.HIGHEST, preferred_element_type=F32
    )


def tile(index, size):
    if isinstance(index, int):
        return pl.ds(index * size, size)
    return pl.ds(pl.multiple_of(index * size, size), size)


def far_limits(bucket_count, far_limit):
    half_count = bucket_count // 2
    exact_count = half_count // 2
    limits = []
    reached = exact_count
    for distance in range(exact_count, 512):
        within = exact_count + int(
            math.log(distance / exact_count)
            / math.log(far_limit / exact_count)
            * (half_count - exact_count)
        )
        within = min(within, half_count - 1)
        while reached < within:
            limits.append(distance)
            reached += 1
    return limits


def bucket_onehot(offset):
    distance = jnp.abs(offset)
    far = jnp.full_like(distance, 8)
    for limit in far_limits(32, MAX_DIST):
        far = far + jnp.where(distance >= limit, 1, 0)
    bucket = jnp.where(distance < 8, distance, far) + jnp.where(offset > 0, 16, 0)
    same = bucket == lax.broadcasted_iota(jnp.int32, (32, FAR), 0)
    return jnp.where(same, 1.0, 0.0).astype(F32)


def split_three(value):
    high = value.astype(BF)
    rest = value - high.astype(F32)
    middle = rest.astype(BF)
    return high, middle, (rest - middle.astype(F32)).astype(BF)


class Place:
    def __init__(self):
        self.tower = lax.axis_index("tower")
        self.rows = lax.axis_index("rows")
        self.flat = lax.rem(self.rows, 4)
        self.deep = lax.div(self.rows, 4)
        bits = {
            "x": lax.rem(self.rows, 2),
            "y": lax.rem(lax.div(self.rows, 2), 2),
            "z": lax.rem(lax.div(self.rows, 4), 2),
            "w": lax.div(self.rows, 8),
        }
        steps = {"x": 1, "y": 2, "z": 4, "w": 8}
        self.bit = {"c": self.tower, **bits}
        self.to = {"c": self.device(1 - self.tower, self.rows)}
        for name, step in steps.items():
            self.to[name] = self.device(self.tower, self.rows + step * (1 - 2 * bits[name]))

    def device(self, tower, rows):
        return {"tower": tower, "rows": rows}

    def along_deep(self, step):
        return self.device(self.tower, lax.rem(self.deep + step, 4) * 4 + self.flat)

    def along_flat(self, step):
        return self.device(self.tower, self.deep * 4 + lax.rem(self.flat + step, 4))


def order_of(unit):
    return (("cxzyw", "cyzxw") if unit < UNITS // 2 else ("cxyZ", "cyxZ"))[unit % 2]


class Sums:
    def __init__(self, place, total, landed, out, small, small_landed, sems):
        self.place, self.total, self.landed, self.out = place, total, landed, out
        self.small, self.small_landed = small, small_landed
        self.send_sem, self.recv_sem, self.out_sem, self.small_send, self.small_recv = sems
        self.plans = {}
        self.stage = {}
        for unit in range(UNITS):
            order = order_of(unit)
            if order not in self.plans:
                self.plans[order] = self.plan(order)

    def plan(self, order):
        place, steps = self.place, []
        base, size, offset, sem = 0, 512, 0, 0
        for name in order:
            ways = 4 if name == "Z" else 2
            size //= ways
            spot = place.deep if name == "Z" else place.bit[name]
            partners = []
            for i in range(1, ways):
                if name == "Z":
                    piece, device = lax.rem(place.deep + i, 4), place.along_deep(i)
                else:
                    piece, device = 1 - spot, place.to[name]
                partners.append((base + piece * size, device, offset, sem))
                offset, sem = offset + size, sem + 1
            base = base + spot * size
            steps.append((size, base, partners))
        return steps

    def remote(self, source, target, index, unit, device):
        return pltpu.make_async_remote_copy(
            src_ref=source,
            dst_ref=target,
            send_sem=self.send_sem.at[index, unit],
            recv_sem=self.recv_sem.at[index, unit],
            device_id=device,
            device_id_type=MESH,
        )

    def depth(self, unit):
        return 5 if unit == SMALL else 2 * len(order_of(unit))

    def rows(self, start, size):
        return pl.ds(pl.multiple_of(start, size), size)

    def keep(self, unit):
        size, base, _ = self.plans[order_of(unit)][-1]
        rows = self.rows(base, size)
        return pltpu.make_async_copy(
            self.total.at[unit, rows], self.out.at[unit, rows], self.out_sem.at[unit]
        )

    def copies(self, stage, unit):
        if unit == SMALL:
            return [
                pltpu.make_async_remote_copy(
                    src_ref=self.small,
                    dst_ref=self.small_landed.at[stage],
                    send_sem=self.small_send.at[stage],
                    recv_sem=self.small_recv.at[stage],
                    device_id=self.place.to["cxyzw"[stage]],
                    device_id_type=MESH,
                )
            ]
        plan = self.plans[order_of(unit)]
        if stage < len(plan):
            size, _, partners = plan[stage]
            return [
                self.remote(
                    self.total.at[unit, self.rows(start, size)],
                    self.landed.at[unit, pl.ds(offset, size)],
                    sem,
                    unit,
                    device,
                )
                for start, device, offset, sem in partners
            ]
        back = 2 * len(plan) - 1 - stage
        size, base, partners = plan[back]
        rows = self.rows(base, size)
        source = self.total if stage == len(plan) else self.out
        return [
            self.remote(source.at[unit, rows], self.out.at[unit, rows], 6 + sem, unit, device)
            for _, device, _, sem in partners
        ]

    def step(self, unit):
        stage = self.stage.get(unit, -1)
        plan = None if unit == SMALL else self.plans[order_of(unit)]
        if stage >= 0:
            for copy in self.copies(stage, unit):
                copy.wait()
            if unit == SMALL:
                self.small[...] += self.small_landed[stage]
            elif stage < len(plan):
                size, base, partners = plan[stage]
                parts = [self.landed[unit, pl.ds(p[2], size), :] for p in partners]
                self.total[unit, self.rows(base, size), :] += sum(parts[1:], parts[0])
            elif stage == len(plan):
                self.keep(unit).wait()
        stage += 1
        self.stage[unit] = stage
        if stage < self.depth(unit):
            for copy in self.copies(stage, unit):
                copy.start()
            if plan is not None and stage == len(plan):
                self.keep(unit).start()

    def fill(self, part, value):
        for i in range(PER_PART):
            self.total[part * PER_PART + i] = value[:, i * WIDE : (i + 1) * WIDE]

    def after(self, piece, *parts):
        for part in parts:
            for i in range(PER_PART):
                self.step(part * PER_PART + i)
        if piece == PIECES - 1:
            self.step(SMALL)
        for unit in STEPS_AFTER[piece]:
            self.step(unit)


class Spread:
    def __init__(self, place, blocks, send_sem, recv_sem):
        self.place, self.blocks = place, blocks
        self.send_sem, self.recv_sem = send_sem, recv_sem

    def copy(self, row, index, where, device):
        ref = self.blocks.at[where]
        return pltpu.make_async_remote_copy(
            src_ref=ref,
            dst_ref=ref,
            send_sem=self.send_sem.at[row, index],
            recv_sem=self.recv_sem.at[row, index],
            device_id=device,
            device_id_type=MESH,
        )

    def one(self, row, i):
        place = self.place
        where = (row, place.tower, place.deep, place.flat)
        return self.copy(row, i, where, place.along_deep(i + 1))

    def copies(self, row, stage):
        place = self.place
        if stage == 0:
            return [self.one(row, i) for i in range(3)]
        if stage == 1:
            where = (row, place.tower, slice(None), place.flat)
            return [self.copy(row, 3 + i, where, place.along_flat(i + 1)) for i in range(3)]
        return [self.copy(row, 6, (row, place.tower), place.to["c"])]

    def start(self, row, stage):
        for copy in self.copies(row, stage):
            copy.start()

    def wait(self, row, stage):
        for copy in self.copies(row, stage):
            copy.wait()


def layer_kernel(
    tokens_hbm,
    segment_ref,
    positive_ref,
    gain_one_ref,
    query_hbm,
    key_hbm,
    value_hbm,
    output_hbm,
    table_ref,
    gain_two_ref,
    inner_hbm,
    outer_hbm,
    layer_hbm,
    token_grad_hbm,
    sums_hbm,
    hidden_sum_hbm,
    rows_grad_hbm,
    small_ref,
    tokens,
    query_w,
    key_w,
    value_w,
    output_w,
    inner_w,
    outer_w,
    normed_one,
    queries,
    keys,
    values,
    probs,
    side_probs,
    mixed,
    middle,
    normed_two,
    hidden,
    bias,
    segment_column,
    segment_row,
    pooled_all,
    hidden_sum,
    normed_one_t,
    normed_two_t,
    mixed_t,
    grad_mixed,
    grad_query,
    grad_key,
    grad_value,
    key_total,
    value_total,
    total,
    landed,
    expand,
    rounded_grads,
    small_landed,
    load_sem,
    store_sem,
    sum_send,
    sum_recv,
    sum_out,
    pool_send,
    pool_recv,
    hidden_send,
    hidden_recv,
    small_send,
    small_recv,
    relay_send,
    relay_recv,
):
    place = Place()
    barrier = pltpu.get_barrier_semaphore()
    partners = [place.to["c"]]
    partners += [place.along_deep(i) for i in (1, 2, 3)]
    partners += [place.along_flat(i) for i in (1, 2, 3)]
    for partner in partners:
        pl.semaphore_signal(barrier, inc=1, device_id=partner, device_id_type=MESH)

    loads = [
        pltpu.make_async_copy(source, target, load_sem.at[i])
        for i, (source, target) in enumerate(
            (
                (tokens_hbm, tokens),
                (query_hbm, query_w),
                (key_hbm, key_w),
                (value_hbm, value_w),
                (output_hbm, output_w),
                (inner_hbm, inner_w),
                (outer_hbm, outer_w),
            )
        )
    ]
    for load in loads:
        load.start()

    segment_row[...] = segment_ref[...].astype(F32)
    for i in range(8):
        row = segment_row[i // 4 : i // 4 + 1, (i % 4) * 128 : (i % 4) * 128 + 128]
        segment_column[i * 128 : (i + 1) * 128, :] = jnp.broadcast_to(row, (128, 128)).T
    place_row = lax.broadcasted_iota(jnp.int32, (32, FAR), 1)
    offsets = jnp.where(place_row >= NEAR, place_row - FAR, place_row) - 128
    by_place = exact_dot(table_ref[...], bucket_onehot(offsets))
    for h in range(8):
        spread = jnp.broadcast_to(by_place[h : h + 1], (128, FAR))
        bias[h] = pltpu.roll(spread, 0, 1, stride=1, stride_axis=0)[:, :NEAR]
    pooling = Spread(place, pooled_all, pool_send, pool_recv)
    sums = Sums(
        place,
        total,
        landed,
        sums_hbm,
        small_ref,
        small_landed,
        (sum_send, sum_recv, sum_out, small_send, small_recv),
    )

    def hidden_slot(row):
        return hidden_sum_hbm.at[row, place.tower, place.deep, place.bit["y"], place.bit["x"]]

    def save_hidden(row):
        return pltpu.make_async_copy(hidden_sum.at[row], hidden_slot(row), store_sem.at[row])

    def hidden_copy(source, target, row, index, device):
        return pltpu.make_async_remote_copy(
            src_ref=source,
            dst_ref=target,
            send_sem=hidden_send.at[row, index],
            recv_sem=hidden_recv.at[row, index],
            device_id=device,
            device_id_type=MESH,
        )

    def go(copies, start):
        for copy in copies:
            if start:
                copy.start()
            else:
                copy.wait()

    def deepen_hidden(row, start):
        source = hidden_sum.at[row]
        target = hidden_slot(row)
        copies = [
            hidden_copy(source, target, row, i - 1, place.along_deep(i)) for i in (1, 2, 3)
        ]
        go(copies, start)

    def widen_hidden(row, step, start):
        ref = hidden_sum_hbm.at[row, place.tower]
        y, x = place.bit["y"], place.bit["x"]
        left, right = pl.ds(0, 1024), pl.ds(1024, 1024)
        if step == 0:
            parts = (ref.at[:, y, x, :, left], "x"), (ref.at[:, y, x, :, right], "y")
        else:
            parts = (ref.at[:, y, :, :, left], "y"), (ref.at[:, :, x, :, right], "x")
        copies = [
            hidden_copy(part, part, row, 3 + 2 * step + i, place.to[name])
            for i, (part, name) in enumerate(parts)
        ]
        go(copies, start)

    def swap_hidden(row, start):
        ref = hidden_sum_hbm.at[row, place.tower]
        go([hidden_copy(ref, ref, row, 7, place.to["c"])], start)

    def relay(step, start):
        ref = pooled_all.at[1, place.tower, lax.rem(place.deep + 4 - step, 4), place.flat]
        copies = [
            pltpu.make_async_remote_copy(
                src_ref=ref,
                dst_ref=ref,
                send_sem=relay_send.at[step, i - 1],
                recv_sem=relay_recv.at[step, i - 1],
                device_id=place.along_flat(i),
                device_id_type=MESH,
            )
            for i in (1, 2, 3)
        ]
        go(copies, start)

    head_lane = lax.broadcasted_iota(jnp.int32, (1, 256), 1) // 64
    head_mask = [jnp.where(head_lane == h, 1.0, 0.0) for h in range(4)]
    head_mask_low = [mask.astype(BF) for mask in head_mask]

    def stack_heads(part):
        return jnp.concatenate([part * mask for mask in head_mask_low], 0)

    def pick_heads(part):
        return sum(part[h * 128 : (h + 1) * 128] * head_mask[h] for h in range(4))

    def project(i, carry):
        rows = tile(i, 256)
        x = tokens[rows, :].astype(F32)
        scale = lax.rsqrt(jnp.mean(x * x, axis=1, keepdims=True) + EPSILON)
        normed = (x * scale * gain_one_ref[...]).astype(BF)
        normed_one[rows, :] = normed
        queries[rows, :] = dot(normed, query_w[...]).astype(BF)
        keys[rows, :] = dot(normed, key_w[...]).astype(BF)
        values[rows, :] = dot(normed, value_w[...]).astype(BF)
        return carry

    def window(r, b):
        start, width, offset = WINDOWS[b]
        base = r * 512
        own = pl.ds(pl.multiple_of(base + b * 128, 128), 128)
        near = pl.ds(pl.multiple_of(base + start, 128), width)
        return own, near, slice(start, start + width), slice(offset, offset + width)

    def soft(r, b, g):
        if b in (0, 3):
            return side_probs.at[r, b // 3, g]
        return probs.at[r, b - 1, g]

    def attend(b, r, carry):
        own, near, near_row, offset = window(r, b)
        column = segment_column[own, :]
        row = segment_row[pl.ds(r, 1), near_row]
        same = jnp.concatenate([column] * (WINDOWS[b][1] // 128), 1) == row
        for g in range(2):
            lanes = slice(g * 256, (g + 1) * 256)
            scores = dot(stack_heads(queries[own, lanes]), keys[near, lanes], NT)
            parts = []
            for h in range(4):
                part = scores[h * 128 : (h + 1) * 128] + bias[g * 4 + h, :, offset]
                part = jnp.where(same, part, -1e30)
                highest = jnp.max(part, axis=1, keepdims=True)
                exp_part = jnp.exp(part - highest)
                exp_total = jnp.sum(exp_part, axis=1, keepdims=True)
                parts.append((exp_part * (1.0 / exp_total)).astype(BF))
            stacked = jnp.concatenate(parts, 0)
            soft(r, b, g)[...] = stacked
            mixed[own, lanes] = pick_heads(dot(stacked, values[near, lanes])).astype(BF)
        return carry

    def attend_row(r, blocks):
        def body(row, carry):
            for b in blocks:
                attend(b, row, 0)
            return carry

        lax.fori_loop(r, r + 1, body, 0)

    def feed(i, carry):
        rows = tile(i, 256)
        branch = dot(mixed[rows, :], output_w[...])
        mid = tokens[rows, :].astype(F32) + branch
        middle[rows, :] = mid
        scale = lax.rsqrt(jnp.mean(mid * mid, axis=1, keepdims=True) + EPSILON)
        normed = (mid * scale * gain_two_ref[...]).astype(BF)
        normed_two[rows, :] = normed
        for c in range(4):
            lanes = slice(c * 512, (c + 1) * 512)
            hidden[rows, lanes] = jnp.maximum(dot(normed, inner_w[:, lanes]), 0.0).astype(BF)
        valid = jnp.where(segment_column[rows, 0:1] < ITEMS_ROW, 1.0, 0.0)
        small_ref[3:4, :] += jnp.sum(valid * branch * branch, axis=0, keepdims=True)
        small_ref[5:6, :] += jnp.sum(valid * jnp.ones_like(branch), axis=0, keepdims=True)
        return carry

    def pool(r):
        rows = slice(r * 512, (r + 1) * 512)
        number = lax.broadcasted_iota(jnp.int32, (8, 512), 0).astype(F32)
        member = jnp.where(segment_row[r : r + 1, :] == number, 1.0, 0.0)
        member_low = jnp.concatenate([member, jnp.zeros_like(member)], 0).astype(BF)
        count = jnp.sum(member, axis=1, keepdims=True)
        hidden_part = dot(member_low, hidden[rows, :])[:8]
        hidden_sum[r] = hidden_part
        middle_part = exact_dot(member, middle[rows, :])
        pieces = split_three(hidden_part)
        stacked = jnp.concatenate([*pieces, jnp.zeros_like(pieces[0])], 0)
        branch = dot(stacked, outer_w[...])
        pooled = (middle_part + (branch[0:8] + branch[8:16] + branch[16:24])) / count
        sublane = lax.broadcasted_iota(jnp.int32, (8, 128), 0)
        ids = jnp.zeros((8, 128), F32)
        for s in range(8):
            ids = jnp.where(sublane == s, positive_ref[r * 8 + s].astype(F32), ids)
        lanes = lax.broadcasted_iota(jnp.int32, (8, 128), 1)
        extra = jnp.where(lanes == 0, ids, count)
        pooled_all[r, place.tower, place.deep, place.flat] = jnp.concatenate([pooled, extra], 1)

    small_ref[...] = jnp.zeros_like(small_ref)
    for i in range(4):
        loads[i].wait()
    lax.fori_loop(0, 2, project, 0)
    attend_row(0, (0, 1, 2, 3))
    for i in (4, 5):
        loads[i].wait()
    lax.fori_loop(0, 2, feed, 0)
    loads[6].wait()
    pool(0)
    pl.semaphore_wait(barrier, len(partners))
    pooling.start(0, 0)
    save_hidden(0).start()
    deepen_hidden(0, start=True)
    lax.fori_loop(2, 4, project, 0)
    attend_row(1, (0, 1))
    pooling.wait(0, 0)
    pooling.start(0, 1)
    attend_row(1, (2, 3))
    save_hidden(0).wait()
    deepen_hidden(0, start=False)
    widen_hidden(0, 0, start=True)
    lax.fori_loop(2, 4, feed, 0)
    pooling.wait(0, 1)
    pooling.start(0, 2)
    pool(1)
    pooling.start(1, 0)
    relay(0, start=True)
    deepen_hidden(1, start=True)
    save_hidden(1).start()

    def store_rows(source, target, i, index):
        rows = tile(i, 256)
        return pltpu.make_async_copy(source.at[rows], target.at[rows], store_sem.at[index])

    def close(i, carry):
        rows = tile(i, 256)
        branch = dot(hidden[rows, :], outer_w[...])
        result = middle[rows, :] + branch
        grad_query[rows, :] = result.astype(BF)
        valid = jnp.where(segment_column[rows, 0:1] < ITEMS_ROW, 1.0, 0.0)
        small_ref[2:3, :] += jnp.sum(valid * result * result, axis=0, keepdims=True)
        small_ref[4:5, :] += jnp.sum(valid * branch * branch, axis=0, keepdims=True)
        return carry

    def turn(i, carry):
        rows = tile(i, 128)
        normed_two_t[:, rows] = normed_two[rows, :].T
        mixed_t[:, rows] = mixed[rows, :].T
        normed_one_t[:, rows] = normed_one[rows, :].T
        return carry

    lax.fori_loop(0, 2, close, 0)
    for step in (1, 2, 3):
        if step > 1:
            lax.fori_loop(step, step + 1, close, 0)
        pooling.one(1, step - 1).wait()
        relay(step, start=True)
    for i in range(4):
        store_rows(grad_query, layer_hbm, i, 2 + i).start()
    save_hidden(1).wait()
    lax.fori_loop(0, 8, turn, 0)
    widen_hidden(0, 0, start=False)
    widen_hidden(0, 1, start=True)
    lane = lax.broadcasted_iota(jnp.int32, (1, 128), 1)
    item = segment_column[...] + jnp.where(
        lax.broadcasted_iota(jnp.int32, (1024, 128), 0) >= 512, 8.0, 0.0
    )
    item = jnp.where(segment_column[...] < ITEMS_ROW, item, -1.0)
    slot = jnp.where(lane < 48, lax.rem(lane, 16), -2).astype(F32)
    expand[...] = jnp.where(item == slot, 1.0, 0.0).astype(BF)
    for step in range(4):
        relay(step, start=False)
    pooling.start(1, 2)
    deepen_hidden(1, start=False)
    widen_hidden(1, 0, start=True)
    pooling.wait(0, 2)
    pooling.wait(1, 2)

    gathered = [
        jnp.concatenate([pooled_all[r, t].reshape(128, 640) for r in range(2)], 0)
        for t in range(2)
    ]
    vectors, inverse, counts, embedded = [], [], [], []
    for t in range(2):
        vector = gathered[t][:, :512]
        scale = lax.rsqrt(jnp.sum(vector * vector, axis=1, keepdims=True) + EPSILON)
        vectors.append(vector)
        inverse.append(scale)
        embedded.append(vector * scale)
        counts.append(gathered[t][:, 513:514])
    logits = exact_dot(embedded[0], embedded[1], NT) / SOFTMAX_TEMP
    highest = jnp.max(logits, axis=1, keepdims=True)
    exp_logits = jnp.exp(logits - highest)
    exp_total = jnp.sum(exp_logits, axis=1, keepdims=True)
    position = lax.broadcasted_iota(jnp.int32, (256, 256), 1)
    number = lax.rem(lax.div(position, 8), 16) * 16 + lax.div(position, 128) * 8
    number = (number + lax.rem(position, 8)).astype(F32)
    is_target = gathered[0][:, 512:513] == number
    target = jnp.sum(jnp.where(is_target, logits, 0.0), axis=1, keepdims=True)
    losses = highest + jnp.log(exp_total) - target
    loss = jnp.sum(losses, axis=0, keepdims=True) / 256
    grad_logits = (exp_logits / exp_total - jnp.where(is_target, 1.0, 0.0)) * (LOSS_SCALE / 256)
    grads = (
        exact_dot(grad_logits, embedded[1]) / SOFTMAX_TEMP,
        exact_dot(grad_logits, embedded[0], TN) / SOFTMAX_TEMP,
    )
    for t in range(2):
        along = jnp.sum(grads[t] * embedded[t], axis=1, keepdims=True)
        per_token = inverse[t] * (grads[t] - embedded[t] * along) / counts[t]
        for r in range(2):
            part = per_token[r * 128 : (r + 1) * 128]
            for i in range(512 // WIDE):
                total[UNITS - 4 + 2 * r + t, i * 128 : (i + 1) * 128] = part[
                    :, i * WIDE : (i + 1) * WIDE
                ]
            rounded_grads[r, t] = per_token[r * 128 : (r + 1) * 128].astype(BF)
    save_grads = pltpu.make_async_copy(rounded_grads, rows_grad_hbm, store_sem.at[6])
    save_grads.start()
    own_parts = []
    for r in range(2):
        spot = UNITS - 4 + 2 * r + place.tower
        lanes = [total[spot, tile(place.rows + 16 * i, 8)] for i in range(512 // WIDE)]
        own_parts.append(jnp.concatenate(lanes, 1))
    own = jnp.concatenate(own_parts, 0)
    pieces = split_three(own)
    own_low = pieces[0]
    own_split = jnp.concatenate([*pieces, jnp.zeros((80, 512), BF)], 0)

    def back_hidden(c):
        lanes = slice(c * 512, (c + 1) * 512)
        row_part = dot(own_low, outer_w[lanes, :], NT).astype(BF)
        row_part = jnp.concatenate([row_part, jnp.zeros((112, 512), BF)], 0)

        def mask(i, carry):
            rows = tile(i, 256)
            spread = dot(expand[rows, :], row_part)
            hidden[rows, lanes] = jnp.where(hidden[rows, lanes] > 0, spread, 0.0).astype(BF)
            return carry

        lax.fori_loop(0, 4, mask, 0)
        for half in range(2):
            part = 2 * c + half
            columns = slice(part * 256, (part + 1) * 256)
            sums.fill(part, dot(normed_two_t[...], hidden[:, columns]))
        sums.after(c, 2 * c, 2 * c + 1)

    def back_middle(i, carry):
        rows = tile(i, 256)
        grad_normed = dot(hidden[rows, :], inner_w[...], NT)
        mid = middle[rows, :]
        scale = lax.rsqrt(jnp.mean(mid * mid, axis=1, keepdims=True) + EPSILON)
        small_ref[1:2, :] += jnp.sum(grad_normed * mid * scale, axis=0, keepdims=True)
        gained = grad_normed * gain_two_ref[...]
        mean = jnp.mean(gained * mid, axis=1, keepdims=True)
        grad_mid = dot(expand[rows, :], own_split) + scale * (gained - mid * scale * scale * mean)
        middle[rows, :] = grad_mid
        rounded = grad_mid.astype(BF)
        mixed[rows, :] = rounded
        grad_mixed[rows, :] = dot(rounded, output_w[...], NT).astype(BF)
        return carry

    for c in range(4):
        back_hidden(c)
    for i in range(4):
        lax.fori_loop(i, i + 1, back_middle, 0)
        sums.after(4 + i)
    for half in range(2):
        sums.fill(8 + half, dot(mixed_t[...], mixed[:, half * 256 : (half + 1) * 256]))
    widen_hidden(1, 0, start=False)
    widen_hidden(1, 1, start=True)
    sums.after(8, 8, 9)

    for i in range(4):
        store_rows(grad_query, layer_hbm, i, 2 + i).wait()
    bias[...] = jnp.zeros_like(bias)

    def attend_back(g, b, r, carry):
        own, near, _, offset = window(r, b)
        lanes = slice(g * 256, (g + 1) * 256)
        grad_stack = stack_heads(grad_mixed[own, lanes])
        grad_soft = dot(grad_stack, values[near, lanes], NT)
        weight = soft(r, b, g)[...]
        parts = []
        for h in range(4):
            rows = slice(h * 128, (h + 1) * 128)
            soft_part = weight[rows].astype(F32)
            grad_part = grad_soft[rows]
            along = jnp.sum(soft_part * grad_part, axis=1, keepdims=True)
            part = (soft_part * (grad_part - along)).astype(BF)
            bias[g * 4 + h, :, offset] += part.astype(F32)
            parts.append(part)
        stacked = jnp.concatenate(parts, 0)
        grad_query[own, lanes] = pick_heads(dot(stacked, keys[near, lanes])).astype(BF)
        key_total[near, :] += dot(stacked, stack_heads(queries[own, lanes]), TN)
        value_total[near, :] += dot(weight, grad_stack, TN)
        return carry

    for g in range(2):
        lanes = slice(g * 256, (g + 1) * 256)
        key_total[...] = jnp.zeros_like(key_total)
        value_total[...] = jnp.zeros_like(value_total)
        for b in range(4):
            lax.fori_loop(0, 2, functools.partial(attend_back, g, b), 0)
            sums.after(9 + 7 * g + b)
        part, piece = 10 + 3 * g, 13 + 7 * g
        sums.fill(part, dot(normed_one_t[...], grad_query[:, lanes]))
        sums.after(piece, part)
        grad_key[:, lanes] = key_total[...].astype(BF)
        sums.fill(part + 1, dot(normed_one_t[...], grad_key[:, lanes]))
        sums.after(piece + 1, part + 1)
        grad_value[:, lanes] = value_total[...].astype(BF)
        sums.fill(part + 2, dot(normed_one_t[...], grad_value[:, lanes]))
        sums.after(piece + 2, part + 2)
        if g == 0:
            widen_hidden(0, 1, start=False)
            swap_hidden(0, start=True)
    widen_hidden(1, 1, start=False)
    swap_hidden(0, start=False)
    swap_hidden(1, start=True)

    def back_tokens(i, carry):
        rows = tile(i, 256)
        grad_normed = (
            dot(grad_query[rows, :], query_w[...], NT)
            + dot(grad_key[rows, :], key_w[...], NT)
            + dot(grad_value[rows, :], value_w[...], NT)
        )
        x = tokens[rows, :].astype(F32)
        scale = lax.rsqrt(jnp.mean(x * x, axis=1, keepdims=True) + EPSILON)
        small_ref[0:1, :] += jnp.sum(grad_normed * x * scale, axis=0, keepdims=True)
        gained = grad_normed * gain_one_ref[...]
        mean = jnp.mean(gained * x, axis=1, keepdims=True)
        grad = middle[rows, :] + scale * (gained - x * scale * scale * mean)
        normed_one[rows, :] = grad.astype(BF)
        return carry

    for i in range(4):
        lax.fori_loop(i, i + 1, back_tokens, 0)
        store_rows(normed_one, token_grad_hbm, i, 2 + i).start()
        sums.after(23 + i)
    mirror = (
        lax.broadcasted_iota(jnp.int32, (128, 128), 0)
        + lax.broadcasted_iota(jnp.int32, (128, 128), 1)
    )
    mirror = jnp.where(mirror == 127, 1.0, 0.0)
    diagonals = []
    for h in range(8):
        turned = exact_dot(mirror, bias[h])
        wide = jnp.concatenate([turned, jnp.zeros((128, FAR - NEAR), F32)], 1)
        wide = pltpu.roll(wide, 0, 1, stride=1, stride_axis=0)
        diagonals.append(jnp.sum(wide, axis=0, keepdims=True))
    buckets = exact_dot(jnp.concatenate(diagonals, 0), bucket_onehot(place_row - 255), NT)
    small_ref[8:16, :] = jnp.concatenate([buckets, jnp.zeros((8, 480), F32)], 1)
    sums.after(27)
    small_ref[6:7, :] = jnp.broadcast_to(loss, (1, 512))
    swap_hidden(1, start=False)
    save_grads.wait()
    for i in range(4):
        store_rows(normed_one, token_grad_hbm, i, 2 + i).wait()


def closing_kernel(
    layer_hbm,
    token_grad_hbm,
    sums_hbm,
    hidden_sum_hbm,
    rows_grad_hbm,
    small_ref,
    layer_out,
    token_out,
    gain_one_out,
    query_out,
    key_out,
    value_out,
    output_out,
    position_out,
    gain_two_out,
    inner_out,
    outer_out,
    loss_out,
    square_out,
    hidden_sum,
    rows_grad,
    hidden_low,
    outer_part,
    rows_part,
    units_part,
    load_sem,
    copy_sem,
    store_sem,
):
    pairs = []
    inner_units = 2048 // WIDE
    for unit in range(inner_units):
        pairs.append((units_part.at[unit], inner_out.at[:, pl.ds(unit * WIDE, WIDE)]))
    places = [(output_out, 0), (output_out, 256)]
    places += [(ref, g * 256) for g in range(2) for ref in (query_out, key_out, value_out)]
    for part, (ref, lane) in enumerate(places):
        for i in range(PER_PART):
            lanes = pl.ds(lane + i * WIDE, WIDE)
            pairs.append((units_part.at[inner_units + part * PER_PART + i], ref.at[:, lanes]))
    pairs += [(rows_part.at[0], layer_out), (rows_part.at[1], token_out)]
    copies = [
        pltpu.make_async_copy(source, target, copy_sem.at[i])
        for i, (source, target) in enumerate(pairs)
    ]
    pairs = [(rows_grad_hbm, rows_grad), (hidden_sum_hbm, hidden_sum)]
    pairs += [(sums_hbm.at[unit], units_part.at[unit]) for unit in range(UNITS)]
    pairs += [(layer_hbm, rows_part.at[0]), (token_grad_hbm, rows_part.at[1])]
    loads = [
        pltpu.make_async_copy(source, target, load_sem.at[i])
        for i, (source, target) in enumerate(pairs)
    ]
    for load in loads:
        load.start()
    gain_one_out[...] = small_ref[0, :]
    gain_two_out[...] = small_ref[1, :]
    position_out[...] = small_ref[8:16, 0:32]
    loss_out[0] = jnp.max(small_ref[6:7, :])
    squares = jnp.sum(small_ref[2:5, :], axis=1, keepdims=True)
    valid = jnp.sum(small_ref[5:6, :], axis=1, keepdims=True)
    roots = jnp.sqrt(squares / valid)
    for i in range(3):
        square_out[i] = jnp.max(roots[i : i + 1, :])
    loads[0].wait()
    loads[1].wait()
    hidden_low[...] = hidden_sum[...].reshape(512, 2048).astype(BF)
    grads = rows_grad[...].reshape(512, 512)
    stores = []
    for c in range(4):
        rows = pl.ds(c * 512, 512)
        outer_part[rows] = dot(hidden_low[:, c * 512 : (c + 1) * 512], grads, TN)
        store = pltpu.make_async_copy(outer_part.at[rows], outer_out.at[rows], store_sem.at[c])
        store.start()
        stores.append(store)
        for i in range(UNITS // 4 * c, UNITS // 4 * (c + 1)):
            loads[2 + i].wait()
            copies[i].start()
    for i in (UNITS, UNITS + 1):
        loads[2 + i].wait()
        copies[i].start()
    for copy in copies + stores:
        copy.wait()


def fast_shards(
    tokens,
    segment_ids,
    positives,
    attention_gain,
    query_weight,
    key_weight,
    value_weight,
    output_weight,
    position_table,
    feedforward_gain,
    inner_weight,
    outer_weight,
):
    block_shape = tokens.shape
    anywhere = pl.BlockSpec(memory_space=pl.ANY)
    vmem = pl.BlockSpec(memory_space=pltpu.VMEM)
    smem = pl.BlockSpec(memory_space=pltpu.SMEM)
    shape = jax.ShapeDtypeStruct
    dma = pltpu.SemaphoreType.DMA
    low = functools.partial(pltpu.VMEM, dtype=BF)
    full = functools.partial(pltpu.VMEM, dtype=F32)
    outs = pl.pallas_call(
        layer_kernel,
        out_shape=[
            shape((1024, 512), BF),
            shape((1024, 512), BF),
            shape((UNITS, 512, WIDE), F32),
            shape((2, 2, 4, 2, 2, 8, 2048), F32),
            shape((2, 2, 128, 512), BF),
            shape((16, 512), F32),
        ],
        in_specs=[anywhere, vmem, smem, vmem]
        + [anywhere] * 4
        + [vmem, vmem, anywhere, anywhere],
        out_specs=[anywhere] * 5 + [vmem],
        scratch_shapes=[
            low((1024, 512)),
            low((512, 512)),
            low((512, 512)),
            low((512, 512)),
            low((512, 512)),
            low((512, 2048)),
            low((2048, 512)),
            low((1024, 512)),
            low((1024, 512)),
            low((1024, 512)),
            low((1024, 512)),
            low((2, 2, 2, 512, 384)),
            low((2, 2, 2, 512, 256)),
            low((1024, 512)),
            full((1024, 512)),
            low((1024, 512)),
            low((1024, 2048)),
            full((8, 128, NEAR)),
            full((1024, 128)),
            full((2, 512)),
            full((2, 2, 4, 4, 8, 640)),
            full((2, 8, 2048)),
            low((512, 1024)),
            low((512, 1024)),
            low((512, 1024)),
            low((1024, 512)),
            low((1024, 512)),
            low((1024, 512)),
            low((1024, 512)),
            full((1024, 256)),
            full((1024, 256)),
            full((UNITS, 512, WIDE)),
            full((UNITS, 496, WIDE)),
            low((1024, 128)),
            low((2, 2, 128, 512)),
            full((5, 16, 512)),
            dma((7,)),
            dma((7,)),
            dma((12, UNITS)),
            dma((12, UNITS)),
            dma((UNITS,)),
            dma((2, 7)),
            dma((2, 7)),
            dma((2, 8)),
            dma((2, 8)),
            dma((5,)),
            dma((5,)),
            dma((4, 3)),
            dma((4, 3)),
        ],
        compiler_params=pltpu.CompilerParams(
            collective_id=0, has_side_effects=True, vmem_limit_bytes=63 * 2**20
        ),
    )(
        tokens.reshape(1024, 512),
        segment_ids.reshape(2, 512),
        positives,
        attention_gain.reshape(1, 512),
        query_weight,
        key_weight,
        value_weight,
        output_weight,
        position_table.T,
        feedforward_gain.reshape(1, 512),
        inner_weight,
        outer_weight,
    )
    results = pl.pallas_call(
        closing_kernel,
        out_shape=[
            shape((1024, 512), BF),
            shape((1024, 512), BF),
            shape((512,), F32),
            shape((512, 512), F32),
            shape((512, 512), F32),
            shape((512, 512), F32),
            shape((512, 512), F32),
            shape((8, 32), F32),
            shape((512,), F32),
            shape((512, 2048), F32),
            shape((2048, 512), F32),
            shape((1,), F32),
            shape((3,), F32),
        ],
        in_specs=[anywhere] * 5 + [vmem],
        out_specs=[anywhere, anywhere, vmem]
        + [anywhere] * 4
        + [vmem, vmem, anywhere, anywhere, smem, smem],
        scratch_shapes=[
            full((2, 2, 4, 2, 2, 8, 2048)),
            low((2, 2, 128, 512)),
            low((512, 2048)),
            full((2048, 512)),
            low((2, 1024, 512)),
            full((UNITS, 512, WIDE)),
            dma((UNITS + 4,)),
            dma((UNITS + 2,)),
            dma((4,)),
        ],
        compiler_params=pltpu.CompilerParams(vmem_limit_bytes=60 * 2**20),
    )(*outs)
    layer, token_grad, *rest = results
    return (
        layer.reshape(block_shape),
        token_grad.reshape(block_shape),
        *rest[:5],
        rest[5].T,
        *rest[6:9],
        rest[9].reshape(()),
        rest[10],
    )


def solution(mesh):
    fast = mesh.shape["tower"] == 2 and mesh.shape["rows"] == 16
    return jax.shard_map(
        fast_shards if fast else shards,
        mesh=mesh,
        in_specs=(
            P("tower", "rows", None, None),
            P("tower", "rows", None),
            P("rows"),
            P(),
            P(),
            P(),
            P(),
            P(),
            P(),
            P(),
            P(),
            P(),
        ),
        out_specs=(
            P("tower", "rows", None, None),
            P("tower", "rows", None, None),
            P(),
            P(),
            P(),
            P(),
            P(),
            P(),
            P(),
            P(),
            P(),
            P(),
            P(),
        ),
        check_vma=False,
    )
```

```python
import functools
import math

import jax
import jax.numpy as jnp
import numpy as np
from jax import lax
from jax.experimental import pallas as pl
from jax.experimental.pallas import tpu as pltpu
from jax.sharding import PartitionSpec as P

MAX_DIST = 128
ITEMS_ROW = 8


EPSILON = 1e-06
SOFTMAX_TEMP = 0.01
LOSS_SCALE = 65536.0
MATMUL_PRECISION = lax.Precision.HIGHEST


def from_partner(value, axis, apart):
    mask = 2**apart
    pairs = [(source, source ^ mask) for source in range(lax.axis_size(axis))]
    return lax.ppermute(value, axis, pairs)


def bucket_table(length, bucket_count, far_limit):
    half_count = bucket_count // 2
    exact_count = half_count // 2
    entries = []
    for offset in range(1 - length, length):
        distance = abs(offset)
        if distance < exact_count:
            within = distance
        else:
            within = exact_count + int(
                math.log(distance / exact_count)
                / math.log(far_limit / exact_count)
                * (half_count - exact_count)
            )
            within = min(within, half_count - 1)
        entries.append(within + (half_count if offset > 0 else 0))
    by_offset = np.array(entries, dtype=np.int32)
    index_grid = np.arange(length)[None, :] - np.arange(length)[:, None] + length - 1
    return (by_offset, by_offset[index_grid])


def contract_rows(left_side, right_side):
    return lax.dot_general(
        left_side, right_side, (((0,), (0,)), ((), ())), preferred_element_type=jnp.float32
    )


def times_transpose(left_side, right_side):
    return lax.dot_general(
        left_side, right_side, (((1,), (1,)), ((), ())), preferred_element_type=jnp.float32
    )


def norm_scale(values):
    return lax.rsqrt(jnp.mean(values * values, axis=1, keepdims=True) + EPSILON)


def norm_back(grad_normed, values, scale, gain):
    gained = grad_normed * gain
    return scale * (
        gained - values * scale * scale * jnp.mean(gained * values, axis=1, keepdims=True)
    )


def row_scores(query_part, key_part, segment_row, position_bias, head_count):
    length = query_part.shape[0]
    query_heads = query_part.reshape(length, head_count, -1)
    key_heads = key_part.reshape(length, head_count, -1)
    scores = (
        jnp.einsum("qhd,khd->hqk", query_heads, key_heads, preferred_element_type=jnp.float32)
        + position_bias
    )
    same_item = segment_row[:, None] == segment_row[None, :]
    return jnp.where(same_item[None], scores, -1e30)


def diagonal_sums(square):
    head_count = square.shape[0]
    length = square.shape[1]
    flipped = square[:, :, ::-1]
    padded = jnp.pad(flipped, ((0, 0), (0, 0), (0, length)))
    sheared = padded.reshape(head_count, 2 * length * length)[:, : length * (2 * length - 1)]
    sheared = sheared.reshape(head_count, length, 2 * length - 1)
    return jnp.sum(sheared, axis=1)[:, ::-1]


def shards(
    tokens,
    segment_ids,
    positives,
    attention_gain,
    query_weight,
    key_weight,
    value_weight,
    output_weight,
    position_table,
    feedforward_gain,
    inner_weight,
    outer_weight,
):
    row_count = tokens.shape[1]
    length = tokens.shape[2]
    model_width = tokens.shape[3]
    head_count = position_table.shape[1]
    inner_width = query_weight.shape[1]
    head_size = inner_width // head_count
    token_count = row_count * length
    by_offset, bucket_index = bucket_table(length, position_table.shape[0], MAX_DIST)
    position_bias = jnp.take(position_table.T, jnp.asarray(bucket_index), axis=1)
    inputs = tokens.reshape(token_count, model_width).astype(jnp.float32)
    segments = segment_ids.reshape(row_count, length)
    scale_one = norm_scale(inputs)
    normed_one = (inputs * scale_one * attention_gain).astype(jnp.bfloat16)
    query_rows = jnp.dot(normed_one, query_weight, preferred_element_type=jnp.float32).astype(
        jnp.bfloat16
    )
    key_rows = jnp.dot(normed_one, key_weight, preferred_element_type=jnp.float32).astype(
        jnp.bfloat16
    )
    value_rows = jnp.dot(normed_one, value_weight, preferred_element_type=jnp.float32).astype(
        jnp.bfloat16
    )
    query_blocks = query_rows.reshape(row_count, length, inner_width)
    key_blocks = key_rows.reshape(row_count, length, inner_width)
    value_blocks = value_rows.reshape(row_count, length, inner_width)

    def attend(packed):
        query_part, key_part, value_part, segment_row = packed
        scores = row_scores(query_part, key_part, segment_row, position_bias, head_count)
        highest = jnp.max(scores, axis=2, keepdims=True)
        exp_scores = jnp.exp(scores - highest)
        exp_total = jnp.sum(exp_scores, axis=2, keepdims=True)
        attention_probs = (exp_scores / exp_total).astype(jnp.bfloat16)
        value_heads = value_part.reshape(length, head_count, head_size)
        mixed_heads = jnp.einsum(
            "hqk,khd->qhd", attention_probs, value_heads, preferred_element_type=jnp.float32
        )
        return (
            mixed_heads.reshape(length, inner_width).astype(jnp.bfloat16),
            (highest + jnp.log(exp_total))[:, :, 0],
        )

    mixed_blocks, log_totals = lax.map(attend, (query_blocks, key_blocks, value_blocks, segments))
    mixed_rows = mixed_blocks.reshape(token_count, inner_width)
    branch_one = jnp.dot(mixed_rows, output_weight, preferred_element_type=jnp.float32)
    middle = inputs + branch_one
    scale_two = norm_scale(middle)
    normed_two = (middle * scale_two * feedforward_gain).astype(jnp.bfloat16)
    hidden = jax.nn.relu(
        jnp.dot(normed_two, inner_weight, preferred_element_type=jnp.float32)
    ).astype(jnp.bfloat16)
    branch_two = jnp.dot(hidden, outer_weight, preferred_element_type=jnp.float32)
    result = middle + branch_two
    valid_mask = (segments < ITEMS_ROW).astype(jnp.float32).reshape(token_count, 1)
    stat_terms = jnp.stack(
        [
            jnp.sum(valid_mask * result * result),
            jnp.sum(valid_mask * branch_one * branch_one),
            jnp.sum(valid_mask * branch_two * branch_two),
            jnp.sum(valid_mask),
        ]
    )
    stat_totals = lax.psum(stat_terms, ("tower", "rows"))
    member = (segments[:, None, :] == jnp.arange(ITEMS_ROW)[None, :, None]).astype(jnp.float32)
    item_sizes = jnp.sum(member, axis=2, keepdims=True)
    result_blocks = result.reshape(row_count, length, model_width)
    pooled = (
        jnp.einsum("ris,rsd->rid", member, result_blocks, precision=MATMUL_PRECISION) / item_sizes
    )
    items_here = row_count * ITEMS_ROW
    pooled = pooled.reshape(items_here, model_width)
    inverse_norm = lax.rsqrt(jnp.sum(pooled * pooled, axis=1, keepdims=True) + EPSILON)
    embedded_tokens = pooled * inverse_norm
    tower_index = lax.axis_index("tower")
    is_query = tower_index == 0
    partner = from_partner(embedded_tokens, "tower", 0)
    query_vectors = jnp.where(is_query, embedded_tokens, partner)
    document_vectors = jnp.where(is_query, partner, embedded_tokens)
    gathered_documents = lax.all_gather(document_vectors, "rows", axis=0, tiled=True)
    item_total = gathered_documents.shape[0]
    half_items = items_here // 2
    my_queries = lax.dynamic_slice_in_dim(query_vectors, tower_index * half_items, half_items, 0)
    my_targets = lax.dynamic_slice_in_dim(positives, tower_index * half_items, half_items, 0)
    similarity_scores = (
        lax.dot_general(
            my_queries,
            gathered_documents,
            (((1,), (1,)), ((), ())),
            precision=MATMUL_PRECISION,
            preferred_element_type=jnp.float32,
        )
        / SOFTMAX_TEMP
    )
    highest = jnp.max(similarity_scores, axis=1, keepdims=True)
    exp_logits = jnp.exp(similarity_scores - highest)
    exp_total = jnp.sum(exp_logits, axis=1, keepdims=True)
    log_total = highest[:, 0] + jnp.log(exp_total[:, 0])
    is_target = jnp.arange(item_total)[None, :] == my_targets[:, None]
    target = jnp.sum(jnp.where(is_target, similarity_scores, 0.0), axis=1)
    loss_part = jnp.sum(log_total - target)
    similarity_gradient = (exp_logits / exp_total - is_target.astype(jnp.float32)) * (
        LOSS_SCALE / item_total
    )
    local_gradient = (
        jnp.dot(similarity_gradient, gathered_documents, precision=MATMUL_PRECISION) / SOFTMAX_TEMP
    )
    grad_documents = lax.psum_scatter(
        lax.dot_general(
            similarity_gradient,
            my_queries,
            (((0,), (0,)), ((), ())),
            precision=MATMUL_PRECISION,
            preferred_element_type=jnp.float32,
        )
        / SOFTMAX_TEMP,
        "rows",
        scatter_dimension=0,
        tiled=True,
    )
    partner_mine, partner_documents = from_partner((local_gradient, grad_documents), "tower", 0)
    query_side = jnp.where(
        is_query,
        jnp.concatenate([local_gradient, partner_mine], 0),
        jnp.concatenate([partner_mine, local_gradient], 0),
    )
    own_grad = jnp.where(is_query, query_side, grad_documents + partner_documents)
    inner_along = jnp.sum(own_grad * embedded_tokens, axis=1, keepdims=True)
    grad_pooled = inverse_norm * (own_grad - embedded_tokens * inner_along)
    per_token = grad_pooled.reshape(row_count, ITEMS_ROW, model_width) / item_sizes
    grad_result = jnp.einsum("ris,rid->rsd", member, per_token, precision=MATMUL_PRECISION).reshape(
        token_count, model_width
    )
    grad_branch_two = grad_result.astype(jnp.bfloat16)
    outer_grad = contract_rows(hidden, grad_branch_two)
    grad_hidden = times_transpose(grad_branch_two, outer_weight)
    grad_pre = jnp.where(hidden > 0, grad_hidden, 0.0).astype(jnp.bfloat16)
    inner_grad = contract_rows(normed_two, grad_pre)
    grad_normed_two = times_transpose(grad_pre, inner_weight)
    feedforward_gain_grad = jnp.sum(grad_normed_two * middle * scale_two, axis=0)
    grad_middle = grad_result + norm_back(grad_normed_two, middle, scale_two, feedforward_gain)
    grad_branch_one = grad_middle.astype(jnp.bfloat16)
    output_grad = contract_rows(mixed_rows, grad_branch_one)
    grad_mixed = times_transpose(grad_branch_one, output_weight).astype(jnp.bfloat16)
    grad_mixed_blocks = grad_mixed.reshape(row_count, length, inner_width)

    def attend_back(running, packed):
        query_part, key_part, value_part, segment_row, row_log_total, grad_part = packed
        scores = row_scores(query_part, key_part, segment_row, position_bias, head_count)
        attention_probs = jnp.exp(scores - row_log_total[:, :, None])
        query_heads = query_part.reshape(length, head_count, head_size)
        key_heads = key_part.reshape(length, head_count, head_size)
        value_heads = value_part.reshape(length, head_count, head_size)
        grad_heads = grad_part.reshape(length, head_count, head_size)
        grad_value = jnp.einsum(
            "hqk,qhd->khd",
            attention_probs.astype(jnp.bfloat16),
            grad_heads,
            preferred_element_type=jnp.float32,
        )
        grad_probs = jnp.einsum(
            "qhd,khd->hqk", grad_heads, value_heads, preferred_element_type=jnp.float32
        )
        row_dot = jnp.sum(attention_probs * grad_probs, axis=2, keepdims=True)
        grad_scores = (attention_probs * (grad_probs - row_dot)).astype(jnp.bfloat16)
        grad_query = jnp.einsum(
            "hqk,khd->qhd", grad_scores, key_heads, preferred_element_type=jnp.float32
        )
        grad_key = jnp.einsum(
            "hqk,qhd->khd", grad_scores, query_heads, preferred_element_type=jnp.float32
        )
        outputs = (
            grad_query.reshape(length, inner_width).astype(jnp.bfloat16),
            grad_key.reshape(length, inner_width).astype(jnp.bfloat16),
            grad_value.reshape(length, inner_width).astype(jnp.bfloat16),
        )
        return (running + grad_scores.astype(jnp.float32), outputs)

    score_sum, grad_rows = lax.scan(
        attend_back,
        jnp.zeros((head_count, length, length), jnp.float32),
        (query_blocks, key_blocks, value_blocks, segments, log_totals, grad_mixed_blocks),
    )
    grad_queries = grad_rows[0].reshape(token_count, inner_width)
    grad_keys = grad_rows[1].reshape(token_count, inner_width)
    grad_values = grad_rows[2].reshape(token_count, inner_width)
    query_grad = contract_rows(normed_one, grad_queries)
    key_grad = contract_rows(normed_one, grad_keys)
    value_grad = contract_rows(normed_one, grad_values)
    grad_normed_one = (
        times_transpose(grad_queries, query_weight)
        + times_transpose(grad_keys, key_weight)
        + times_transpose(grad_values, value_weight)
    )
    attention_gain_grad = jnp.sum(grad_normed_one * inputs * scale_one, axis=0)
    token_grad = grad_middle + norm_back(grad_normed_one, inputs, scale_one, attention_gain)
    offset_onehot = jnp.asarray(
        (by_offset[:, None] == np.arange(position_table.shape[0])[None, :]).astype(np.float32)
    )
    position_grad = jnp.dot(diagonal_sums(score_sum), offset_onehot, precision=MATMUL_PRECISION).T
    closing_terms = loss_part[None]
    summed = lax.psum(
        (
            attention_gain_grad,
            query_grad,
            key_grad,
            value_grad,
            output_grad,
            position_grad,
            feedforward_gain_grad,
            inner_grad,
            outer_grad,
            closing_terms,
        ),
        ("tower", "rows"),
    )
    (
        attention_gain_grad,
        query_grad,
        key_grad,
        value_grad,
        output_grad,
        position_grad,
        feedforward_gain_grad,
        inner_grad,
        outer_grad,
        closing_totals,
    ) = summed
    contrastive_loss = closing_totals[0] / item_total
    root_mean_squares = jnp.sqrt(stat_totals[:3] / (stat_totals[3] * model_width))
    block_shape = (1, row_count, length, model_width)
    return (
        result.reshape(block_shape).astype(jnp.bfloat16),
        token_grad.reshape(block_shape).astype(jnp.bfloat16),
        attention_gain_grad,
        query_grad,
        key_grad,
        value_grad,
        output_grad,
        position_grad,
        feedforward_gain_grad,
        inner_grad,
        outer_grad,
        contrastive_loss,
        root_mean_squares,
    )


F32 = jnp.float32
BF = jnp.bfloat16
MESH = pl.DeviceIdType.MESH
NN = (((1,), (0,)), ((), ()))
NT = (((1,), (1,)), ((), ()))
TN = (((0,), (0,)), ((), ()))
WIDE = 128
UNITS = 4096 // WIDE
PER_PART = 256 // WIDE
STEPS_AFTER = (
    (),
    (0, 1, 2, 3,),
    (4, 5, 6, 7,),
    (8, 9, 10, 11, 0, 1,),
    (12, 13, 14, 15, 2, 3,),
    (),
    (4, 5, 0, 1,),
    (6, 7, 2, 3,),
    (8, 9,),
    (10, 11, 4, 5, 16, 17, 18, 19,),
    (12, 13, 14, 15, 6, 7, 8,),
    (9, 10, 0, 1, 2, 3,),
    (11, 12,),
    (13,),
    (14,),
    (15, 20, 21,),
    (22, 23, 24, 25, 4, 5, 0, 1, 2, 3,),
    (16, 17,),
    (6, 7, 8, 9, 11, 10, 18, 19, 4, 5, 13, 12, 0,),
    (14, 15, 1, 2, 20, 21, 3,),
    (),
    (6, 7,),
    (26, 27, 22, 23, 8, 9, 11, 28,),
    (29, 30, 31, 24, 25, 10, 13, 16, 17, 4, 5,),
    (12, 14, 15, 18, 19, 6, 21, 0, 7, 1, 2,),
    (20, 8, 9, 11, 10, 3,),
    (26, 27, 22, 23, 13, 16,),
    (28, 29, 12, 14, 15, 17, 0, 18, 30, 31, 1, 32, 19, 25, 24, 5, 4, 2, 21, 7, 6, 9, 8, 11, 10, 20, 3, 27, 26, 13, 22, 28, 29, 12, 23, 15, 14, 16, 30, 17, 18, 0, 19, 31, 1, 0, 32, 25, 5, 1, 24, 3, 4, 2, 16, 3, 21, 17, 18, 7, 2, 32, 19, 6, 9, 8, 5, 4, 11, 5, 10, 4, 17, 16, 20, 21, 17, 16, 27, 7, 26, 13, 18, 7, 19, 22, 18, 28, 6, 19, 29, 9, 12, 6, 8, 9, 23, 15, 11, 14, 20, 8, 10, 11, 30, 10, 21, 31, 12, 25, 23, 32, 24, 21, 13, 12, 22, 27, 13, 14, 26, 28, 15, 14, 20, 29, 32, 30, 25, 15, 23, 20, 31, 24, 22, 23, 26, 27, 28, 22, 29, 30, 31, 25, 24, 25, 27, 24, 26, 27, 29, 26, 28, 29, 31, 28, 30, 31, 30,),
)
SMALL = UNITS
PIECES = len(STEPS_AFTER)
FAR = 512
NEAR = 384
WINDOWS = ((0, 256, 128), (0, 384, 0), (128, 384, 0), (256, 256, 0))


def dot(a, b, dims=NN):
    return lax.dot_general(a, b, dims, preferred_element_type=F32)


def exact_dot(a, b, dims=NN):
    return lax.dot_general(
        a, b, dims, precision=lax.Precision.HIGHEST, preferred_element_type=F32
    )


def tile(index, size):
    if isinstance(index, int):
        return pl.ds(index * size, size)
    return pl.ds(pl.multiple_of(index * size, size), size)


def far_limits(bucket_count, far_limit):
    half_count = bucket_count // 2
    exact_count = half_count // 2
    limits = []
    reached = exact_count
    for distance in range(exact_count, 512):
        within = exact_count + int(
            math.log(distance / exact_count)
            / math.log(far_limit / exact_count)
            * (half_count - exact_count)
        )
        within = min(within, half_count - 1)
        while reached < within:
            limits.append(distance)
            reached += 1
    return limits


def bucket_onehot(offset):
    distance = jnp.abs(offset)
    far = jnp.full_like(distance, 8)
    for limit in far_limits(32, MAX_DIST):
        far = far + jnp.where(distance >= limit, 1, 0)
    bucket = jnp.where(distance < 8, distance, far) + jnp.where(offset > 0, 16, 0)
    same = bucket == lax.broadcasted_iota(jnp.int32, (32, FAR), 0)
    return jnp.where(same, 1.0, 0.0).astype(F32)


def split_three(value):
    high = value.astype(BF)
    rest = value - high.astype(F32)
    middle = rest.astype(BF)
    return high, middle, (rest - middle.astype(F32)).astype(BF)


class Place:
    def __init__(self):
        self.tower = lax.axis_index("tower")
        self.rows = lax.axis_index("rows")
        self.flat = lax.rem(self.rows, 4)
        self.deep = lax.div(self.rows, 4)
        bits = {
            "x": lax.rem(self.rows, 2),
            "y": lax.rem(lax.div(self.rows, 2), 2),
            "z": lax.rem(lax.div(self.rows, 4), 2),
            "w": lax.div(self.rows, 8),
        }
        steps = {"x": 1, "y": 2, "z": 4, "w": 8}
        self.bit = {"c": self.tower, **bits}
        self.to = {"c": self.device(1 - self.tower, self.rows)}
        for name, step in steps.items():
            self.to[name] = self.device(self.tower, self.rows + step * (1 - 2 * bits[name]))

    def device(self, tower, rows):
        return {"tower": tower, "rows": rows}

    def along_deep(self, step):
        return self.device(self.tower, lax.rem(self.deep + step, 4) * 4 + self.flat)

    def along_flat(self, step):
        return self.device(self.tower, self.deep * 4 + lax.rem(self.flat + step, 4))


def order_of(unit):
    return (("cxzyw", "cyzxw") if unit < UNITS // 2 else ("cxyZ", "cyxZ"))[unit % 2]


class Sums:
    def __init__(self, place, total, landed, out, small, small_landed, sems):
        self.place, self.total, self.landed, self.out = place, total, landed, out
        self.small, self.small_landed = small, small_landed
        self.send_sem, self.recv_sem, self.out_sem, self.small_send, self.small_recv = sems
        self.plans = {}
        self.stage = {}
        for unit in range(UNITS):
            order = order_of(unit)
            if order not in self.plans:
                self.plans[order] = self.plan(order)

    def plan(self, order):
        place, steps = self.place, []
        base, size, offset, sem = 0, 512, 0, 0
        for name in order:
            ways = 4 if name == "Z" else 2
            size //= ways
            spot = place.deep if name == "Z" else place.bit[name]
            partners = []
            for i in range(1, ways):
                if name == "Z":
                    piece, device = lax.rem(place.deep + i, 4), place.along_deep(i)
                else:
                    piece, device = 1 - spot, place.to[name]
                partners.append((base + piece * size, device, offset, sem))
                offset, sem = offset + size, sem + 1
            base = base + spot * size
            steps.append((size, base, partners))
        return steps

    def remote(self, source, target, index, unit, device):
        return pltpu.make_async_remote_copy(
            src_ref=source,
            dst_ref=target,
            send_sem=self.send_sem.at[index, unit],
            recv_sem=self.recv_sem.at[index, unit],
            device_id=device,
            device_id_type=MESH,
        )

    def depth(self, unit):
        return 5 if unit == SMALL else 2 * len(order_of(unit))

    def rows(self, start, size):
        return pl.ds(pl.multiple_of(start, size), size)

    def keep(self, unit):
        size, base, _ = self.plans[order_of(unit)][-1]
        rows = self.rows(base, size)
        return pltpu.make_async_copy(
            self.total.at[unit, rows], self.out.at[unit, rows], self.out_sem.at[unit]
        )

    def copies(self, stage, unit):
        if unit == SMALL:
            return [
                pltpu.make_async_remote_copy(
                    src_ref=self.small,
                    dst_ref=self.small_landed.at[stage],
                    send_sem=self.small_send.at[stage],
                    recv_sem=self.small_recv.at[stage],
                    device_id=self.place.to["cxyzw"[stage]],
                    device_id_type=MESH,
                )
            ]
        plan = self.plans[order_of(unit)]
        if stage < len(plan):
            size, _, partners = plan[stage]
            return [
                self.remote(
                    self.total.at[unit, self.rows(start, size)],
                    self.landed.at[unit, pl.ds(offset, size)],
                    sem,
                    unit,
                    device,
                )
                for start, device, offset, sem in partners
            ]
        back = 2 * len(plan) - 1 - stage
        size, base, partners = plan[back]
        rows = self.rows(base, size)
        source = self.total if stage == len(plan) else self.out
        return [
            self.remote(source.at[unit, rows], self.out.at[unit, rows], 6 + sem, unit, device)
            for _, device, _, sem in partners
        ]

    def step(self, unit):
        stage = self.stage.get(unit, -1)
        plan = None if unit == SMALL else self.plans[order_of(unit)]
        if stage >= 0:
            for copy in self.copies(stage, unit):
                copy.wait()
            if unit == SMALL:
                self.small[...] += self.small_landed[stage]
            elif stage < len(plan):
                size, base, partners = plan[stage]
                parts = [self.landed[unit, pl.ds(p[2], size), :] for p in partners]
                self.total[unit, self.rows(base, size), :] += sum(parts[1:], parts[0])
            elif stage == len(plan):
                self.keep(unit).wait()
        stage += 1
        self.stage[unit] = stage
        if stage < self.depth(unit):
            for copy in self.copies(stage, unit):
                copy.start()
            if plan is not None and stage == len(plan):
                self.keep(unit).start()

    def fill(self, part, value):
        for i in range(PER_PART):
            self.total[part * PER_PART + i] = value[:, i * WIDE : (i + 1) * WIDE]

    def after(self, piece, *parts):
        for part in parts:
            for i in range(PER_PART):
                self.step(part * PER_PART + i)
        if piece == PIECES - 1:
            self.step(SMALL)
        for unit in STEPS_AFTER[piece]:
            self.step(unit)


class Spread:
    def __init__(self, place, blocks, send_sem, recv_sem):
        self.place, self.blocks = place, blocks
        self.send_sem, self.recv_sem = send_sem, recv_sem

    def copy(self, row, index, where, device):
        ref = self.blocks.at[where]
        return pltpu.make_async_remote_copy(
            src_ref=ref,
            dst_ref=ref,
            send_sem=self.send_sem.at[row, index],
            recv_sem=self.recv_sem.at[row, index],
            device_id=device,
            device_id_type=MESH,
        )

    def one(self, row, i):
        place = self.place
        where = (row, place.tower, place.deep, place.flat)
        return self.copy(row, i, where, place.along_deep(i + 1))

    def copies(self, row, stage):
        place = self.place
        if stage == 0:
            return [self.one(row, i) for i in range(3)]
        if stage == 1:
            where = (row, place.tower, slice(None), place.flat)
            return [self.copy(row, 3 + i, where, place.along_flat(i + 1)) for i in range(3)]
        return [self.copy(row, 6, (row, place.tower), place.to["c"])]

    def start(self, row, stage):
        for copy in self.copies(row, stage):
            copy.start()

    def wait(self, row, stage):
        for copy in self.copies(row, stage):
            copy.wait()


def layer_kernel(
    tokens_hbm,
    segment_ref,
    positive_ref,
    gain_one_ref,
    query_hbm,
    key_hbm,
    value_hbm,
    output_hbm,
    table_ref,
    gain_two_ref,
    inner_hbm,
    outer_hbm,
    layer_hbm,
    token_grad_hbm,
    sums_hbm,
    hidden_sum_hbm,
    rows_grad_hbm,
    small_ref,
    tokens,
    query_w,
    key_w,
    value_w,
    output_w,
    inner_w,
    outer_w,
    normed_one,
    queries,
    keys,
    values,
    probs,
    side_probs,
    mixed,
    middle,
    normed_two,
    hidden,
    bias,
    segment_column,
    segment_row,
    pooled_all,
    hidden_sum,
    normed_one_t,
    normed_two_t,
    mixed_t,
    grad_mixed,
    grad_query,
    grad_key,
    grad_value,
    key_total,
    value_total,
    total,
    landed,
    expand,
    rounded_grads,
    small_landed,
    load_sem,
    store_sem,
    sum_send,
    sum_recv,
    sum_out,
    pool_send,
    pool_recv,
    hidden_send,
    hidden_recv,
    small_send,
    small_recv,
    relay_send,
    relay_recv,
):
    place = Place()
    barrier = pltpu.get_barrier_semaphore()
    partners = [place.to["c"]]
    partners += [place.along_deep(i) for i in (1, 2, 3)]
    partners += [place.along_flat(i) for i in (1, 2, 3)]
    for partner in partners:
        pl.semaphore_signal(barrier, inc=1, device_id=partner, device_id_type=MESH)

    loads = [
        pltpu.make_async_copy(source, target, load_sem.at[i])
        for i, (source, target) in enumerate(
            (
                (tokens_hbm, tokens),
                (query_hbm, query_w),
                (key_hbm, key_w),
                (value_hbm, value_w),
                (output_hbm, output_w),
                (inner_hbm, inner_w),
                (outer_hbm, outer_w),
            )
        )
    ]
    for load in loads:
        load.start()

    segment_row[...] = segment_ref[...].astype(F32)
    for i in range(8):
        row = segment_row[i // 4 : i // 4 + 1, (i % 4) * 128 : (i % 4) * 128 + 128]
        segment_column[i * 128 : (i + 1) * 128, :] = jnp.broadcast_to(row, (128, 128)).T
    place_row = lax.broadcasted_iota(jnp.int32, (32, FAR), 1)
    offsets = jnp.where(place_row >= NEAR, place_row - FAR, place_row) - 128
    by_place = exact_dot(table_ref[...], bucket_onehot(offsets))
    for h in range(8):
        spread = jnp.broadcast_to(by_place[h : h + 1], (128, FAR))
        bias[h] = pltpu.roll(spread, 0, 1, stride=1, stride_axis=0)[:, :NEAR]
    pooling = Spread(place, pooled_all, pool_send, pool_recv)
    sums = Sums(
        place,
        total,
        landed,
        sums_hbm,
        small_ref,
        small_landed,
        (sum_send, sum_recv, sum_out, small_send, small_recv),
    )

    def hidden_slot(row):
        return hidden_sum_hbm.at[row, place.tower, place.deep, place.bit["y"], place.bit["x"]]

    def save_hidden(row):
        return pltpu.make_async_copy(hidden_sum.at[row], hidden_slot(row), store_sem.at[row])

    def hidden_copy(source, target, row, index, device):
        return pltpu.make_async_remote_copy(
            src_ref=source,
            dst_ref=target,
            send_sem=hidden_send.at[row, index],
            recv_sem=hidden_recv.at[row, index],
            device_id=device,
            device_id_type=MESH,
        )

    def go(copies, start):
        for copy in copies:
            if start:
                copy.start()
            else:
                copy.wait()

    def deepen_hidden(row, start):
        source = hidden_sum.at[row]
        target = hidden_slot(row)
        copies = [
            hidden_copy(source, target, row, i - 1, place.along_deep(i)) for i in (1, 2, 3)
        ]
        go(copies, start)

    def widen_hidden(row, step, start):
        ref = hidden_sum_hbm.at[row, place.tower]
        y, x = place.bit["y"], place.bit["x"]
        left, right = pl.ds(0, 1024), pl.ds(1024, 1024)
        if step == 0:
            parts = (ref.at[:, y, x, :, left], "x"), (ref.at[:, y, x, :, right], "y")
        else:
            parts = (ref.at[:, y, :, :, left], "y"), (ref.at[:, :, x, :, right], "x")
        copies = [
            hidden_copy(part, part, row, 3 + 2 * step + i, place.to[name])
            for i, (part, name) in enumerate(parts)
        ]
        go(copies, start)

    def swap_hidden(row, start):
        ref = hidden_sum_hbm.at[row, place.tower]
        go([hidden_copy(ref, ref, row, 7, place.to["c"])], start)

    def relay(step, start):
        ref = pooled_all.at[1, place.tower, lax.rem(place.deep + 4 - step, 4), place.flat]
        copies = [
            pltpu.make_async_remote_copy(
                src_ref=ref,
                dst_ref=ref,
                send_sem=relay_send.at[step, i - 1],
                recv_sem=relay_recv.at[step, i - 1],
                device_id=place.along_flat(i),
                device_id_type=MESH,
            )
            for i in (1, 2, 3)
        ]
        go(copies, start)

    head_lane = lax.broadcasted_iota(jnp.int32, (1, 256), 1) // 64
    head_mask = [jnp.where(head_lane == h, 1.0, 0.0) for h in range(4)]
    head_mask_low = [mask.astype(BF) for mask in head_mask]

    def stack_heads(part):
        return jnp.concatenate([part * mask for mask in head_mask_low], 0)

    def pick_heads(part):
        return sum(part[h * 128 : (h + 1) * 128] * head_mask[h] for h in range(4))

    def project(i, carry):
        rows = tile(i, 256)
        x = tokens[rows, :].astype(F32)
        scale = lax.rsqrt(jnp.mean(x * x, axis=1, keepdims=True) + EPSILON)
        normed = (x * scale * gain_one_ref[...]).astype(BF)
        normed_one[rows, :] = normed
        queries[rows, :] = dot(normed, query_w[...]).astype(BF)
        keys[rows, :] = dot(normed, key_w[...]).astype(BF)
        values[rows, :] = dot(normed, value_w[...]).astype(BF)
        return carry

    def window(r, b):
        start, width, offset = WINDOWS[b]
        base = r * 512
        own = pl.ds(pl.multiple_of(base + b * 128, 128), 128)
        near = pl.ds(pl.multiple_of(base + start, 128), width)
        return own, near, slice(start, start + width), slice(offset, offset + width)

    def soft(r, b, g):
        if b in (0, 3):
            return side_probs.at[r, b // 3, g]
        return probs.at[r, b - 1, g]

    def attend(b, r, carry):
        own, near, near_row, offset = window(r, b)
        column = segment_column[own, :]
        row = segment_row[pl.ds(r, 1), near_row]
        same = jnp.concatenate([column] * (WINDOWS[b][1] // 128), 1) == row
        for g in range(2):
            lanes = slice(g * 256, (g + 1) * 256)
            scores = dot(stack_heads(queries[own, lanes]), keys[near, lanes], NT)
            parts = []
            for h in range(4):
                part = scores[h * 128 : (h + 1) * 128] + bias[g * 4 + h, :, offset]
                part = jnp.where(same, part, -1e30)
                highest = jnp.max(part, axis=1, keepdims=True)
                exp_part = jnp.exp(part - highest)
                exp_total = jnp.sum(exp_part, axis=1, keepdims=True)
                parts.append((exp_part * (1.0 / exp_total)).astype(BF))
            stacked = jnp.concatenate(parts, 0)
            soft(r, b, g)[...] = stacked
            mixed[own, lanes] = pick_heads(dot(stacked, values[near, lanes])).astype(BF)
        return carry

    def feed(i, carry):
        rows = tile(i, 256)
        branch = dot(mixed[rows, :], output_w[...])
        mid = tokens[rows, :].astype(F32) + branch
        middle[rows, :] = mid
        scale = lax.rsqrt(jnp.mean(mid * mid, axis=1, keepdims=True) + EPSILON)
        normed = (mid * scale * gain_two_ref[...]).astype(BF)
        normed_two[rows, :] = normed
        for c in range(4):
            lanes = slice(c * 512, (c + 1) * 512)
            hidden[rows, lanes] = jnp.maximum(dot(normed, inner_w[:, lanes]), 0.0).astype(BF)
        valid = jnp.where(segment_column[rows, 0:1] < ITEMS_ROW, 1.0, 0.0)
        small_ref[3:4, :] += jnp.sum(valid * branch * branch, axis=0, keepdims=True)
        small_ref[5:6, :] += jnp.sum(valid * jnp.ones_like(branch), axis=0, keepdims=True)
        return carry

    def pool(r):
        rows = tile(r, 512)
        number = lax.broadcasted_iota(jnp.int32, (8, 512), 0).astype(F32)
        member = jnp.where(segment_row[pl.ds(r, 1), :] == number, 1.0, 0.0)
        member_low = jnp.concatenate([member, jnp.zeros_like(member)], 0).astype(BF)
        count = jnp.sum(member, axis=1, keepdims=True)
        hidden_part = dot(member_low, hidden[rows, :])[:8]
        hidden_sum[r] = hidden_part
        middle_part = exact_dot(member, middle[rows, :])
        pieces = split_three(hidden_part)
        stacked = jnp.concatenate([*pieces, jnp.zeros_like(pieces[0])], 0)
        branch = dot(stacked, outer_w[...])
        pooled = (middle_part + (branch[0:8] + branch[8:16] + branch[16:24])) / count
        sublane = lax.broadcasted_iota(jnp.int32, (8, 128), 0)
        ids = jnp.zeros((8, 128), F32)
        for s in range(8):
            ids = jnp.where(sublane == s, positive_ref[r * 8 + s].astype(F32), ids)
        lanes = lax.broadcasted_iota(jnp.int32, (8, 128), 1)
        extra = jnp.where(lanes == 0, ids, count)
        pooled_all[r, place.tower, place.deep, place.flat] = jnp.concatenate([pooled, extra], 1)

    small_ref[...] = jnp.zeros_like(small_ref)
    for i in range(4):
        loads[i].wait()
    pl.semaphore_wait(barrier, len(partners))

    def forward(r, carry):
        first, second = r == 0, r == 1
        lax.fori_loop(2 * r, 2 * r + 2, project, 0)
        attend(0, r, 0)
        attend(1, r, 0)

        @pl.when(second)
        def _():
            pooling.wait(0, 0)
            pooling.start(0, 1)

        attend(2, r, 0)
        attend(3, r, 0)

        @pl.when(first)
        def _():
            for i in (4, 5):
                loads[i].wait()

        @pl.when(second)
        def _():
            save_hidden(0).wait()
            deepen_hidden(0, start=False)
            widen_hidden(0, 0, start=True)

        lax.fori_loop(2 * r, 2 * r + 2, feed, 0)

        @pl.when(first)
        def _():
            loads[6].wait()

        @pl.when(second)
        def _():
            pooling.wait(0, 1)
            pooling.start(0, 2)

        pool(r)
        pooling.start(r, 0)

        @pl.when(second)
        def _():
            relay(0, start=True)

        deepen_hidden(r, start=True)
        save_hidden(r).start()
        return carry

    lax.fori_loop(0, 2, forward, 0)

    def store_rows(source, target, i, index):
        rows = tile(i, 256)
        return pltpu.make_async_copy(source.at[rows], target.at[rows], store_sem.at[index])

    def close(i, carry):
        rows = tile(i, 256)
        branch = dot(hidden[rows, :], outer_w[...])
        result = middle[rows, :] + branch
        grad_query[rows, :] = result.astype(BF)
        valid = jnp.where(segment_column[rows, 0:1] < ITEMS_ROW, 1.0, 0.0)
        small_ref[2:3, :] += jnp.sum(valid * result * result, axis=0, keepdims=True)
        small_ref[4:5, :] += jnp.sum(valid * branch * branch, axis=0, keepdims=True)
        return carry

    def turn(i, carry):
        rows = tile(i, 128)
        normed_two_t[:, rows] = normed_two[rows, :].T
        mixed_t[:, rows] = mixed[rows, :].T
        normed_one_t[:, rows] = normed_one[rows, :].T
        return carry

    lax.fori_loop(0, 3, close, 0)
    for step in (1, 2, 3):
        if step == 3:
            lax.fori_loop(3, 4, close, 0)
        pooling.one(1, step - 1).wait()
        relay(step, start=True)
    for i in range(4):
        store_rows(grad_query, layer_hbm, i, 2 + i).start()
    save_hidden(1).wait()
    lax.fori_loop(0, 8, turn, 0)
    widen_hidden(0, 0, start=False)
    widen_hidden(0, 1, start=True)
    lane = lax.broadcasted_iota(jnp.int32, (1, 128), 1)
    item = segment_column[...] + jnp.where(
        lax.broadcasted_iota(jnp.int32, (1024, 128), 0) >= 512, 8.0, 0.0
    )
    item = jnp.where(segment_column[...] < ITEMS_ROW, item, -1.0)
    slot = jnp.where(lane < 48, lax.rem(lane, 16), -2).astype(F32)
    expand[...] = jnp.where(item == slot, 1.0, 0.0).astype(BF)
    for step in range(4):
        relay(step, start=False)
    pooling.start(1, 2)
    deepen_hidden(1, start=False)
    widen_hidden(1, 0, start=True)
    pooling.wait(0, 2)
    pooling.wait(1, 2)

    gathered = [
        jnp.concatenate([pooled_all[r, t].reshape(128, 640) for r in range(2)], 0)
        for t in range(2)
    ]
    vectors, inverse, counts, embedded = [], [], [], []
    for t in range(2):
        vector = gathered[t][:, :512]
        scale = lax.rsqrt(jnp.sum(vector * vector, axis=1, keepdims=True) + EPSILON)
        vectors.append(vector)
        inverse.append(scale)
        embedded.append(vector * scale)
        counts.append(gathered[t][:, 513:514])
    logits = exact_dot(embedded[0], embedded[1], NT) / SOFTMAX_TEMP
    highest = jnp.max(logits, axis=1, keepdims=True)
    exp_logits = jnp.exp(logits - highest)
    exp_total = jnp.sum(exp_logits, axis=1, keepdims=True)
    position = lax.broadcasted_iota(jnp.int32, (256, 256), 1)
    number = lax.rem(lax.div(position, 8), 16) * 16 + lax.div(position, 128) * 8
    number = (number + lax.rem(position, 8)).astype(F32)
    is_target = gathered[0][:, 512:513] == number
    target = jnp.sum(jnp.where(is_target, logits, 0.0), axis=1, keepdims=True)
    losses = highest + jnp.log(exp_total) - target
    loss = jnp.sum(losses, axis=0, keepdims=True) / 256
    grad_logits = (exp_logits / exp_total - jnp.where(is_target, 1.0, 0.0)) * (LOSS_SCALE / 256)
    grads = (
        exact_dot(grad_logits, embedded[1]) / SOFTMAX_TEMP,
        exact_dot(grad_logits, embedded[0], TN) / SOFTMAX_TEMP,
    )
    for t in range(2):
        along = jnp.sum(grads[t] * embedded[t], axis=1, keepdims=True)
        per_token = inverse[t] * (grads[t] - embedded[t] * along) / counts[t]
        for r in range(2):
            part = per_token[r * 128 : (r + 1) * 128]
            for i in range(512 // WIDE):
                total[UNITS - 4 + 2 * r + t, i * 128 : (i + 1) * 128] = part[
                    :, i * WIDE : (i + 1) * WIDE
                ]
            rounded_grads[r, t] = per_token[r * 128 : (r + 1) * 128].astype(BF)
    save_grads = pltpu.make_async_copy(rounded_grads, rows_grad_hbm, store_sem.at[6])
    save_grads.start()
    own_parts = []
    for r in range(2):
        spot = UNITS - 4 + 2 * r + place.tower
        lanes = [total[spot, tile(place.rows + 16 * i, 8)] for i in range(512 // WIDE)]
        own_parts.append(jnp.concatenate(lanes, 1))
    own = jnp.concatenate(own_parts, 0)
    pieces = split_three(own)
    own_low = pieces[0]
    own_split = jnp.concatenate([*pieces, jnp.zeros((80, 512), BF)], 0)

    def back_hidden(c):
        lanes = slice(c * 512, (c + 1) * 512)
        row_part = dot(own_low, outer_w[lanes, :], NT).astype(BF)
        row_part = jnp.concatenate([row_part, jnp.zeros((112, 512), BF)], 0)

        def mask(i, carry):
            rows = tile(i, 256)
            spread = dot(expand[rows, :], row_part)
            hidden[rows, lanes] = jnp.where(hidden[rows, lanes] > 0, spread, 0.0).astype(BF)
            return carry

        lax.fori_loop(0, 4, mask, 0)
        for half in range(2):
            part = 2 * c + half
            columns = slice(part * 256, (part + 1) * 256)
            sums.fill(part, dot(normed_two_t[...], hidden[:, columns]))
        sums.after(c, 2 * c, 2 * c + 1)

    def back_middle(i, carry):
        rows = tile(i, 256)
        grad_normed = dot(hidden[rows, :], inner_w[...], NT)
        mid = middle[rows, :]
        scale = lax.rsqrt(jnp.mean(mid * mid, axis=1, keepdims=True) + EPSILON)
        small_ref[1:2, :] += jnp.sum(grad_normed * mid * scale, axis=0, keepdims=True)
        gained = grad_normed * gain_two_ref[...]
        mean = jnp.mean(gained * mid, axis=1, keepdims=True)
        grad_mid = dot(expand[rows, :], own_split) + scale * (gained - mid * scale * scale * mean)
        middle[rows, :] = grad_mid
        rounded = grad_mid.astype(BF)
        mixed[rows, :] = rounded
        grad_mixed[rows, :] = dot(rounded, output_w[...], NT).astype(BF)
        return carry

    for c in range(4):
        back_hidden(c)
    for i in range(2):
        lax.fori_loop(2 * i, 2 * i + 2, back_middle, 0)
        sums.after(4 + 2 * i)
        sums.after(5 + 2 * i)
    for half in range(2):
        sums.fill(8 + half, dot(mixed_t[...], mixed[:, half * 256 : (half + 1) * 256]))
    widen_hidden(1, 0, start=False)
    widen_hidden(1, 1, start=True)
    sums.after(8, 8, 9)

    for i in range(4):
        store_rows(grad_query, layer_hbm, i, 2 + i).wait()
    bias[...] = jnp.zeros_like(bias)

    def attend_back(g, b, r, carry):
        own, near, _, offset = window(r, b)
        lanes = slice(g * 256, (g + 1) * 256)
        grad_stack = stack_heads(grad_mixed[own, lanes])
        grad_soft = dot(grad_stack, values[near, lanes], NT)
        weight = soft(r, b, g)[...]
        parts = []
        for h in range(4):
            rows = slice(h * 128, (h + 1) * 128)
            soft_part = weight[rows].astype(F32)
            grad_part = grad_soft[rows]
            along = jnp.sum(soft_part * grad_part, axis=1, keepdims=True)
            part = (soft_part * (grad_part - along)).astype(BF)
            bias[g * 4 + h, :, offset] += part.astype(F32)
            parts.append(part)
        stacked = jnp.concatenate(parts, 0)
        grad_query[own, lanes] = pick_heads(dot(stacked, keys[near, lanes])).astype(BF)
        key_total[near, :] += dot(stacked, stack_heads(queries[own, lanes]), TN)
        value_total[near, :] += dot(weight, grad_stack, TN)
        return carry

    for g in range(2):
        lanes = slice(g * 256, (g + 1) * 256)
        key_total[...] = jnp.zeros_like(key_total)
        value_total[...] = jnp.zeros_like(value_total)
        for b in range(4):
            lax.fori_loop(0, 2, functools.partial(attend_back, g, b), 0)
            sums.after(9 + 7 * g + b)
        part, piece = 10 + 3 * g, 13 + 7 * g
        sums.fill(part, dot(normed_one_t[...], grad_query[:, lanes]))
        sums.after(piece, part)
        grad_key[:, lanes] = key_total[...].astype(BF)
        sums.fill(part + 1, dot(normed_one_t[...], grad_key[:, lanes]))
        sums.after(piece + 1, part + 1)
        grad_value[:, lanes] = value_total[...].astype(BF)
        sums.fill(part + 2, dot(normed_one_t[...], grad_value[:, lanes]))
        sums.after(piece + 2, part + 2)
        if g == 0:
            widen_hidden(0, 1, start=False)
            swap_hidden(0, start=True)
    widen_hidden(1, 1, start=False)
    swap_hidden(0, start=False)
    swap_hidden(1, start=True)

    def back_tokens(i, carry):
        rows = tile(i, 256)
        grad_normed = (
            dot(grad_query[rows, :], query_w[...], NT)
            + dot(grad_key[rows, :], key_w[...], NT)
            + dot(grad_value[rows, :], value_w[...], NT)
        )
        x = tokens[rows, :].astype(F32)
        scale = lax.rsqrt(jnp.mean(x * x, axis=1, keepdims=True) + EPSILON)
        small_ref[0:1, :] += jnp.sum(grad_normed * x * scale, axis=0, keepdims=True)
        gained = grad_normed * gain_one_ref[...]
        mean = jnp.mean(gained * x, axis=1, keepdims=True)
        grad = middle[rows, :] + scale * (gained - x * scale * scale * mean)
        normed_one[rows, :] = grad.astype(BF)
        return carry

    for i in range(2):
        lax.fori_loop(2 * i, 2 * i + 2, back_tokens, 0)
        for j in (2 * i, 2 * i + 1):
            store_rows(normed_one, token_grad_hbm, j, 2 + j).start()
            sums.after(23 + j)
    mirror = (
        lax.broadcasted_iota(jnp.int32, (128, 128), 0)
        + lax.broadcasted_iota(jnp.int32, (128, 128), 1)
    )
    mirror = jnp.where(mirror == 127, 1.0, 0.0)
    diagonals = []
    for h in range(8):
        turned = exact_dot(mirror, bias[h])
        wide = jnp.concatenate([turned, jnp.zeros((128, FAR - NEAR), F32)], 1)
        wide = pltpu.roll(wide, 0, 1, stride=1, stride_axis=0)
        diagonals.append(jnp.sum(wide, axis=0, keepdims=True))
    buckets = exact_dot(jnp.concatenate(diagonals, 0), bucket_onehot(place_row - 255), NT)
    small_ref[8:16, :] = jnp.concatenate([buckets, jnp.zeros((8, 480), F32)], 1)
    sums.after(27)
    small_ref[6:7, :] = jnp.broadcast_to(loss, (1, 512))
    swap_hidden(1, start=False)
    save_grads.wait()
    for i in range(4):
        store_rows(normed_one, token_grad_hbm, i, 2 + i).wait()


def closing_kernel(
    layer_hbm,
    token_grad_hbm,
    sums_hbm,
    hidden_sum_hbm,
    rows_grad_hbm,
    small_ref,
    layer_out,
    token_out,
    gain_one_out,
    query_out,
    key_out,
    value_out,
    output_out,
    position_out,
    gain_two_out,
    inner_out,
    outer_out,
    loss_out,
    square_out,
    hidden_sum,
    rows_grad,
    hidden_low,
    outer_part,
    rows_part,
    units_part,
    load_sem,
    copy_sem,
    store_sem,
):
    pairs = []
    inner_units = 2048 // WIDE
    for unit in range(inner_units):
        pairs.append((units_part.at[unit], inner_out.at[:, pl.ds(unit * WIDE, WIDE)]))
    places = [(output_out, 0), (output_out, 256)]
    places += [(ref, g * 256) for g in range(2) for ref in (query_out, key_out, value_out)]
    for part, (ref, lane) in enumerate(places):
        for i in range(PER_PART):
            lanes = pl.ds(lane + i * WIDE, WIDE)
            pairs.append((units_part.at[inner_units + part * PER_PART + i], ref.at[:, lanes]))
    pairs += [(rows_part.at[0], layer_out), (rows_part.at[1], token_out)]
    copies = [
        pltpu.make_async_copy(source, target, copy_sem.at[i])
        for i, (source, target) in enumerate(pairs)
    ]
    pairs = [(rows_grad_hbm, rows_grad), (hidden_sum_hbm, hidden_sum)]
    pairs += [(sums_hbm.at[unit], units_part.at[unit]) for unit in range(UNITS)]
    pairs += [(layer_hbm, rows_part.at[0]), (token_grad_hbm, rows_part.at[1])]
    loads = [
        pltpu.make_async_copy(source, target, load_sem.at[i])
        for i, (source, target) in enumerate(pairs)
    ]
    for load in loads:
        load.start()
    gain_one_out[...] = small_ref[0, :]
    gain_two_out[...] = small_ref[1, :]
    position_out[...] = small_ref[8:16, 0:32]
    loss_out[0] = jnp.max(small_ref[6:7, :])
    squares = jnp.sum(small_ref[2:5, :], axis=1, keepdims=True)
    valid = jnp.sum(small_ref[5:6, :], axis=1, keepdims=True)
    roots = jnp.sqrt(squares / valid)
    for i in range(3):
        square_out[i] = jnp.max(roots[i : i + 1, :])
    loads[0].wait()
    loads[1].wait()
    hidden_low[...] = hidden_sum[...].reshape(512, 2048).astype(BF)
    grads = rows_grad[...].reshape(512, 512)
    stores = []
    for c in range(4):
        rows = pl.ds(c * 512, 512)
        outer_part[rows] = dot(hidden_low[:, c * 512 : (c + 1) * 512], grads, TN)
        store = pltpu.make_async_copy(outer_part.at[rows], outer_out.at[rows], store_sem.at[c])
        store.start()
        stores.append(store)
        for i in range(UNITS // 4 * c, UNITS // 4 * (c + 1)):
            loads[2 + i].wait()
            copies[i].start()
    for i in (UNITS, UNITS + 1):
        loads[2 + i].wait()
        copies[i].start()
    for copy in copies + stores:
        copy.wait()


def fast_shards(
    tokens,
    segment_ids,
    positives,
    attention_gain,
    query_weight,
    key_weight,
    value_weight,
    output_weight,
    position_table,
    feedforward_gain,
    inner_weight,
    outer_weight,
):
    block_shape = tokens.shape
    anywhere = pl.BlockSpec(memory_space=pl.ANY)
    vmem = pl.BlockSpec(memory_space=pltpu.VMEM)
    smem = pl.BlockSpec(memory_space=pltpu.SMEM)
    shape = jax.ShapeDtypeStruct
    dma = pltpu.SemaphoreType.DMA
    low = functools.partial(pltpu.VMEM, dtype=BF)
    full = functools.partial(pltpu.VMEM, dtype=F32)
    outs = pl.pallas_call(
        layer_kernel,
        out_shape=[
            shape((1024, 512), BF),
            shape((1024, 512), BF),
            shape((UNITS, 512, WIDE), F32),
            shape((2, 2, 4, 2, 2, 8, 2048), F32),
            shape((2, 2, 128, 512), BF),
            shape((16, 512), F32),
        ],
        in_specs=[anywhere, vmem, smem, vmem]
        + [anywhere] * 4
        + [vmem, vmem, anywhere, anywhere],
        out_specs=[anywhere] * 5 + [vmem],
        scratch_shapes=[
            low((1024, 512)),
            low((512, 512)),
            low((512, 512)),
            low((512, 512)),
            low((512, 512)),
            low((512, 2048)),
            low((2048, 512)),
            low((1024, 512)),
            low((1024, 512)),
            low((1024, 512)),
            low((1024, 512)),
            low((2, 2, 2, 512, 384)),
            low((2, 2, 2, 512, 256)),
            low((1024, 512)),
            full((1024, 512)),
            low((1024, 512)),
            low((1024, 2048)),
            full((8, 128, NEAR)),
            full((1024, 128)),
            full((2, 512)),
            full((2, 2, 4, 4, 8, 640)),
            full((2, 8, 2048)),
            low((512, 1024)),
            low((512, 1024)),
            low((512, 1024)),
            low((1024, 512)),
            low((1024, 512)),
            low((1024, 512)),
            low((1024, 512)),
            full((1024, 256)),
            full((1024, 256)),
            full((UNITS, 512, WIDE)),
            full((UNITS, 496, WIDE)),
            low((1024, 128)),
            low((2, 2, 128, 512)),
            full((5, 16, 512)),
            dma((7,)),
            dma((7,)),
            dma((12, UNITS)),
            dma((12, UNITS)),
            dma((UNITS,)),
            dma((2, 7)),
            dma((2, 7)),
            dma((2, 8)),
            dma((2, 8)),
            dma((5,)),
            dma((5,)),
            dma((4, 3)),
            dma((4, 3)),
        ],
        compiler_params=pltpu.CompilerParams(
            collective_id=0, has_side_effects=True, vmem_limit_bytes=63 * 2**20
        ),
    )(
        tokens.reshape(1024, 512),
        segment_ids.reshape(2, 512),
        positives,
        attention_gain.reshape(1, 512),
        query_weight,
        key_weight,
        value_weight,
        output_weight,
        position_table.T,
        feedforward_gain.reshape(1, 512),
        inner_weight,
        outer_weight,
    )
    results = pl.pallas_call(
        closing_kernel,
        out_shape=[
            shape((1024, 512), BF),
            shape((1024, 512), BF),
            shape((512,), F32),
            shape((512, 512), F32),
            shape((512, 512), F32),
            shape((512, 512), F32),
            shape((512, 512), F32),
            shape((8, 32), F32),
            shape((512,), F32),
            shape((512, 2048), F32),
            shape((2048, 512), F32),
            shape((1,), F32),
            shape((3,), F32),
        ],
        in_specs=[anywhere] * 5 + [vmem],
        out_specs=[anywhere, anywhere, vmem]
        + [anywhere] * 4
        + [vmem, vmem, anywhere, anywhere, smem, smem],
        scratch_shapes=[
            full((2, 2, 4, 2, 2, 8, 2048)),
            low((2, 2, 128, 512)),
            low((512, 2048)),
            full((2048, 512)),
            low((2, 1024, 512)),
            full((UNITS, 512, WIDE)),
            dma((UNITS + 4,)),
            dma((UNITS + 2,)),
            dma((4,)),
        ],
        compiler_params=pltpu.CompilerParams(vmem_limit_bytes=60 * 2**20),
    )(*outs)
    layer, token_grad, *rest = results
    return (
        layer.reshape(block_shape),
        token_grad.reshape(block_shape),
        *rest[:5],
        rest[5].T,
        *rest[6:9],
        rest[9].reshape(()),
        rest[10],
    )


def solution(mesh):
    fast = mesh.shape["tower"] == 2 and mesh.shape["rows"] == 16
    return jax.shard_map(
        fast_shards if fast else shards,
        mesh=mesh,
        in_specs=(
            P("tower", "rows", None, None),
            P("tower", "rows", None),
            P("rows"),
            P(),
            P(),
            P(),
            P(),
            P(),
            P(),
            P(),
            P(),
            P(),
        ),
        out_specs=(
            P("tower", "rows", None, None),
            P("tower", "rows", None, None),
            P(),
            P(),
            P(),
            P(),
            P(),
            P(),
            P(),
            P(),
            P(),
            P(),
            P(),
        ),
        check_vma=False,
    )
```

```python
import functools
import math

import jax
import jax.numpy as jnp
import numpy as np
from jax import lax
from jax.experimental import pallas as pl
from jax.experimental.pallas import tpu as pltpu
from jax.sharding import PartitionSpec as P

MAX_DIST = 128
ITEMS_ROW = 8


EPSILON = 1e-06
SOFTMAX_TEMP = 0.01
LOSS_SCALE = 65536.0
MATMUL_PRECISION = lax.Precision.HIGHEST


def from_partner(value, axis, apart):
    mask = 2**apart
    pairs = [(source, source ^ mask) for source in range(lax.axis_size(axis))]
    return lax.ppermute(value, axis, pairs)


def bucket_table(length, bucket_count, far_limit):
    half_count = bucket_count // 2
    exact_count = half_count // 2
    entries = []
    for offset in range(1 - length, length):
        distance = abs(offset)
        if distance < exact_count:
            within = distance
        else:
            within = exact_count + int(
                math.log(distance / exact_count)
                / math.log(far_limit / exact_count)
                * (half_count - exact_count)
            )
            within = min(within, half_count - 1)
        entries.append(within + (half_count if offset > 0 else 0))
    by_offset = np.array(entries, dtype=np.int32)
    index_grid = np.arange(length)[None, :] - np.arange(length)[:, None] + length - 1
    return (by_offset, by_offset[index_grid])


def contract_rows(left_side, right_side):
    return lax.dot_general(
        left_side, right_side, (((0,), (0,)), ((), ())), preferred_element_type=jnp.float32
    )


def times_transpose(left_side, right_side):
    return lax.dot_general(
        left_side, right_side, (((1,), (1,)), ((), ())), preferred_element_type=jnp.float32
    )


def norm_scale(values):
    return lax.rsqrt(jnp.mean(values * values, axis=1, keepdims=True) + EPSILON)


def norm_back(grad_normed, values, scale, gain):
    gained = grad_normed * gain
    return scale * (
        gained - values * scale * scale * jnp.mean(gained * values, axis=1, keepdims=True)
    )


def row_scores(query_part, key_part, segment_row, position_bias, head_count):
    length = query_part.shape[0]
    query_heads = query_part.reshape(length, head_count, -1)
    key_heads = key_part.reshape(length, head_count, -1)
    scores = (
        jnp.einsum("qhd,khd->hqk", query_heads, key_heads, preferred_element_type=jnp.float32)
        + position_bias
    )
    same_item = segment_row[:, None] == segment_row[None, :]
    return jnp.where(same_item[None], scores, -1e30)


def diagonal_sums(square):
    head_count = square.shape[0]
    length = square.shape[1]
    flipped = square[:, :, ::-1]
    padded = jnp.pad(flipped, ((0, 0), (0, 0), (0, length)))
    sheared = padded.reshape(head_count, 2 * length * length)[:, : length * (2 * length - 1)]
    sheared = sheared.reshape(head_count, length, 2 * length - 1)
    return jnp.sum(sheared, axis=1)[:, ::-1]


def shards(
    tokens,
    segment_ids,
    positives,
    attention_gain,
    query_weight,
    key_weight,
    value_weight,
    output_weight,
    position_table,
    feedforward_gain,
    inner_weight,
    outer_weight,
):
    row_count = tokens.shape[1]
    length = tokens.shape[2]
    model_width = tokens.shape[3]
    head_count = position_table.shape[1]
    inner_width = query_weight.shape[1]
    head_size = inner_width // head_count
    token_count = row_count * length
    by_offset, bucket_index = bucket_table(length, position_table.shape[0], MAX_DIST)
    position_bias = jnp.take(position_table.T, jnp.asarray(bucket_index), axis=1)
    inputs = tokens.reshape(token_count, model_width).astype(jnp.float32)
    segments = segment_ids.reshape(row_count, length)
    scale_one = norm_scale(inputs)
    normed_one = (inputs * scale_one * attention_gain).astype(jnp.bfloat16)
    query_rows = jnp.dot(normed_one, query_weight, preferred_element_type=jnp.float32).astype(
        jnp.bfloat16
    )
    key_rows = jnp.dot(normed_one, key_weight, preferred_element_type=jnp.float32).astype(
        jnp.bfloat16
    )
    value_rows = jnp.dot(normed_one, value_weight, preferred_element_type=jnp.float32).astype(
        jnp.bfloat16
    )
    query_blocks = query_rows.reshape(row_count, length, inner_width)
    key_blocks = key_rows.reshape(row_count, length, inner_width)
    value_blocks = value_rows.reshape(row_count, length, inner_width)

    def attend(packed):
        query_part, key_part, value_part, segment_row = packed
        scores = row_scores(query_part, key_part, segment_row, position_bias, head_count)
        highest = jnp.max(scores, axis=2, keepdims=True)
        exp_scores = jnp.exp(scores - highest)
        exp_total = jnp.sum(exp_scores, axis=2, keepdims=True)
        attention_probs = (exp_scores / exp_total).astype(jnp.bfloat16)
        value_heads = value_part.reshape(length, head_count, head_size)
        mixed_heads = jnp.einsum(
            "hqk,khd->qhd", attention_probs, value_heads, preferred_element_type=jnp.float32
        )
        return (
            mixed_heads.reshape(length, inner_width).astype(jnp.bfloat16),
            (highest + jnp.log(exp_total))[:, :, 0],
        )

    mixed_blocks, log_totals = lax.map(attend, (query_blocks, key_blocks, value_blocks, segments))
    mixed_rows = mixed_blocks.reshape(token_count, inner_width)
    branch_one = jnp.dot(mixed_rows, output_weight, preferred_element_type=jnp.float32)
    middle = inputs + branch_one
    scale_two = norm_scale(middle)
    normed_two = (middle * scale_two * feedforward_gain).astype(jnp.bfloat16)
    hidden = jax.nn.relu(
        jnp.dot(normed_two, inner_weight, preferred_element_type=jnp.float32)
    ).astype(jnp.bfloat16)
    branch_two = jnp.dot(hidden, outer_weight, preferred_element_type=jnp.float32)
    result = middle + branch_two
    valid_mask = (segments < ITEMS_ROW).astype(jnp.float32).reshape(token_count, 1)
    stat_terms = jnp.stack(
        [
            jnp.sum(valid_mask * result * result),
            jnp.sum(valid_mask * branch_one * branch_one),
            jnp.sum(valid_mask * branch_two * branch_two),
            jnp.sum(valid_mask),
        ]
    )
    stat_totals = lax.psum(stat_terms, ("tower", "rows"))
    member = (segments[:, None, :] == jnp.arange(ITEMS_ROW)[None, :, None]).astype(jnp.float32)
    item_sizes = jnp.sum(member, axis=2, keepdims=True)
    result_blocks = result.reshape(row_count, length, model_width)
    pooled = (
        jnp.einsum("ris,rsd->rid", member, result_blocks, precision=MATMUL_PRECISION) / item_sizes
    )
    items_here = row_count * ITEMS_ROW
    pooled = pooled.reshape(items_here, model_width)
    inverse_norm = lax.rsqrt(jnp.sum(pooled * pooled, axis=1, keepdims=True) + EPSILON)
    embedded_tokens = pooled * inverse_norm
    tower_index = lax.axis_index("tower")
    is_query = tower_index == 0
    partner = from_partner(embedded_tokens, "tower", 0)
    query_vectors = jnp.where(is_query, embedded_tokens, partner)
    document_vectors = jnp.where(is_query, partner, embedded_tokens)
    gathered_documents = lax.all_gather(document_vectors, "rows", axis=0, tiled=True)
    item_total = gathered_documents.shape[0]
    half_items = items_here // 2
    my_queries = lax.dynamic_slice_in_dim(query_vectors, tower_index * half_items, half_items, 0)
    my_targets = lax.dynamic_slice_in_dim(positives, tower_index * half_items, half_items, 0)
    similarity_scores = (
        lax.dot_general(
            my_queries,
            gathered_documents,
            (((1,), (1,)), ((), ())),
            precision=MATMUL_PRECISION,
            preferred_element_type=jnp.float32,
        )
        / SOFTMAX_TEMP
    )
    highest = jnp.max(similarity_scores, axis=1, keepdims=True)
    exp_logits = jnp.exp(similarity_scores - highest)
    exp_total = jnp.sum(exp_logits, axis=1, keepdims=True)
    log_total = highest[:, 0] + jnp.log(exp_total[:, 0])
    is_target = jnp.arange(item_total)[None, :] == my_targets[:, None]
    target = jnp.sum(jnp.where(is_target, similarity_scores, 0.0), axis=1)
    loss_part = jnp.sum(log_total - target)
    similarity_gradient = (exp_logits / exp_total - is_target.astype(jnp.float32)) * (
        LOSS_SCALE / item_total
    )
    local_gradient = (
        jnp.dot(similarity_gradient, gathered_documents, precision=MATMUL_PRECISION) / SOFTMAX_TEMP
    )
    grad_documents = lax.psum_scatter(
        lax.dot_general(
            similarity_gradient,
            my_queries,
            (((0,), (0,)), ((), ())),
            precision=MATMUL_PRECISION,
            preferred_element_type=jnp.float32,
        )
        / SOFTMAX_TEMP,
        "rows",
        scatter_dimension=0,
        tiled=True,
    )
    partner_mine, partner_documents = from_partner((local_gradient, grad_documents), "tower", 0)
    query_side = jnp.where(
        is_query,
        jnp.concatenate([local_gradient, partner_mine], 0),
        jnp.concatenate([partner_mine, local_gradient], 0),
    )
    own_grad = jnp.where(is_query, query_side, grad_documents + partner_documents)
    inner_along = jnp.sum(own_grad * embedded_tokens, axis=1, keepdims=True)
    grad_pooled = inverse_norm * (own_grad - embedded_tokens * inner_along)
    per_token = grad_pooled.reshape(row_count, ITEMS_ROW, model_width) / item_sizes
    grad_result = jnp.einsum("ris,rid->rsd", member, per_token, precision=MATMUL_PRECISION).reshape(
        token_count, model_width
    )
    grad_branch_two = grad_result.astype(jnp.bfloat16)
    outer_grad = contract_rows(hidden, grad_branch_two)
    grad_hidden = times_transpose(grad_branch_two, outer_weight)
    grad_pre = jnp.where(hidden > 0, grad_hidden, 0.0).astype(jnp.bfloat16)
    inner_grad = contract_rows(normed_two, grad_pre)
    grad_normed_two = times_transpose(grad_pre, inner_weight)
    feedforward_gain_grad = jnp.sum(grad_normed_two * middle * scale_two, axis=0)
    grad_middle = grad_result + norm_back(grad_normed_two, middle, scale_two, feedforward_gain)
    grad_branch_one = grad_middle.astype(jnp.bfloat16)
    output_grad = contract_rows(mixed_rows, grad_branch_one)
    grad_mixed = times_transpose(grad_branch_one, output_weight).astype(jnp.bfloat16)
    grad_mixed_blocks = grad_mixed.reshape(row_count, length, inner_width)

    def attend_back(running, packed):
        query_part, key_part, value_part, segment_row, row_log_total, grad_part = packed
        scores = row_scores(query_part, key_part, segment_row, position_bias, head_count)
        attention_probs = jnp.exp(scores - row_log_total[:, :, None])
        query_heads = query_part.reshape(length, head_count, head_size)
        key_heads = key_part.reshape(length, head_count, head_size)
        value_heads = value_part.reshape(length, head_count, head_size)
        grad_heads = grad_part.reshape(length, head_count, head_size)
        grad_value = jnp.einsum(
            "hqk,qhd->khd",
            attention_probs.astype(jnp.bfloat16),
            grad_heads,
            preferred_element_type=jnp.float32,
        )
        grad_probs = jnp.einsum(
            "qhd,khd->hqk", grad_heads, value_heads, preferred_element_type=jnp.float32
        )
        row_dot = jnp.sum(attention_probs * grad_probs, axis=2, keepdims=True)
        grad_scores = (attention_probs * (grad_probs - row_dot)).astype(jnp.bfloat16)
        grad_query = jnp.einsum(
            "hqk,khd->qhd", grad_scores, key_heads, preferred_element_type=jnp.float32
        )
        grad_key = jnp.einsum(
            "hqk,qhd->khd", grad_scores, query_heads, preferred_element_type=jnp.float32
        )
        outputs = (
            grad_query.reshape(length, inner_width).astype(jnp.bfloat16),
            grad_key.reshape(length, inner_width).astype(jnp.bfloat16),
            grad_value.reshape(length, inner_width).astype(jnp.bfloat16),
        )
        return (running + grad_scores.astype(jnp.float32), outputs)

    score_sum, grad_rows = lax.scan(
        attend_back,
        jnp.zeros((head_count, length, length), jnp.float32),
        (query_blocks, key_blocks, value_blocks, segments, log_totals, grad_mixed_blocks),
    )
    grad_queries = grad_rows[0].reshape(token_count, inner_width)
    grad_keys = grad_rows[1].reshape(token_count, inner_width)
    grad_values = grad_rows[2].reshape(token_count, inner_width)
    query_grad = contract_rows(normed_one, grad_queries)
    key_grad = contract_rows(normed_one, grad_keys)
    value_grad = contract_rows(normed_one, grad_values)
    grad_normed_one = (
        times_transpose(grad_queries, query_weight)
        + times_transpose(grad_keys, key_weight)
        + times_transpose(grad_values, value_weight)
    )
    attention_gain_grad = jnp.sum(grad_normed_one * inputs * scale_one, axis=0)
    token_grad = grad_middle + norm_back(grad_normed_one, inputs, scale_one, attention_gain)
    offset_onehot = jnp.asarray(
        (by_offset[:, None] == np.arange(position_table.shape[0])[None, :]).astype(np.float32)
    )
    position_grad = jnp.dot(diagonal_sums(score_sum), offset_onehot, precision=MATMUL_PRECISION).T
    closing_terms = loss_part[None]
    summed = lax.psum(
        (
            attention_gain_grad,
            query_grad,
            key_grad,
            value_grad,
            output_grad,
            position_grad,
            feedforward_gain_grad,
            inner_grad,
            outer_grad,
            closing_terms,
        ),
        ("tower", "rows"),
    )
    (
        attention_gain_grad,
        query_grad,
        key_grad,
        value_grad,
        output_grad,
        position_grad,
        feedforward_gain_grad,
        inner_grad,
        outer_grad,
        closing_totals,
    ) = summed
    contrastive_loss = closing_totals[0] / item_total
    root_mean_squares = jnp.sqrt(stat_totals[:3] / (stat_totals[3] * model_width))
    block_shape = (1, row_count, length, model_width)
    return (
        result.reshape(block_shape).astype(jnp.bfloat16),
        token_grad.reshape(block_shape).astype(jnp.bfloat16),
        attention_gain_grad,
        query_grad,
        key_grad,
        value_grad,
        output_grad,
        position_grad,
        feedforward_gain_grad,
        inner_grad,
        outer_grad,
        contrastive_loss,
        root_mean_squares,
    )


F32 = jnp.float32
BF = jnp.bfloat16
MESH = pl.DeviceIdType.MESH
NN = (((1,), (0,)), ((), ()))
NT = (((1,), (1,)), ((), ()))
TN = (((0,), (0,)), ((), ()))
WIDE = 128
UNITS = 4096 // WIDE
PER_PART = 256 // WIDE
STEPS_AFTER = (
    (),
    (0, 1, 2, 3,),
    (4, 5, 6, 7,),
    (8, 9, 10, 11, 0, 1,),
    (12, 13, 2, 3, 14, 15,),
    (),
    (0, 1, 4, 5,),
    (2, 3, 6, 7,),
    (8, 9,),
    (4, 5, 10, 11, 16, 17, 18, 19,),
    (6, 7, 12, 13, 8, 14, 15,),
    (0, 1, 2, 3, 9, 10,),
    (11, 12,),
    (13,),
    (14,),
    (20, 15, 21,),
    (0, 1, 2, 3, 4, 5, 22, 23, 24, 25,),
    (16, 17,),
    (0, 6, 1, 7, 8, 9, 10, 11, 2, 18, 13, 12, 19,),
    (3, 4, 5, 14, 15, 16, 17, 20, 21,),
    (),
    (6, 7, 22, 23, 8,),
    (9, 18, 10, 26, 27, 28,),
    (0, 1, 2, 3, 4, 11, 12, 13, 16, 17, 5, 19, 24, 25, 29, 30, 14, 31,),
    (6, 7, 15, 18, 20, 8, 21, 22, 23,),
    (0, 9, 10, 26, 27,),
    (1, 2, 4, 5, 24, 28,),
    (3, 11, 12, 13, 14, 15, 16, 17, 18, 19, 25, 29, 30, 7, 6, 20, 31, 32, 8, 21, 10, 22, 0, 26, 23, 4, 9, 5, 27, 0, 1, 16, 24, 28, 17, 2, 18, 1, 19, 11, 13, 25, 7, 15, 2, 3, 12, 6, 29, 14, 3, 31, 30, 20, 8, 32, 5, 21, 10, 16, 4, 18, 17, 5, 22, 4, 26, 7, 6, 23, 9, 20, 7, 32, 6, 27, 8, 24, 22, 21, 19, 28, 8, 11, 13, 10, 9, 23, 25, 15, 10, 24, 9, 12, 20, 21, 29, 14, 20, 22, 19, 21, 31, 11, 25, 30, 22, 16, 11, 18, 13, 24, 17, 13, 23, 24, 32, 26, 12, 23, 15, 27, 12, 14, 28, 29, 15, 19, 25, 14, 16, 32, 31, 25, 17, 30, 16, 18, 26, 27, 17, 28, 18, 29, 31, 19, 30, 19, 26, 27, 26, 28, 27, 29, 28, 30, 29, 31, 30, 31,),
)
SMALL = UNITS
PIECES = len(STEPS_AFTER)
FAR = 512
NEAR = 384
WINDOWS = ((0, 256, 128), (0, 384, 0), (128, 384, 0), (256, 256, 0))


def dot(a, b, dims=NN):
    return lax.dot_general(a, b, dims, preferred_element_type=F32)


def exact_dot(a, b, dims=NN):
    return lax.dot_general(
        a, b, dims, precision=lax.Precision.HIGHEST, preferred_element_type=F32
    )


def tile(index, size):
    if isinstance(index, int):
        return pl.ds(index * size, size)
    return pl.ds(pl.multiple_of(index * size, size), size)


def far_limits(bucket_count, far_limit):
    half_count = bucket_count // 2
    exact_count = half_count // 2
    limits = []
    reached = exact_count
    for distance in range(exact_count, 512):
        within = exact_count + int(
            math.log(distance / exact_count)
            / math.log(far_limit / exact_count)
            * (half_count - exact_count)
        )
        within = min(within, half_count - 1)
        while reached < within:
            limits.append(distance)
            reached += 1
    return limits


def bucket_onehot(offset):
    distance = jnp.abs(offset)
    far = jnp.full_like(distance, 8)
    for limit in far_limits(32, MAX_DIST):
        far = far + jnp.where(distance >= limit, 1, 0)
    bucket = jnp.where(distance < 8, distance, far) + jnp.where(offset > 0, 16, 0)
    same = bucket == lax.broadcasted_iota(jnp.int32, (32, FAR), 0)
    return jnp.where(same, 1.0, 0.0).astype(F32)


def split_three(value):
    high = value.astype(BF)
    rest = value - high.astype(F32)
    middle = rest.astype(BF)
    return high, middle, (rest - middle.astype(F32)).astype(BF)


class Place:
    def __init__(self):
        self.tower = lax.axis_index("tower")
        self.rows = lax.axis_index("rows")
        self.flat = lax.rem(self.rows, 4)
        self.deep = lax.div(self.rows, 4)
        bits = {
            "x": lax.rem(self.rows, 2),
            "y": lax.rem(lax.div(self.rows, 2), 2),
            "z": lax.rem(lax.div(self.rows, 4), 2),
            "w": lax.div(self.rows, 8),
        }
        steps = {"x": 1, "y": 2, "z": 4, "w": 8}
        self.bit = {"c": self.tower, **bits}
        self.to = {"c": self.device(1 - self.tower, self.rows)}
        for name, step in steps.items():
            self.to[name] = self.device(self.tower, self.rows + step * (1 - 2 * bits[name]))

    def device(self, tower, rows):
        return {"tower": tower, "rows": rows}

    def along_deep(self, step):
        return self.device(self.tower, lax.rem(self.deep + step, 4) * 4 + self.flat)

    def along_flat(self, step):
        return self.device(self.tower, self.deep * 4 + lax.rem(self.flat + step, 4))


def order_of(unit):
    return (("cxzyw", "cyzxw") if 8 * unit < 5 * UNITS else ("cxyZ", "cyxZ"))[unit % 2]


class Sums:
    def __init__(self, place, total, landed, out, small, small_landed, sems):
        self.place, self.total, self.landed, self.out = place, total, landed, out
        self.small, self.small_landed = small, small_landed
        self.send_sem, self.recv_sem, self.out_sem, self.small_send, self.small_recv = sems
        self.plans = {}
        self.stage = {}
        for unit in range(UNITS):
            order = order_of(unit)
            if order not in self.plans:
                self.plans[order] = self.plan(order)

    def plan(self, order):
        place, steps = self.place, []
        base, size, offset, sem = 0, 512, 0, 0
        for name in order:
            ways = 4 if name == "Z" else 2
            size //= ways
            spot = place.deep if name == "Z" else place.bit[name]
            partners = []
            for i in range(1, ways):
                if name == "Z":
                    piece, device = lax.rem(place.deep + i, 4), place.along_deep(i)
                else:
                    piece, device = 1 - spot, place.to[name]
                partners.append((base + piece * size, device, offset, sem))
                offset, sem = offset + size, sem + 1
            base = base + spot * size
            steps.append((size, base, partners))
        return steps

    def remote(self, source, target, index, unit, device):
        return pltpu.make_async_remote_copy(
            src_ref=source,
            dst_ref=target,
            send_sem=self.send_sem.at[index, unit],
            recv_sem=self.recv_sem.at[index, unit],
            device_id=device,
            device_id_type=MESH,
        )

    def depth(self, unit):
        return 5 if unit == SMALL else 2 * len(order_of(unit))

    def rows(self, start, size):
        return pl.ds(pl.multiple_of(start, size), size)

    def keep(self, unit):
        size, base, _ = self.plans[order_of(unit)][-1]
        rows = self.rows(base, size)
        return pltpu.make_async_copy(
            self.total.at[unit, rows], self.out.at[unit, rows], self.out_sem.at[unit]
        )

    def copies(self, stage, unit):
        if unit == SMALL:
            return [
                pltpu.make_async_remote_copy(
                    src_ref=self.small,
                    dst_ref=self.small_landed.at[stage],
                    send_sem=self.small_send.at[stage],
                    recv_sem=self.small_recv.at[stage],
                    device_id=self.place.to["cxyzw"[stage]],
                    device_id_type=MESH,
                )
            ]
        plan = self.plans[order_of(unit)]
        if stage < len(plan):
            size, _, partners = plan[stage]
            return [
                self.remote(
                    self.total.at[unit, self.rows(start, size)],
                    self.landed.at[unit, pl.ds(offset, size)],
                    sem,
                    unit,
                    device,
                )
                for start, device, offset, sem in partners
            ]
        back = 2 * len(plan) - 1 - stage
        size, base, partners = plan[back]
        rows = self.rows(base, size)
        source = self.total if stage == len(plan) else self.out
        return [
            self.remote(source.at[unit, rows], self.out.at[unit, rows], 6 + sem, unit, device)
            for _, device, _, sem in partners
        ]

    def step(self, unit):
        stage = self.stage.get(unit, -1)
        plan = None if unit == SMALL else self.plans[order_of(unit)]
        if stage >= 0:
            for copy in self.copies(stage, unit):
                copy.wait()
            if unit == SMALL:
                self.small[...] += self.small_landed[stage]
            elif stage < len(plan):
                size, base, partners = plan[stage]
                parts = [self.landed[unit, pl.ds(p[2], size), :] for p in partners]
                self.total[unit, self.rows(base, size), :] += sum(parts[1:], parts[0])
            elif stage == len(plan):
                self.keep(unit).wait()
        stage += 1
        self.stage[unit] = stage
        if stage < self.depth(unit):
            for copy in self.copies(stage, unit):
                copy.start()
            if plan is not None and stage == len(plan):
                self.keep(unit).start()

    def fill(self, part, value):
        for i in range(PER_PART):
            self.total[part * PER_PART + i] = value[:, i * WIDE : (i + 1) * WIDE]

    def after(self, piece, *parts):
        for part in parts:
            for i in range(PER_PART):
                self.step(part * PER_PART + i)
        if piece == PIECES - 1:
            self.step(SMALL)
        for unit in STEPS_AFTER[piece]:
            self.step(unit)


class Spread:
    def __init__(self, place, blocks, send_sem, recv_sem):
        self.place, self.blocks = place, blocks
        self.send_sem, self.recv_sem = send_sem, recv_sem

    def copy(self, row, index, where, device):
        ref = self.blocks.at[where]
        return pltpu.make_async_remote_copy(
            src_ref=ref,
            dst_ref=ref,
            send_sem=self.send_sem.at[row, index],
            recv_sem=self.recv_sem.at[row, index],
            device_id=device,
            device_id_type=MESH,
        )

    def one(self, row, i):
        place = self.place
        where = (row, place.tower, place.deep, place.flat)
        return self.copy(row, i, where, place.along_deep(i + 1))

    def copies(self, row, stage):
        place = self.place
        if stage == 0:
            return [self.one(row, i) for i in range(3)]
        if stage == 1:
            where = (row, place.tower, slice(None), place.flat)
            return [self.copy(row, 3 + i, where, place.along_flat(i + 1)) for i in range(3)]
        return [self.copy(row, 6, (row, place.tower), place.to["c"])]

    def start(self, row, stage):
        for copy in self.copies(row, stage):
            copy.start()

    def wait(self, row, stage):
        for copy in self.copies(row, stage):
            copy.wait()


def layer_kernel(
    tokens_hbm,
    segment_ref,
    positive_ref,
    gain_one_ref,
    query_hbm,
    key_hbm,
    value_hbm,
    output_hbm,
    table_ref,
    gain_two_ref,
    inner_hbm,
    outer_hbm,
    layer_hbm,
    token_grad_hbm,
    sums_hbm,
    hidden_sum_hbm,
    rows_grad_hbm,
    small_ref,
    tokens,
    query_w,
    key_w,
    value_w,
    output_w,
    inner_w,
    outer_w,
    normed_one,
    queries,
    keys,
    values,
    probs,
    side_probs,
    mixed,
    middle,
    normed_two,
    hidden,
    bias,
    segment_column,
    segment_row,
    pooled_all,
    hidden_sum,
    normed_one_t,
    normed_two_t,
    mixed_t,
    grad_mixed,
    grad_query,
    grad_key,
    grad_value,
    key_total,
    value_total,
    total,
    landed,
    expand,
    rounded_grads,
    small_landed,
    load_sem,
    store_sem,
    sum_send,
    sum_recv,
    sum_out,
    pool_send,
    pool_recv,
    hidden_send,
    hidden_recv,
    small_send,
    small_recv,
    relay_send,
    relay_recv,
):
    place = Place()
    barrier = pltpu.get_barrier_semaphore()
    partners = [place.to["c"]]
    partners += [place.along_deep(i) for i in (1, 2, 3)]
    partners += [place.along_flat(i) for i in (1, 2, 3)]
    for partner in partners:
        pl.semaphore_signal(barrier, inc=1, device_id=partner, device_id_type=MESH)

    loads = [
        pltpu.make_async_copy(source, target, load_sem.at[i])
        for i, (source, target) in enumerate(
            (
                (tokens_hbm, tokens),
                (query_hbm, query_w),
                (key_hbm, key_w),
                (value_hbm, value_w),
                (output_hbm, output_w),
                (inner_hbm, inner_w),
                (outer_hbm, outer_w),
            )
        )
    ]
    for load in loads:
        load.start()

    segment_row[...] = segment_ref[...].astype(F32)
    for i in range(8):
        row = segment_row[i // 4 : i // 4 + 1, (i % 4) * 128 : (i % 4) * 128 + 128]
        segment_column[i * 128 : (i + 1) * 128, :] = jnp.broadcast_to(row, (128, 128)).T
    place_row = lax.broadcasted_iota(jnp.int32, (32, FAR), 1)
    offsets = jnp.where(place_row >= NEAR, place_row - FAR, place_row) - 128
    by_place = exact_dot(table_ref[...], bucket_onehot(offsets))
    for h in range(8):
        spread = jnp.broadcast_to(by_place[h : h + 1], (128, FAR))
        bias[h] = pltpu.roll(spread, 0, 1, stride=1, stride_axis=0)[:, :NEAR]
    pooling = Spread(place, pooled_all, pool_send, pool_recv)
    sums = Sums(
        place,
        total,
        landed,
        sums_hbm,
        small_ref,
        small_landed,
        (sum_send, sum_recv, sum_out, small_send, small_recv),
    )

    def hidden_slot(row):
        return hidden_sum_hbm.at[row, place.tower, place.deep, place.bit["y"], place.bit["x"]]

    def save_hidden(row):
        return pltpu.make_async_copy(hidden_sum.at[row], hidden_slot(row), store_sem.at[row])

    def hidden_copy(source, target, row, index, device):
        return pltpu.make_async_remote_copy(
            src_ref=source,
            dst_ref=target,
            send_sem=hidden_send.at[row, index],
            recv_sem=hidden_recv.at[row, index],
            device_id=device,
            device_id_type=MESH,
        )

    def go(copies, start):
        for copy in copies:
            if start:
                copy.start()
            else:
                copy.wait()

    def deepen_hidden(row, start):
        source = hidden_sum.at[row]
        target = hidden_slot(row)
        copies = [
            hidden_copy(source, target, row, i - 1, place.along_deep(i)) for i in (1, 2, 3)
        ]
        go(copies, start)

    def widen_hidden(row, step, start):
        ref = hidden_sum_hbm.at[row, place.tower]
        y, x = place.bit["y"], place.bit["x"]
        left, right = pl.ds(0, 1024), pl.ds(1024, 1024)
        if step == 0:
            parts = (ref.at[:, y, x, :, left], "x"), (ref.at[:, y, x, :, right], "y")
        else:
            parts = (ref.at[:, y, :, :, left], "y"), (ref.at[:, :, x, :, right], "x")
        copies = [
            hidden_copy(part, part, row, 3 + 2 * step + i, place.to[name])
            for i, (part, name) in enumerate(parts)
        ]
        go(copies, start)

    def swap_hidden(row, start):
        ref = hidden_sum_hbm.at[row, place.tower]
        go([hidden_copy(ref, ref, row, 7, place.to["c"])], start)

    def relay(step, start):
        ref = pooled_all.at[1, place.tower, lax.rem(place.deep + 4 - step, 4), place.flat]
        copies = [
            pltpu.make_async_remote_copy(
                src_ref=ref,
                dst_ref=ref,
                send_sem=relay_send.at[step, i - 1],
                recv_sem=relay_recv.at[step, i - 1],
                device_id=place.along_flat(i),
                device_id_type=MESH,
            )
            for i in (1, 2, 3)
        ]
        go(copies, start)

    head_lane = lax.broadcasted_iota(jnp.int32, (1, 256), 1) // 64
    head_mask = [jnp.where(head_lane == h, 1.0, 0.0) for h in range(4)]
    head_mask_low = [mask.astype(BF) for mask in head_mask]

    def stack_heads(part):
        return jnp.concatenate([part * mask for mask in head_mask_low], 0)

    def pick_heads(part):
        return sum(part[h * 128 : (h + 1) * 128] * head_mask[h] for h in range(4))

    def project(i, carry):
        rows = tile(i, 256)
        x = tokens[rows, :].astype(F32)
        scale = lax.rsqrt(jnp.mean(x * x, axis=1, keepdims=True) + EPSILON)
        normed = (x * scale * gain_one_ref[...]).astype(BF)
        normed_one[rows, :] = normed
        queries[rows, :] = dot(normed, query_w[...]).astype(BF)
        keys[rows, :] = dot(normed, key_w[...]).astype(BF)
        values[rows, :] = dot(normed, value_w[...]).astype(BF)
        return carry

    def window(r, b):
        start, width, offset = WINDOWS[b]
        base = r * 512
        own = pl.ds(pl.multiple_of(base + b * 128, 128), 128)
        near = pl.ds(pl.multiple_of(base + start, 128), width)
        return own, near, slice(start, start + width), slice(offset, offset + width)

    def soft(r, b, g):
        if b in (0, 3):
            return side_probs.at[r, b // 3, g]
        return probs.at[r, b - 1, g]

    def attend(b, r, carry):
        own, near, near_row, offset = window(r, b)
        column = segment_column[own, :]
        row = segment_row[pl.ds(r, 1), near_row]
        same = jnp.concatenate([column] * (WINDOWS[b][1] // 128), 1) == row
        for g in range(2):
            lanes = slice(g * 256, (g + 1) * 256)
            scores = dot(stack_heads(queries[own, lanes]), keys[near, lanes], NT)
            parts = []
            for h in range(4):
                part = scores[h * 128 : (h + 1) * 128] + bias[g * 4 + h, :, offset]
                part = jnp.where(same, part, -1e30)
                highest = jnp.max(part, axis=1, keepdims=True)
                exp_part = jnp.exp(part - highest)
                exp_total = jnp.sum(exp_part, axis=1, keepdims=True)
                parts.append((exp_part * (1.0 / exp_total)).astype(BF))
            stacked = jnp.concatenate(parts, 0)
            soft(r, b, g)[...] = stacked
            mixed[own, lanes] = pick_heads(dot(stacked, values[near, lanes])).astype(BF)
        return carry

    def feed(i, carry):
        rows = tile(i, 256)
        branch = dot(mixed[rows, :], output_w[...])
        mid = tokens[rows, :].astype(F32) + branch
        middle[rows, :] = mid
        scale = lax.rsqrt(jnp.mean(mid * mid, axis=1, keepdims=True) + EPSILON)
        normed = (mid * scale * gain_two_ref[...]).astype(BF)
        normed_two[rows, :] = normed
        for c in range(4):
            lanes = slice(c * 512, (c + 1) * 512)
            hidden[rows, lanes] = jnp.maximum(dot(normed, inner_w[:, lanes]), 0.0).astype(BF)
        valid = jnp.where(segment_column[rows, 0:1] < ITEMS_ROW, 1.0, 0.0)
        small_ref[3:4, :] += jnp.sum(valid * branch * branch, axis=0, keepdims=True)
        small_ref[5:6, :] += jnp.sum(valid * jnp.ones_like(branch), axis=0, keepdims=True)
        return carry

    def pool(r):
        rows = tile(r, 512)
        number = lax.broadcasted_iota(jnp.int32, (8, 512), 0).astype(F32)
        member = jnp.where(segment_row[pl.ds(r, 1), :] == number, 1.0, 0.0)
        member_low = jnp.concatenate([member, jnp.zeros_like(member)], 0).astype(BF)
        count = jnp.sum(member, axis=1, keepdims=True)
        hidden_part = dot(member_low, hidden[rows, :])[:8]
        hidden_sum[r] = hidden_part
        middle_part = exact_dot(member, middle[rows, :])
        pieces = split_three(hidden_part)
        stacked = jnp.concatenate([*pieces, jnp.zeros_like(pieces[0])], 0)
        branch = dot(stacked, outer_w[...])
        pooled = (middle_part + (branch[0:8] + branch[8:16] + branch[16:24])) / count
        sublane = lax.broadcasted_iota(jnp.int32, (8, 128), 0)
        ids = jnp.zeros((8, 128), F32)
        for s in range(8):
            ids = jnp.where(sublane == s, positive_ref[r * 8 + s].astype(F32), ids)
        lanes = lax.broadcasted_iota(jnp.int32, (8, 128), 1)
        extra = jnp.where(lanes == 0, ids, count)
        pooled_all[r, place.tower, place.deep, place.flat] = jnp.concatenate([pooled, extra], 1)

    small_ref[...] = jnp.zeros_like(small_ref)
    for i in range(4):
        loads[i].wait()
    pl.semaphore_wait(barrier, len(partners))

    def forward(r, carry):
        first, second = r == 0, r == 1
        lax.fori_loop(2 * r, 2 * r + 2, project, 0)
        attend(0, r, 0)
        attend(1, r, 0)

        attend(2, r, 0)
        attend(3, r, 0)

        @pl.when(first)
        def _():
            for i in (4, 5):
                loads[i].wait()

        @pl.when(second)
        def _():
            pooling.wait(0, 0)
            pooling.start(0, 1)

        lax.fori_loop(2 * r, 2 * r + 2, feed, 0)

        @pl.when(first)
        def _():
            loads[6].wait()

        pool(r)
        pooling.start(r, 0)

        @pl.when(second)
        def _():
            relay(0, start=True)
            save_hidden(0).wait()
            deepen_hidden(0, start=False)
            widen_hidden(0, 0, start=True)

        deepen_hidden(r, start=True)
        save_hidden(r).start()
        return carry

    lax.fori_loop(0, 2, forward, 0)

    def store_rows(source, target, i, index):
        rows = tile(i, 256)
        return pltpu.make_async_copy(source.at[rows], target.at[rows], store_sem.at[index])

    def close(i, carry):
        rows = tile(i, 256)
        branch = dot(hidden[rows, :], outer_w[...])
        result = middle[rows, :] + branch
        grad_query[rows, :] = result.astype(BF)
        valid = jnp.where(segment_column[rows, 0:1] < ITEMS_ROW, 1.0, 0.0)
        small_ref[2:3, :] += jnp.sum(valid * result * result, axis=0, keepdims=True)
        small_ref[4:5, :] += jnp.sum(valid * branch * branch, axis=0, keepdims=True)
        return carry

    def turn(i, carry):
        rows = tile(i, 128)
        normed_two_t[:, rows] = normed_two[rows, :].T
        mixed_t[:, rows] = mixed[rows, :].T
        normed_one_t[:, rows] = normed_one[rows, :].T
        return carry

    lax.fori_loop(0, 3, close, 0)
    for step in (1, 2, 3):
        if step == 3:
            lax.fori_loop(3, 4, close, 0)
        pooling.one(1, step - 1).wait()
        relay(step, start=True)
    pooling.wait(0, 1)
    pooling.start(0, 2)
    for i in range(4):
        store_rows(grad_query, layer_hbm, i, 2 + i).start()
    save_hidden(1).wait()
    lax.fori_loop(0, 8, turn, 0)
    widen_hidden(0, 0, start=False)
    widen_hidden(0, 1, start=True)
    lane = lax.broadcasted_iota(jnp.int32, (1, 128), 1)
    item = segment_column[...] + jnp.where(
        lax.broadcasted_iota(jnp.int32, (1024, 128), 0) >= 512, 8.0, 0.0
    )
    item = jnp.where(segment_column[...] < ITEMS_ROW, item, -1.0)
    slot = jnp.where(lane < 48, lax.rem(lane, 16), -2).astype(F32)
    expand[...] = jnp.where(item == slot, 1.0, 0.0).astype(BF)
    for step in range(4):
        relay(step, start=False)
    pooling.start(1, 2)
    deepen_hidden(1, start=False)
    widen_hidden(1, 0, start=True)
    pooling.wait(0, 2)
    pooling.wait(1, 2)

    gathered = [
        jnp.concatenate([pooled_all[r, t].reshape(128, 640) for r in range(2)], 0)
        for t in range(2)
    ]
    vectors, inverse, counts, embedded = [], [], [], []
    for t in range(2):
        vector = gathered[t][:, :512]
        scale = lax.rsqrt(jnp.sum(vector * vector, axis=1, keepdims=True) + EPSILON)
        vectors.append(vector)
        inverse.append(scale)
        embedded.append(vector * scale)
        counts.append(gathered[t][:, 513:514])
    logits = exact_dot(embedded[0], embedded[1], NT) / SOFTMAX_TEMP
    highest = jnp.max(logits, axis=1, keepdims=True)
    exp_logits = jnp.exp(logits - highest)
    exp_total = jnp.sum(exp_logits, axis=1, keepdims=True)
    position = lax.broadcasted_iota(jnp.int32, (256, 256), 1)
    number = lax.rem(lax.div(position, 8), 16) * 16 + lax.div(position, 128) * 8
    number = (number + lax.rem(position, 8)).astype(F32)
    is_target = gathered[0][:, 512:513] == number
    target = jnp.sum(jnp.where(is_target, logits, 0.0), axis=1, keepdims=True)
    losses = highest + jnp.log(exp_total) - target
    loss = jnp.sum(losses, axis=0, keepdims=True) / 256
    grad_logits = (exp_logits / exp_total - jnp.where(is_target, 1.0, 0.0)) * (LOSS_SCALE / 256)
    grads = (
        exact_dot(grad_logits, embedded[1]) / SOFTMAX_TEMP,
        exact_dot(grad_logits, embedded[0], TN) / SOFTMAX_TEMP,
    )
    for t in range(2):
        along = jnp.sum(grads[t] * embedded[t], axis=1, keepdims=True)
        per_token = inverse[t] * (grads[t] - embedded[t] * along) / counts[t]
        for r in range(2):
            part = per_token[r * 128 : (r + 1) * 128]
            for i in range(512 // WIDE):
                total[UNITS - 4 + 2 * r + t, i * 128 : (i + 1) * 128] = part[
                    :, i * WIDE : (i + 1) * WIDE
                ]
            rounded_grads[r, t] = per_token[r * 128 : (r + 1) * 128].astype(BF)
    save_grads = pltpu.make_async_copy(rounded_grads, rows_grad_hbm, store_sem.at[6])
    save_grads.start()
    own_parts = []
    for r in range(2):
        spot = UNITS - 4 + 2 * r + place.tower
        lanes = [total[spot, tile(place.rows + 16 * i, 8)] for i in range(512 // WIDE)]
        own_parts.append(jnp.concatenate(lanes, 1))
    own = jnp.concatenate(own_parts, 0)
    pieces = split_three(own)
    own_low = pieces[0]
    own_split = jnp.concatenate([*pieces, jnp.zeros((80, 512), BF)], 0)

    def back_hidden(c):
        lanes = slice(c * 512, (c + 1) * 512)
        row_part = dot(own_low, outer_w[lanes, :], NT).astype(BF)
        row_part = jnp.concatenate([row_part, jnp.zeros((112, 512), BF)], 0)

        def mask(i, carry):
            rows = tile(i, 256)
            spread = dot(expand[rows, :], row_part)
            hidden[rows, lanes] = jnp.where(hidden[rows, lanes] > 0, spread, 0.0).astype(BF)
            return carry

        lax.fori_loop(0, 4, mask, 0)
        for half in range(2):
            part = 2 * c + half
            columns = slice(part * 256, (part + 1) * 256)
            sums.fill(part, dot(normed_two_t[...], hidden[:, columns]))
        sums.after(c, 2 * c, 2 * c + 1)

    def back_middle(i, carry):
        rows = tile(i, 256)
        grad_normed = dot(hidden[rows, :], inner_w[...], NT)
        mid = middle[rows, :]
        scale = lax.rsqrt(jnp.mean(mid * mid, axis=1, keepdims=True) + EPSILON)
        small_ref[1:2, :] += jnp.sum(grad_normed * mid * scale, axis=0, keepdims=True)
        gained = grad_normed * gain_two_ref[...]
        mean = jnp.mean(gained * mid, axis=1, keepdims=True)
        grad_mid = dot(expand[rows, :], own_split) + scale * (gained - mid * scale * scale * mean)
        middle[rows, :] = grad_mid
        rounded = grad_mid.astype(BF)
        mixed[rows, :] = rounded
        grad_mixed[rows, :] = dot(rounded, output_w[...], NT).astype(BF)
        return carry

    for c in range(4):
        back_hidden(c)
    for i in range(2):
        lax.fori_loop(2 * i, 2 * i + 2, back_middle, 0)
        sums.after(4 + 2 * i)
        sums.after(5 + 2 * i)
    for half in range(2):
        sums.fill(8 + half, dot(mixed_t[...], mixed[:, half * 256 : (half + 1) * 256]))
    widen_hidden(1, 0, start=False)
    widen_hidden(1, 1, start=True)
    sums.after(8, 8, 9)

    for i in range(4):
        store_rows(grad_query, layer_hbm, i, 2 + i).wait()
    bias[...] = jnp.zeros_like(bias)

    def attend_back(g, b, r, carry):
        own, near, _, offset = window(r, b)
        lanes = slice(g * 256, (g + 1) * 256)
        grad_stack = stack_heads(grad_mixed[own, lanes])
        grad_soft = dot(grad_stack, values[near, lanes], NT)
        weight = soft(r, b, g)[...]
        parts = []
        for h in range(4):
            rows = slice(h * 128, (h + 1) * 128)
            soft_part = weight[rows].astype(F32)
            grad_part = grad_soft[rows]
            along = jnp.sum(soft_part * grad_part, axis=1, keepdims=True)
            part = (soft_part * (grad_part - along)).astype(BF)
            bias[g * 4 + h, :, offset] += part.astype(F32)
            parts.append(part)
        stacked = jnp.concatenate(parts, 0)
        grad_query[own, lanes] = pick_heads(dot(stacked, keys[near, lanes])).astype(BF)
        key_total[near, :] += dot(stacked, stack_heads(queries[own, lanes]), TN)
        value_total[near, :] += dot(weight, grad_stack, TN)
        return carry

    for g in range(2):
        lanes = slice(g * 256, (g + 1) * 256)
        key_total[...] = jnp.zeros_like(key_total)
        value_total[...] = jnp.zeros_like(value_total)
        for b in range(4):
            lax.fori_loop(0, 2, functools.partial(attend_back, g, b), 0)
            sums.after(9 + 7 * g + b)
        part, piece = 10 + 3 * g, 13 + 7 * g
        sums.fill(part, dot(normed_one_t[...], grad_query[:, lanes]))
        sums.after(piece, part)
        grad_key[:, lanes] = key_total[...].astype(BF)
        sums.fill(part + 1, dot(normed_one_t[...], grad_key[:, lanes]))
        sums.after(piece + 1, part + 1)
        grad_value[:, lanes] = value_total[...].astype(BF)
        sums.fill(part + 2, dot(normed_one_t[...], grad_value[:, lanes]))
        sums.after(piece + 2, part + 2)
        if g == 0:
            widen_hidden(0, 1, start=False)
            swap_hidden(0, start=True)
    widen_hidden(1, 1, start=False)
    swap_hidden(0, start=False)
    swap_hidden(1, start=True)

    def back_tokens(i, carry):
        rows = tile(i, 256)
        grad_normed = (
            dot(grad_query[rows, :], query_w[...], NT)
            + dot(grad_key[rows, :], key_w[...], NT)
            + dot(grad_value[rows, :], value_w[...], NT)
        )
        x = tokens[rows, :].astype(F32)
        scale = lax.rsqrt(jnp.mean(x * x, axis=1, keepdims=True) + EPSILON)
        small_ref[0:1, :] += jnp.sum(grad_normed * x * scale, axis=0, keepdims=True)
        gained = grad_normed * gain_one_ref[...]
        mean = jnp.mean(gained * x, axis=1, keepdims=True)
        grad = middle[rows, :] + scale * (gained - x * scale * scale * mean)
        normed_one[rows, :] = grad.astype(BF)
        return carry

    for i in range(2):
        lax.fori_loop(2 * i, 2 * i + 2, back_tokens, 0)
        for j in (2 * i, 2 * i + 1):
            store_rows(normed_one, token_grad_hbm, j, 2 + j).start()
            sums.after(23 + j)
    mirror = (
        lax.broadcasted_iota(jnp.int32, (128, 128), 0)
        + lax.broadcasted_iota(jnp.int32, (128, 128), 1)
    )
    mirror = jnp.where(mirror == 127, 1.0, 0.0)
    diagonals = []
    for h in range(8):
        turned = exact_dot(mirror, bias[h])
        wide = jnp.concatenate([turned, jnp.zeros((128, FAR - NEAR), F32)], 1)
        wide = pltpu.roll(wide, 0, 1, stride=1, stride_axis=0)
        diagonals.append(jnp.sum(wide, axis=0, keepdims=True))
    buckets = exact_dot(jnp.concatenate(diagonals, 0), bucket_onehot(place_row - 255), NT)
    small_ref[8:16, :] = jnp.concatenate([buckets, jnp.zeros((8, 480), F32)], 1)
    sums.after(27)
    small_ref[6:7, :] = jnp.broadcast_to(loss, (1, 512))
    swap_hidden(1, start=False)
    save_grads.wait()
    for i in range(4):
        store_rows(normed_one, token_grad_hbm, i, 2 + i).wait()


def closing_kernel(
    layer_hbm,
    token_grad_hbm,
    sums_hbm,
    hidden_sum_hbm,
    rows_grad_hbm,
    small_ref,
    layer_out,
    token_out,
    gain_one_out,
    query_out,
    key_out,
    value_out,
    output_out,
    position_out,
    gain_two_out,
    inner_out,
    outer_out,
    loss_out,
    square_out,
    hidden_sum,
    rows_grad,
    hidden_low,
    outer_part,
    rows_part,
    units_part,
    load_sem,
    copy_sem,
    store_sem,
):
    pairs = []
    inner_units = 2048 // WIDE
    for unit in range(inner_units):
        pairs.append((units_part.at[unit], inner_out.at[:, pl.ds(unit * WIDE, WIDE)]))
    places = [(output_out, 0), (output_out, 256)]
    places += [(ref, g * 256) for g in range(2) for ref in (query_out, key_out, value_out)]
    for part, (ref, lane) in enumerate(places):
        for i in range(PER_PART):
            lanes = pl.ds(lane + i * WIDE, WIDE)
            pairs.append((units_part.at[inner_units + part * PER_PART + i], ref.at[:, lanes]))
    pairs += [(rows_part.at[0], layer_out), (rows_part.at[1], token_out)]
    copies = [
        pltpu.make_async_copy(source, target, copy_sem.at[i])
        for i, (source, target) in enumerate(pairs)
    ]
    pairs = [(rows_grad_hbm, rows_grad), (hidden_sum_hbm, hidden_sum)]
    pairs += [(sums_hbm.at[unit], units_part.at[unit]) for unit in range(UNITS)]
    pairs += [(layer_hbm, rows_part.at[0]), (token_grad_hbm, rows_part.at[1])]
    loads = [
        pltpu.make_async_copy(source, target, load_sem.at[i])
        for i, (source, target) in enumerate(pairs)
    ]
    for load in loads:
        load.start()
    gain_one_out[...] = small_ref[0, :]
    gain_two_out[...] = small_ref[1, :]
    position_out[...] = small_ref[8:16, 0:32]
    loss_out[0] = jnp.max(small_ref[6:7, :])
    squares = jnp.sum(small_ref[2:5, :], axis=1, keepdims=True)
    valid = jnp.sum(small_ref[5:6, :], axis=1, keepdims=True)
    roots = jnp.sqrt(squares / valid)
    for i in range(3):
        square_out[i] = jnp.max(roots[i : i + 1, :])
    loads[0].wait()
    loads[1].wait()
    hidden_low[...] = hidden_sum[...].reshape(512, 2048).astype(BF)
    grads = rows_grad[...].reshape(512, 512)
    stores = []
    for c in range(4):
        rows = pl.ds(c * 512, 512)
        outer_part[rows] = dot(hidden_low[:, c * 512 : (c + 1) * 512], grads, TN)
        store = pltpu.make_async_copy(outer_part.at[rows], outer_out.at[rows], store_sem.at[c])
        store.start()
        stores.append(store)
        for i in range(UNITS // 4 * c, UNITS // 4 * (c + 1)):
            loads[2 + i].wait()
            copies[i].start()
    for i in (UNITS, UNITS + 1):
        loads[2 + i].wait()
        copies[i].start()
    for copy in copies + stores:
        copy.wait()


def fast_shards(
    tokens,
    segment_ids,
    positives,
    attention_gain,
    query_weight,
    key_weight,
    value_weight,
    output_weight,
    position_table,
    feedforward_gain,
    inner_weight,
    outer_weight,
):
    block_shape = tokens.shape
    anywhere = pl.BlockSpec(memory_space=pl.ANY)
    vmem = pl.BlockSpec(memory_space=pltpu.VMEM)
    smem = pl.BlockSpec(memory_space=pltpu.SMEM)
    shape = jax.ShapeDtypeStruct
    dma = pltpu.SemaphoreType.DMA
    low = functools.partial(pltpu.VMEM, dtype=BF)
    full = functools.partial(pltpu.VMEM, dtype=F32)
    outs = pl.pallas_call(
        layer_kernel,
        out_shape=[
            shape((1024, 512), BF),
            shape((1024, 512), BF),
            shape((UNITS, 512, WIDE), F32),
            shape((2, 2, 4, 2, 2, 8, 2048), F32),
            shape((2, 2, 128, 512), BF),
            shape((16, 512), F32),
        ],
        in_specs=[anywhere, vmem, smem, vmem]
        + [anywhere] * 4
        + [vmem, vmem, anywhere, anywhere],
        out_specs=[anywhere] * 5 + [vmem],
        scratch_shapes=[
            low((1024, 512)),
            low((512, 512)),
            low((512, 512)),
            low((512, 512)),
            low((512, 512)),
            low((512, 2048)),
            low((2048, 512)),
            low((1024, 512)),
            low((1024, 512)),
            low((1024, 512)),
            low((1024, 512)),
            low((2, 2, 2, 512, 384)),
            low((2, 2, 2, 512, 256)),
            low((1024, 512)),
            full((1024, 512)),
            low((1024, 512)),
            low((1024, 2048)),
            full((8, 128, NEAR)),
            full((1024, 128)),
            full((2, 512)),
            full((2, 2, 4, 4, 8, 640)),
            full((2, 8, 2048)),
            low((512, 1024)),
            low((512, 1024)),
            low((512, 1024)),
            low((1024, 512)),
            low((1024, 512)),
            low((1024, 512)),
            low((1024, 512)),
            full((1024, 256)),
            full((1024, 256)),
            full((UNITS, 512, WIDE)),
            full((UNITS, 496, WIDE)),
            low((1024, 128)),
            low((2, 2, 128, 512)),
            full((5, 16, 512)),
            dma((7,)),
            dma((7,)),
            dma((12, UNITS)),
            dma((12, UNITS)),
            dma((UNITS,)),
            dma((2, 7)),
            dma((2, 7)),
            dma((2, 8)),
            dma((2, 8)),
            dma((5,)),
            dma((5,)),
            dma((4, 3)),
            dma((4, 3)),
        ],
        compiler_params=pltpu.CompilerParams(
            collective_id=0, has_side_effects=True, vmem_limit_bytes=63 * 2**20
        ),
    )(
        tokens.reshape(1024, 512),
        segment_ids.reshape(2, 512),
        positives,
        attention_gain.reshape(1, 512),
        query_weight,
        key_weight,
        value_weight,
        output_weight,
        position_table.T,
        feedforward_gain.reshape(1, 512),
        inner_weight,
        outer_weight,
    )
    results = pl.pallas_call(
        closing_kernel,
        out_shape=[
            shape((1024, 512), BF),
            shape((1024, 512), BF),
            shape((512,), F32),
            shape((512, 512), F32),
            shape((512, 512), F32),
            shape((512, 512), F32),
            shape((512, 512), F32),
            shape((8, 32), F32),
            shape((512,), F32),
            shape((512, 2048), F32),
            shape((2048, 512), F32),
            shape((1,), F32),
            shape((3,), F32),
        ],
        in_specs=[anywhere] * 5 + [vmem],
        out_specs=[anywhere, anywhere, vmem]
        + [anywhere] * 4
        + [vmem, vmem, anywhere, anywhere, smem, smem],
        scratch_shapes=[
            full((2, 2, 4, 2, 2, 8, 2048)),
            low((2, 2, 128, 512)),
            low((512, 2048)),
            full((2048, 512)),
            low((2, 1024, 512)),
            full((UNITS, 512, WIDE)),
            dma((UNITS + 4,)),
            dma((UNITS + 2,)),
            dma((4,)),
        ],
        compiler_params=pltpu.CompilerParams(vmem_limit_bytes=60 * 2**20),
    )(*outs)
    layer, token_grad, *rest = results
    return (
        layer.reshape(block_shape),
        token_grad.reshape(block_shape),
        *rest[:5],
        rest[5].T,
        *rest[6:9],
        rest[9].reshape(()),
        rest[10],
    )


def solution(mesh):
    fast = mesh.shape["tower"] == 2 and mesh.shape["rows"] == 16
    return jax.shard_map(
        fast_shards if fast else shards,
        mesh=mesh,
        in_specs=(
            P("tower", "rows", None, None),
            P("tower", "rows", None),
            P("rows"),
            P(),
            P(),
            P(),
            P(),
            P(),
            P(),
            P(),
            P(),
            P(),
        ),
        out_specs=(
            P("tower", "rows", None, None),
            P("tower", "rows", None, None),
            P(),
            P(),
            P(),
            P(),
            P(),
            P(),
            P(),
            P(),
            P(),
            P(),
            P(),
        ),
        check_vma=False,
    )
```

```python
import functools
import math

import jax
import jax.numpy as jnp
import numpy as np
from jax import lax
from jax.experimental import pallas as pl
from jax.experimental.pallas import tpu as pltpu
from jax.sharding import PartitionSpec as P

MAX_DIST = 128
ITEMS_ROW = 8


EPSILON = 1e-06
SOFTMAX_TEMP = 0.01
LOSS_SCALE = 65536.0
MATMUL_PRECISION = lax.Precision.HIGHEST


def from_partner(value, axis, apart):
    mask = 2**apart
    pairs = [(source, source ^ mask) for source in range(lax.axis_size(axis))]
    return lax.ppermute(value, axis, pairs)


def bucket_table(length, bucket_count, far_limit):
    half_count = bucket_count // 2
    exact_count = half_count // 2
    entries = []
    for offset in range(1 - length, length):
        distance = abs(offset)
        if distance < exact_count:
            within = distance
        else:
            within = exact_count + int(
                math.log(distance / exact_count)
                / math.log(far_limit / exact_count)
                * (half_count - exact_count)
            )
            within = min(within, half_count - 1)
        entries.append(within + (half_count if offset > 0 else 0))
    by_offset = np.array(entries, dtype=np.int32)
    index_grid = np.arange(length)[None, :] - np.arange(length)[:, None] + length - 1
    return (by_offset, by_offset[index_grid])


def contract_rows(left_side, right_side):
    return lax.dot_general(
        left_side, right_side, (((0,), (0,)), ((), ())), preferred_element_type=jnp.float32
    )


def times_transpose(left_side, right_side):
    return lax.dot_general(
        left_side, right_side, (((1,), (1,)), ((), ())), preferred_element_type=jnp.float32
    )


def norm_scale(values):
    return lax.rsqrt(jnp.mean(values * values, axis=1, keepdims=True) + EPSILON)


def norm_back(grad_normed, values, scale, gain):
    gained = grad_normed * gain
    return scale * (
        gained - values * scale * scale * jnp.mean(gained * values, axis=1, keepdims=True)
    )


def row_scores(query_part, key_part, segment_row, position_bias, head_count):
    length = query_part.shape[0]
    query_heads = query_part.reshape(length, head_count, -1)
    key_heads = key_part.reshape(length, head_count, -1)
    scores = (
        jnp.einsum("qhd,khd->hqk", query_heads, key_heads, preferred_element_type=jnp.float32)
        + position_bias
    )
    same_item = segment_row[:, None] == segment_row[None, :]
    return jnp.where(same_item[None], scores, -1e30)


def diagonal_sums(square):
    head_count = square.shape[0]
    length = square.shape[1]
    flipped = square[:, :, ::-1]
    padded = jnp.pad(flipped, ((0, 0), (0, 0), (0, length)))
    sheared = padded.reshape(head_count, 2 * length * length)[:, : length * (2 * length - 1)]
    sheared = sheared.reshape(head_count, length, 2 * length - 1)
    return jnp.sum(sheared, axis=1)[:, ::-1]


def shards(
    tokens,
    segment_ids,
    positives,
    attention_gain,
    query_weight,
    key_weight,
    value_weight,
    output_weight,
    position_table,
    feedforward_gain,
    inner_weight,
    outer_weight,
):
    row_count = tokens.shape[1]
    length = tokens.shape[2]
    model_width = tokens.shape[3]
    head_count = position_table.shape[1]
    inner_width = query_weight.shape[1]
    head_size = inner_width // head_count
    token_count = row_count * length
    by_offset, bucket_index = bucket_table(length, position_table.shape[0], MAX_DIST)
    position_bias = jnp.take(position_table.T, jnp.asarray(bucket_index), axis=1)
    inputs = tokens.reshape(token_count, model_width).astype(jnp.float32)
    segments = segment_ids.reshape(row_count, length)
    scale_one = norm_scale(inputs)
    normed_one = (inputs * scale_one * attention_gain).astype(jnp.bfloat16)
    query_rows = jnp.dot(normed_one, query_weight, preferred_element_type=jnp.float32).astype(
        jnp.bfloat16
    )
    key_rows = jnp.dot(normed_one, key_weight, preferred_element_type=jnp.float32).astype(
        jnp.bfloat16
    )
    value_rows = jnp.dot(normed_one, value_weight, preferred_element_type=jnp.float32).astype(
        jnp.bfloat16
    )
    query_blocks = query_rows.reshape(row_count, length, inner_width)
    key_blocks = key_rows.reshape(row_count, length, inner_width)
    value_blocks = value_rows.reshape(row_count, length, inner_width)

    def attend(packed):
        query_part, key_part, value_part, segment_row = packed
        scores = row_scores(query_part, key_part, segment_row, position_bias, head_count)
        highest = jnp.max(scores, axis=2, keepdims=True)
        exp_scores = jnp.exp(scores - highest)
        exp_total = jnp.sum(exp_scores, axis=2, keepdims=True)
        attention_probs = (exp_scores / exp_total).astype(jnp.bfloat16)
        value_heads = value_part.reshape(length, head_count, head_size)
        mixed_heads = jnp.einsum(
            "hqk,khd->qhd", attention_probs, value_heads, preferred_element_type=jnp.float32
        )
        return (
            mixed_heads.reshape(length, inner_width).astype(jnp.bfloat16),
            (highest + jnp.log(exp_total))[:, :, 0],
        )

    mixed_blocks, log_totals = lax.map(attend, (query_blocks, key_blocks, value_blocks, segments))
    mixed_rows = mixed_blocks.reshape(token_count, inner_width)
    branch_one = jnp.dot(mixed_rows, output_weight, preferred_element_type=jnp.float32)
    middle = inputs + branch_one
    scale_two = norm_scale(middle)
    normed_two = (middle * scale_two * feedforward_gain).astype(jnp.bfloat16)
    hidden = jax.nn.relu(
        jnp.dot(normed_two, inner_weight, preferred_element_type=jnp.float32)
    ).astype(jnp.bfloat16)
    branch_two = jnp.dot(hidden, outer_weight, preferred_element_type=jnp.float32)
    result = middle + branch_two
    valid_mask = (segments < ITEMS_ROW).astype(jnp.float32).reshape(token_count, 1)
    stat_terms = jnp.stack(
        [
            jnp.sum(valid_mask * result * result),
            jnp.sum(valid_mask * branch_one * branch_one),
            jnp.sum(valid_mask * branch_two * branch_two),
            jnp.sum(valid_mask),
        ]
    )
    stat_totals = lax.psum(stat_terms, ("tower", "rows"))
    member = (segments[:, None, :] == jnp.arange(ITEMS_ROW)[None, :, None]).astype(jnp.float32)
    item_sizes = jnp.sum(member, axis=2, keepdims=True)
    result_blocks = result.reshape(row_count, length, model_width)
    pooled = (
        jnp.einsum("ris,rsd->rid", member, result_blocks, precision=MATMUL_PRECISION) / item_sizes
    )
    items_here = row_count * ITEMS_ROW
    pooled = pooled.reshape(items_here, model_width)
    inverse_norm = lax.rsqrt(jnp.sum(pooled * pooled, axis=1, keepdims=True) + EPSILON)
    embedded_tokens = pooled * inverse_norm
    tower_index = lax.axis_index("tower")
    is_query = tower_index == 0
    partner = from_partner(embedded_tokens, "tower", 0)
    query_vectors = jnp.where(is_query, embedded_tokens, partner)
    document_vectors = jnp.where(is_query, partner, embedded_tokens)
    gathered_documents = lax.all_gather(document_vectors, "rows", axis=0, tiled=True)
    item_total = gathered_documents.shape[0]
    half_items = items_here // 2
    my_queries = lax.dynamic_slice_in_dim(query_vectors, tower_index * half_items, half_items, 0)
    my_targets = lax.dynamic_slice_in_dim(positives, tower_index * half_items, half_items, 0)
    similarity_scores = (
        lax.dot_general(
            my_queries,
            gathered_documents,
            (((1,), (1,)), ((), ())),
            precision=MATMUL_PRECISION,
            preferred_element_type=jnp.float32,
        )
        / SOFTMAX_TEMP
    )
    highest = jnp.max(similarity_scores, axis=1, keepdims=True)
    exp_logits = jnp.exp(similarity_scores - highest)
    exp_total = jnp.sum(exp_logits, axis=1, keepdims=True)
    log_total = highest[:, 0] + jnp.log(exp_total[:, 0])
    is_target = jnp.arange(item_total)[None, :] == my_targets[:, None]
    target = jnp.sum(jnp.where(is_target, similarity_scores, 0.0), axis=1)
    loss_part = jnp.sum(log_total - target)
    similarity_gradient = (exp_logits / exp_total - is_target.astype(jnp.float32)) * (
        LOSS_SCALE / item_total
    )
    local_gradient = (
        jnp.dot(similarity_gradient, gathered_documents, precision=MATMUL_PRECISION) / SOFTMAX_TEMP
    )
    grad_documents = lax.psum_scatter(
        lax.dot_general(
            similarity_gradient,
            my_queries,
            (((0,), (0,)), ((), ())),
            precision=MATMUL_PRECISION,
            preferred_element_type=jnp.float32,
        )
        / SOFTMAX_TEMP,
        "rows",
        scatter_dimension=0,
        tiled=True,
    )
    partner_mine, partner_documents = from_partner((local_gradient, grad_documents), "tower", 0)
    query_side = jnp.where(
        is_query,
        jnp.concatenate([local_gradient, partner_mine], 0),
        jnp.concatenate([partner_mine, local_gradient], 0),
    )
    own_grad = jnp.where(is_query, query_side, grad_documents + partner_documents)
    inner_along = jnp.sum(own_grad * embedded_tokens, axis=1, keepdims=True)
    grad_pooled = inverse_norm * (own_grad - embedded_tokens * inner_along)
    per_token = grad_pooled.reshape(row_count, ITEMS_ROW, model_width) / item_sizes
    grad_result = jnp.einsum("ris,rid->rsd", member, per_token, precision=MATMUL_PRECISION).reshape(
        token_count, model_width
    )
    grad_branch_two = grad_result.astype(jnp.bfloat16)
    outer_grad = contract_rows(hidden, grad_branch_two)
    grad_hidden = times_transpose(grad_branch_two, outer_weight)
    grad_pre = jnp.where(hidden > 0, grad_hidden, 0.0).astype(jnp.bfloat16)
    inner_grad = contract_rows(normed_two, grad_pre)
    grad_normed_two = times_transpose(grad_pre, inner_weight)
    feedforward_gain_grad = jnp.sum(grad_normed_two * middle * scale_two, axis=0)
    grad_middle = grad_result + norm_back(grad_normed_two, middle, scale_two, feedforward_gain)
    grad_branch_one = grad_middle.astype(jnp.bfloat16)
    output_grad = contract_rows(mixed_rows, grad_branch_one)
    grad_mixed = times_transpose(grad_branch_one, output_weight).astype(jnp.bfloat16)
    grad_mixed_blocks = grad_mixed.reshape(row_count, length, inner_width)

    def attend_back(running, packed):
        query_part, key_part, value_part, segment_row, row_log_total, grad_part = packed
        scores = row_scores(query_part, key_part, segment_row, position_bias, head_count)
        attention_probs = jnp.exp(scores - row_log_total[:, :, None])
        query_heads = query_part.reshape(length, head_count, head_size)
        key_heads = key_part.reshape(length, head_count, head_size)
        value_heads = value_part.reshape(length, head_count, head_size)
        grad_heads = grad_part.reshape(length, head_count, head_size)
        grad_value = jnp.einsum(
            "hqk,qhd->khd",
            attention_probs.astype(jnp.bfloat16),
            grad_heads,
            preferred_element_type=jnp.float32,
        )
        grad_probs = jnp.einsum(
            "qhd,khd->hqk", grad_heads, value_heads, preferred_element_type=jnp.float32
        )
        row_dot = jnp.sum(attention_probs * grad_probs, axis=2, keepdims=True)
        grad_scores = (attention_probs * (grad_probs - row_dot)).astype(jnp.bfloat16)
        grad_query = jnp.einsum(
            "hqk,khd->qhd", grad_scores, key_heads, preferred_element_type=jnp.float32
        )
        grad_key = jnp.einsum(
            "hqk,qhd->khd", grad_scores, query_heads, preferred_element_type=jnp.float32
        )
        outputs = (
            grad_query.reshape(length, inner_width).astype(jnp.bfloat16),
            grad_key.reshape(length, inner_width).astype(jnp.bfloat16),
            grad_value.reshape(length, inner_width).astype(jnp.bfloat16),
        )
        return (running + grad_scores.astype(jnp.float32), outputs)

    score_sum, grad_rows = lax.scan(
        attend_back,
        jnp.zeros((head_count, length, length), jnp.float32),
        (query_blocks, key_blocks, value_blocks, segments, log_totals, grad_mixed_blocks),
    )
    grad_queries = grad_rows[0].reshape(token_count, inner_width)
    grad_keys = grad_rows[1].reshape(token_count, inner_width)
    grad_values = grad_rows[2].reshape(token_count, inner_width)
    query_grad = contract_rows(normed_one, grad_queries)
    key_grad = contract_rows(normed_one, grad_keys)
    value_grad = contract_rows(normed_one, grad_values)
    grad_normed_one = (
        times_transpose(grad_queries, query_weight)
        + times_transpose(grad_keys, key_weight)
        + times_transpose(grad_values, value_weight)
    )
    attention_gain_grad = jnp.sum(grad_normed_one * inputs * scale_one, axis=0)
    token_grad = grad_middle + norm_back(grad_normed_one, inputs, scale_one, attention_gain)
    offset_onehot = jnp.asarray(
        (by_offset[:, None] == np.arange(position_table.shape[0])[None, :]).astype(np.float32)
    )
    position_grad = jnp.dot(diagonal_sums(score_sum), offset_onehot, precision=MATMUL_PRECISION).T
    closing_terms = loss_part[None]
    summed = lax.psum(
        (
            attention_gain_grad,
            query_grad,
            key_grad,
            value_grad,
            output_grad,
            position_grad,
            feedforward_gain_grad,
            inner_grad,
            outer_grad,
            closing_terms,
        ),
        ("tower", "rows"),
    )
    (
        attention_gain_grad,
        query_grad,
        key_grad,
        value_grad,
        output_grad,
        position_grad,
        feedforward_gain_grad,
        inner_grad,
        outer_grad,
        closing_totals,
    ) = summed
    contrastive_loss = closing_totals[0] / item_total
    root_mean_squares = jnp.sqrt(stat_totals[:3] / (stat_totals[3] * model_width))
    block_shape = (1, row_count, length, model_width)
    return (
        result.reshape(block_shape).astype(jnp.bfloat16),
        token_grad.reshape(block_shape).astype(jnp.bfloat16),
        attention_gain_grad,
        query_grad,
        key_grad,
        value_grad,
        output_grad,
        position_grad,
        feedforward_gain_grad,
        inner_grad,
        outer_grad,
        contrastive_loss,
        root_mean_squares,
    )


F32 = jnp.float32
BF = jnp.bfloat16
MESH = pl.DeviceIdType.MESH
NN = (((1,), (0,)), ((), ()))
NT = (((1,), (1,)), ((), ()))
TN = (((0,), (0,)), ((), ()))
WIDE = 128
UNITS = 4096 // WIDE
PER_PART = 256 // WIDE
STEPS_AFTER = (
    (),
    (0, 1, 2, 3,),
    (4, 5, 6, 7,),
    (8, 9, 10, 11, 0, 1,),
    (12, 13, 2, 3, 14, 15,),
    (),
    (0, 1, 4, 5,),
    (2, 3, 6, 7,),
    (8, 9,),
    (4, 5, 10, 11, 16, 17, 18, 19,),
    (6, 7, 12, 13, 8, 14, 15,),
    (0, 1, 2, 3, 9, 10,),
    (11, 12,),
    (13,),
    (14,),
    (20, 15, 21,),
    (0, 1, 2, 3, 4, 5, 22, 23, 24, 25,),
    (16, 17,),
    (0, 6, 1, 7, 8, 9, 10, 11, 2, 18, 13, 12, 19,),
    (3, 4, 5, 14, 15, 16, 17, 20, 21,),
    (),
    (6, 7, 22, 23, 8,),
    (9, 18, 10, 26, 27, 28,),
    (0, 1, 2, 3, 4, 11, 12, 13, 16, 17, 5, 19, 24, 25, 29, 30, 14, 31,),
    (6, 7, 15, 18, 20, 8, 21, 22, 23,),
    (0, 9, 10, 26, 27,),
    (1, 2, 4, 5, 24, 28,),
    (3, 11, 12, 13, 14, 15, 16, 17, 18, 19, 25, 29, 30, 7, 6, 20, 31, 32, 8, 21, 10, 22, 0, 26, 23, 4, 9, 5, 27, 0, 1, 16, 24, 28, 17, 2, 18, 1, 19, 11, 13, 25, 7, 15, 2, 3, 12, 6, 29, 14, 3, 31, 30, 20, 8, 32, 5, 21, 10, 16, 4, 18, 17, 5, 22, 4, 26, 7, 6, 23, 9, 20, 7, 32, 6, 27, 8, 24, 22, 21, 19, 28, 8, 11, 13, 10, 9, 23, 25, 15, 10, 24, 9, 12, 20, 21, 29, 14, 20, 22, 19, 21, 31, 11, 25, 30, 22, 16, 11, 18, 13, 24, 17, 13, 23, 24, 32, 26, 12, 23, 15, 27, 12, 14, 28, 29, 15, 19, 25, 14, 16, 32, 31, 25, 17, 30, 16, 18, 26, 27, 17, 28, 18, 29, 31, 19, 30, 19, 26, 27, 26, 28, 27, 29, 28, 30, 29, 31, 30, 31,),
)
SMALL = UNITS
PIECES = len(STEPS_AFTER)
FAR = 512
NEAR = 384
WINDOWS = ((0, 256, 128), (0, 384, 0), (128, 384, 0), (256, 256, 0))


def dot(a, b, dims=NN):
    return lax.dot_general(a, b, dims, preferred_element_type=F32)


def exact_dot(a, b, dims=NN):
    return lax.dot_general(
        a, b, dims, precision=lax.Precision.HIGHEST, preferred_element_type=F32
    )


def tile(index, size):
    if isinstance(index, int):
        return pl.ds(index * size, size)
    return pl.ds(pl.multiple_of(index * size, size), size)


def far_limits(bucket_count, far_limit):
    half_count = bucket_count // 2
    exact_count = half_count // 2
    limits = []
    reached = exact_count
    for distance in range(exact_count, 512):
        within = exact_count + int(
            math.log(distance / exact_count)
            / math.log(far_limit / exact_count)
            * (half_count - exact_count)
        )
        within = min(within, half_count - 1)
        while reached < within:
            limits.append(distance)
            reached += 1
    return limits


def bucket_onehot(offset):
    distance = jnp.abs(offset)
    far = jnp.full_like(distance, 8)
    for limit in far_limits(32, MAX_DIST):
        far = far + jnp.where(distance >= limit, 1, 0)
    bucket = jnp.where(distance < 8, distance, far) + jnp.where(offset > 0, 16, 0)
    same = bucket == lax.broadcasted_iota(jnp.int32, (32, FAR), 0)
    return jnp.where(same, 1.0, 0.0).astype(F32)


def split_three(value):
    high = value.astype(BF)
    rest = value - high.astype(F32)
    middle = rest.astype(BF)
    return high, middle, (rest - middle.astype(F32)).astype(BF)


class Place:
    def __init__(self):
        self.tower = lax.axis_index("tower")
        self.rows = lax.axis_index("rows")
        self.flat = lax.rem(self.rows, 4)
        self.deep = lax.div(self.rows, 4)
        bits = {
            "x": lax.rem(self.rows, 2),
            "y": lax.rem(lax.div(self.rows, 2), 2),
            "z": lax.rem(lax.div(self.rows, 4), 2),
            "w": lax.div(self.rows, 8),
        }
        steps = {"x": 1, "y": 2, "z": 4, "w": 8}
        self.bit = {"c": self.tower, **bits}
        self.to = {"c": self.device(1 - self.tower, self.rows)}
        for name, step in steps.items():
            self.to[name] = self.device(self.tower, self.rows + step * (1 - 2 * bits[name]))

    def device(self, tower, rows):
        return {"tower": tower, "rows": rows}

    def along_deep(self, step):
        return self.device(self.tower, lax.rem(self.deep + step, 4) * 4 + self.flat)

    def along_flat(self, step):
        return self.device(self.tower, self.deep * 4 + lax.rem(self.flat + step, 4))


def order_of(unit):
    return (("cxzyw", "cyzxw") if 8 * unit < 5 * UNITS else ("cxyZ", "cyxZ"))[unit % 2]


class Sums:
    def __init__(self, place, total, landed, out, small, small_landed, sems):
        self.place, self.total, self.landed, self.out = place, total, landed, out
        self.small, self.small_landed = small, small_landed
        self.send_sem, self.recv_sem, self.out_sem, self.small_send, self.small_recv = sems
        self.plans = {}
        self.stage = {}
        for unit in range(UNITS):
            order = order_of(unit)
            if order not in self.plans:
                self.plans[order] = self.plan(order)

    def plan(self, order):
        place, steps = self.place, []
        base, size, offset, sem = 0, 512, 0, 0
        for name in order:
            ways = 4 if name == "Z" else 2
            size //= ways
            spot = place.deep if name == "Z" else place.bit[name]
            partners = []
            for i in range(1, ways):
                if name == "Z":
                    piece, device = lax.rem(place.deep + i, 4), place.along_deep(i)
                else:
                    piece, device = 1 - spot, place.to[name]
                partners.append((base + piece * size, device, offset, sem))
                offset, sem = offset + size, sem + 1
            base = base + spot * size
            steps.append((size, base, partners))
        return steps

    def remote(self, source, target, index, unit, device):
        return pltpu.make_async_remote_copy(
            src_ref=source,
            dst_ref=target,
            send_sem=self.send_sem.at[index, unit],
            recv_sem=self.recv_sem.at[index, unit],
            device_id=device,
            device_id_type=MESH,
        )

    def depth(self, unit):
        return 5 if unit == SMALL else 2 * len(order_of(unit))

    def rows(self, start, size):
        return pl.ds(pl.multiple_of(start, size), size)

    def keep(self, unit):
        size, base, _ = self.plans[order_of(unit)][-1]
        rows = self.rows(base, size)
        return pltpu.make_async_copy(
            self.total.at[unit, rows], self.out.at[unit, rows], self.out_sem.at[unit]
        )

    def copies(self, stage, unit):
        if unit == SMALL:
            return [
                pltpu.make_async_remote_copy(
                    src_ref=self.small,
                    dst_ref=self.small_landed.at[stage],
                    send_sem=self.small_send.at[stage],
                    recv_sem=self.small_recv.at[stage],
                    device_id=self.place.to["cxyzw"[stage]],
                    device_id_type=MESH,
                )
            ]
        plan = self.plans[order_of(unit)]
        if stage < len(plan):
            size, _, partners = plan[stage]
            return [
                self.remote(
                    self.total.at[unit, self.rows(start, size)],
                    self.landed.at[unit, pl.ds(offset, size)],
                    sem,
                    unit,
                    device,
                )
                for start, device, offset, sem in partners
            ]
        back = 2 * len(plan) - 1 - stage
        size, base, partners = plan[back]
        rows = self.rows(base, size)
        source = self.total if stage == len(plan) else self.out
        return [
            self.remote(source.at[unit, rows], self.out.at[unit, rows], 6 + sem, unit, device)
            for _, device, _, sem in partners
        ]

    def step(self, unit):
        stage = self.stage.get(unit, -1)
        plan = None if unit == SMALL else self.plans[order_of(unit)]
        if stage >= 0:
            for copy in self.copies(stage, unit):
                copy.wait()
            if unit == SMALL:
                self.small[...] += self.small_landed[stage]
            elif stage < len(plan):
                size, base, partners = plan[stage]
                parts = [self.landed[unit, pl.ds(p[2], size), :] for p in partners]
                self.total[unit, self.rows(base, size), :] += sum(parts[1:], parts[0])
            elif stage == len(plan):
                self.keep(unit).wait()
        stage += 1
        self.stage[unit] = stage
        if stage < self.depth(unit):
            for copy in self.copies(stage, unit):
                copy.start()
            if plan is not None and stage == len(plan):
                self.keep(unit).start()

    def fill(self, part, value):
        for i in range(PER_PART):
            self.total[part * PER_PART + i] = value[:, i * WIDE : (i + 1) * WIDE]

    def after(self, piece, *parts):
        for part in parts:
            for i in range(PER_PART):
                self.step(part * PER_PART + i)
        if piece == PIECES - 1:
            self.step(SMALL)
        for unit in STEPS_AFTER[piece]:
            self.step(unit)


class Spread:
    def __init__(self, place, blocks, send_sem, recv_sem):
        self.place, self.blocks = place, blocks
        self.send_sem, self.recv_sem = send_sem, recv_sem

    def copy(self, row, index, where, device):
        ref = self.blocks.at[where]
        return pltpu.make_async_remote_copy(
            src_ref=ref,
            dst_ref=ref,
            send_sem=self.send_sem.at[row, index],
            recv_sem=self.recv_sem.at[row, index],
            device_id=device,
            device_id_type=MESH,
        )

    def one(self, row, i):
        place = self.place
        where = (row, place.tower, place.deep, place.flat)
        return self.copy(row, i, where, place.along_deep(i + 1))

    def copies(self, row, stage):
        place = self.place
        if stage == 0:
            return [self.one(row, i) for i in range(3)]
        if stage == 1:
            where = (row, place.tower, slice(None), place.flat)
            return [self.copy(row, 3 + i, where, place.along_flat(i + 1)) for i in range(3)]
        return [self.copy(row, 6, (row, place.tower), place.to["c"])]

    def start(self, row, stage):
        for copy in self.copies(row, stage):
            copy.start()

    def wait(self, row, stage):
        for copy in self.copies(row, stage):
            copy.wait()


def layer_kernel(
    tokens_hbm,
    segment_ref,
    positive_ref,
    gain_one_ref,
    query_hbm,
    key_hbm,
    value_hbm,
    output_hbm,
    table_ref,
    gain_two_ref,
    inner_hbm,
    outer_hbm,
    layer_hbm,
    token_grad_hbm,
    sums_hbm,
    hidden_sum_hbm,
    rows_grad_hbm,
    small_ref,
    tokens,
    query_w,
    key_w,
    value_w,
    output_w,
    inner_w,
    outer_w,
    normed_one,
    queries,
    keys,
    values,
    probs,
    side_probs,
    mixed,
    middle,
    normed_two,
    hidden,
    bias,
    segment_column,
    segment_row,
    pooled_all,
    hidden_sum,
    normed_one_t,
    normed_two_t,
    mixed_t,
    grad_mixed,
    grad_query,
    grad_key,
    grad_value,
    key_total,
    value_total,
    total,
    landed,
    expand,
    rounded_grads,
    small_landed,
    load_sem,
    store_sem,
    sum_send,
    sum_recv,
    sum_out,
    pool_send,
    pool_recv,
    hidden_send,
    hidden_recv,
    small_send,
    small_recv,
    relay_send,
    relay_recv,
):
    place = Place()
    barrier = pltpu.get_barrier_semaphore()
    partners = [place.to["c"]]
    partners += [place.along_deep(i) for i in (1, 2, 3)]
    partners += [place.along_flat(i) for i in (1, 2, 3)]
    for partner in partners:
        pl.semaphore_signal(barrier, inc=1, device_id=partner, device_id_type=MESH)

    loads = [
        pltpu.make_async_copy(source, target, load_sem.at[i])
        for i, (source, target) in enumerate(
            (
                (tokens_hbm, tokens),
                (query_hbm, query_w),
                (key_hbm, key_w),
                (value_hbm, value_w),
                (output_hbm, output_w),
                (inner_hbm, inner_w),
                (outer_hbm, outer_w),
            )
        )
    ]
    for load in loads:
        load.start()

    segment_row[...] = segment_ref[...].astype(F32)
    for i in range(8):
        row = segment_row[i // 4 : i // 4 + 1, (i % 4) * 128 : (i % 4) * 128 + 128]
        segment_column[i * 128 : (i + 1) * 128, :] = jnp.broadcast_to(row, (128, 128)).T
    place_row = lax.broadcasted_iota(jnp.int32, (32, FAR), 1)
    offsets = jnp.where(place_row >= NEAR, place_row - FAR, place_row) - 128
    by_place = exact_dot(table_ref[...], bucket_onehot(offsets))
    for h in range(8):
        spread = jnp.broadcast_to(by_place[h : h + 1], (128, FAR))
        bias[h] = pltpu.roll(spread, 0, 1, stride=1, stride_axis=0)[:, :NEAR]
    pooling = Spread(place, pooled_all, pool_send, pool_recv)
    sums = Sums(
        place,
        total,
        landed,
        sums_hbm,
        small_ref,
        small_landed,
        (sum_send, sum_recv, sum_out, small_send, small_recv),
    )

    def hidden_slot(row):
        return hidden_sum_hbm.at[row, place.tower, place.deep, place.bit["y"], place.bit["x"]]

    def save_hidden(row):
        return pltpu.make_async_copy(hidden_sum.at[row], hidden_slot(row), store_sem.at[row])

    def hidden_copy(source, target, row, index, device):
        return pltpu.make_async_remote_copy(
            src_ref=source,
            dst_ref=target,
            send_sem=hidden_send.at[row, index],
            recv_sem=hidden_recv.at[row, index],
            device_id=device,
            device_id_type=MESH,
        )

    def go(copies, start):
        for copy in copies:
            if start:
                copy.start()
            else:
                copy.wait()

    def deepen_hidden(row, start):
        source = hidden_sum.at[row]
        target = hidden_slot(row)
        copies = [
            hidden_copy(source, target, row, i - 1, place.along_deep(i)) for i in (1, 2, 3)
        ]
        go(copies, start)

    def widen_hidden(row, step, start):
        ref = hidden_sum_hbm.at[row, place.tower]
        y, x = place.bit["y"], place.bit["x"]
        left, right = pl.ds(0, 1024), pl.ds(1024, 1024)
        if step == 0:
            parts = (ref.at[:, y, x, :, left], "x"), (ref.at[:, y, x, :, right], "y")
        else:
            parts = (ref.at[:, y, :, :, left], "y"), (ref.at[:, :, x, :, right], "x")
        copies = [
            hidden_copy(part, part, row, 3 + 2 * step + i, place.to[name])
            for i, (part, name) in enumerate(parts)
        ]
        go(copies, start)

    def swap_hidden(row, start):
        ref = hidden_sum_hbm.at[row, place.tower]
        go([hidden_copy(ref, ref, row, 7, place.to["c"])], start)

    def relay(step, start):
        ref = pooled_all.at[1, place.tower, lax.rem(place.deep + 4 - step, 4), place.flat]
        copies = [
            pltpu.make_async_remote_copy(
                src_ref=ref,
                dst_ref=ref,
                send_sem=relay_send.at[step, i - 1],
                recv_sem=relay_recv.at[step, i - 1],
                device_id=place.along_flat(i),
                device_id_type=MESH,
            )
            for i in (1, 2, 3)
        ]
        go(copies, start)

    head_lane = lax.broadcasted_iota(jnp.int32, (1, 256), 1) // 64
    head_mask = [jnp.where(head_lane == h, 1.0, 0.0) for h in range(4)]
    head_mask_low = [mask.astype(BF) for mask in head_mask]

    def stack_heads(part):
        return jnp.concatenate([part * mask for mask in head_mask_low], 0)

    def pick_heads(part):
        return sum(part[h * 128 : (h + 1) * 128] * head_mask[h] for h in range(4))

    def project(i, carry):
        rows = tile(i, 256)
        x = tokens[rows, :].astype(F32)
        scale = lax.rsqrt(jnp.mean(x * x, axis=1, keepdims=True) + EPSILON)
        normed = (x * scale * gain_one_ref[...]).astype(BF)
        normed_one[rows, :] = normed
        queries[rows, :] = dot(normed, query_w[...]).astype(BF)
        keys[rows, :] = dot(normed, key_w[...]).astype(BF)
        values[rows, :] = dot(normed, value_w[...]).astype(BF)
        return carry

    def window(r, b):
        start, width, offset = WINDOWS[b]
        base = r * 512
        own = pl.ds(pl.multiple_of(base + b * 128, 128), 128)
        near = pl.ds(pl.multiple_of(base + start, 128), width)
        return own, near, slice(start, start + width), slice(offset, offset + width)

    def soft(r, b, g):
        if b in (0, 3):
            return side_probs.at[r, b // 3, g]
        return probs.at[r, b - 1, g]

    def attend(b, r, carry):
        own, near, near_row, offset = window(r, b)
        column = segment_column[own, :]
        row = segment_row[pl.ds(r, 1), near_row]
        same = jnp.concatenate([column] * (WINDOWS[b][1] // 128), 1) == row
        for g in range(2):
            lanes = slice(g * 256, (g + 1) * 256)
            scores = dot(stack_heads(queries[own, lanes]), keys[near, lanes], NT)
            parts = []
            for h in range(4):
                part = scores[h * 128 : (h + 1) * 128] + bias[g * 4 + h, :, offset]
                part = jnp.where(same, part, -1e30)
                highest = jnp.max(part, axis=1, keepdims=True)
                exp_part = jnp.exp(part - highest)
                exp_total = jnp.sum(exp_part, axis=1, keepdims=True)
                parts.append((exp_part * (1.0 / exp_total)).astype(BF))
            stacked = jnp.concatenate(parts, 0)
            soft(r, b, g)[...] = stacked
            mixed[own, lanes] = pick_heads(dot(stacked, values[near, lanes])).astype(BF)
        return carry

    def feed(i, carry):
        rows = tile(i, 256)
        branch = dot(mixed[rows, :], output_w[...])
        mid = tokens[rows, :].astype(F32) + branch
        middle[rows, :] = mid
        scale = lax.rsqrt(jnp.mean(mid * mid, axis=1, keepdims=True) + EPSILON)
        normed = (mid * scale * gain_two_ref[...]).astype(BF)
        normed_two[rows, :] = normed
        for c in range(4):
            lanes = slice(c * 512, (c + 1) * 512)
            hidden[rows, lanes] = jnp.maximum(dot(normed, inner_w[:, lanes]), 0.0).astype(BF)
        return carry

    def pool(r):
        rows = tile(r, 512)
        number = lax.broadcasted_iota(jnp.int32, (8, 512), 0).astype(F32)
        member = jnp.where(segment_row[pl.ds(r, 1), :] == number, 1.0, 0.0)
        member_low = jnp.concatenate([member, jnp.zeros_like(member)], 0).astype(BF)
        count = jnp.sum(member, axis=1, keepdims=True)
        hidden_part = dot(member_low, hidden[rows, :])[:8]
        hidden_sum[r] = hidden_part
        middle_part = sum(dot(member_low, piece) for piece in split_three(middle[rows, :]))[:8]
        pieces = split_three(hidden_part)
        stacked = jnp.concatenate([*pieces, jnp.zeros_like(pieces[0])], 0)
        branch = dot(stacked, outer_w[...])
        pooled = (middle_part + (branch[0:8] + branch[8:16] + branch[16:24])) / count
        sublane = lax.broadcasted_iota(jnp.int32, (8, 128), 0)
        ids = jnp.zeros((8, 128), F32)
        for s in range(8):
            ids = jnp.where(sublane == s, positive_ref[r * 8 + s].astype(F32), ids)
        lanes = lax.broadcasted_iota(jnp.int32, (8, 128), 1)
        extra = jnp.where(lanes == 0, ids, count)
        pooled_all[r, place.tower, place.deep, place.flat] = jnp.concatenate([pooled, extra], 1)

    small_ref[...] = jnp.zeros_like(small_ref)
    in_item = jnp.where(segment_row[...] < ITEMS_ROW, 512.0, 0.0)
    small_ref[5:6, :] = jnp.sum(in_item, axis=0, keepdims=True)
    for i in range(4):
        loads[i].wait()
    pl.semaphore_wait(barrier, len(partners))

    def forward(r, carry):
        first, second = r == 0, r == 1
        lax.fori_loop(2 * r, 2 * r + 2, project, 0)
        attend(0, r, 0)
        attend(1, r, 0)

        attend(2, r, 0)
        attend(3, r, 0)

        @pl.when(first)
        def _():
            for i in (4, 5):
                loads[i].wait()

        @pl.when(second)
        def _():
            pooling.wait(0, 0)
            pooling.start(0, 1)

        lax.fori_loop(2 * r, 2 * r + 2, feed, 0)

        @pl.when(first)
        def _():
            loads[6].wait()

        pool(r)
        pooling.start(r, 0)

        @pl.when(second)
        def _():
            relay(0, start=True)
            save_hidden(0).wait()
            deepen_hidden(0, start=False)
            widen_hidden(0, 0, start=True)

        deepen_hidden(r, start=True)
        save_hidden(r).start()
        return carry

    lax.fori_loop(0, 2, forward, 0)

    def store_rows(source, target, i, index):
        rows = tile(i, 256)
        return pltpu.make_async_copy(source.at[rows], target.at[rows], store_sem.at[index])

    def close(i, carry):
        rows = tile(i, 256)
        branch = dot(hidden[rows, :], outer_w[...])
        mid = middle[rows, :]
        first = mid - tokens[rows, :].astype(F32)
        result = mid + branch
        grad_query[rows, :] = result.astype(BF)
        valid = jnp.where(segment_column[rows, 0:1] < ITEMS_ROW, 1.0, 0.0)
        small_ref[2:3, :] += jnp.sum(valid * result * result, axis=0, keepdims=True)
        small_ref[3:4, :] += jnp.sum(valid * first * first, axis=0, keepdims=True)
        small_ref[4:5, :] += jnp.sum(valid * branch * branch, axis=0, keepdims=True)
        return carry

    def turn(i, carry):
        rows = tile(i, 128)
        normed_two_t[:, rows] = normed_two[rows, :].T
        mixed_t[:, rows] = mixed[rows, :].T
        normed_one_t[:, rows] = normed_one[rows, :].T
        return carry

    lax.fori_loop(0, 3, close, 0)
    for step in (1, 2, 3):
        if step == 3:
            lax.fori_loop(3, 4, close, 0)
        pooling.one(1, step - 1).wait()
        relay(step, start=True)
    pooling.wait(0, 1)
    pooling.start(0, 2)
    for i in range(4):
        store_rows(grad_query, layer_hbm, i, 2 + i).start()
    save_hidden(1).wait()
    lax.fori_loop(0, 8, turn, 0)
    widen_hidden(0, 0, start=False)
    widen_hidden(0, 1, start=True)
    lane = lax.broadcasted_iota(jnp.int32, (1, 128), 1)
    item = segment_column[...] + jnp.where(
        lax.broadcasted_iota(jnp.int32, (1024, 128), 0) >= 512, 8.0, 0.0
    )
    item = jnp.where(segment_column[...] < ITEMS_ROW, item, -1.0)
    slot = jnp.where(lane < 48, lax.rem(lane, 16), -2).astype(F32)
    expand[...] = jnp.where(item == slot, 1.0, 0.0).astype(BF)
    for step in range(4):
        relay(step, start=False)
    pooling.start(1, 2)
    deepen_hidden(1, start=False)
    widen_hidden(1, 0, start=True)
    pooling.wait(0, 2)
    pooling.wait(1, 2)

    gathered = [
        jnp.concatenate([pooled_all[r, t].reshape(128, 640) for r in range(2)], 0)
        for t in range(2)
    ]
    vectors, inverse, counts, embedded = [], [], [], []
    for t in range(2):
        vector = gathered[t][:, :512]
        scale = lax.rsqrt(jnp.sum(vector * vector, axis=1, keepdims=True) + EPSILON)
        vectors.append(vector)
        inverse.append(scale)
        embedded.append(vector * scale)
        counts.append(gathered[t][:, 513:514])
    logits = exact_dot(embedded[0], embedded[1], NT) / SOFTMAX_TEMP
    highest = jnp.max(logits, axis=1, keepdims=True)
    exp_logits = jnp.exp(logits - highest)
    exp_total = jnp.sum(exp_logits, axis=1, keepdims=True)
    position = lax.broadcasted_iota(jnp.int32, (256, 256), 1)
    number = lax.rem(lax.div(position, 8), 16) * 16 + lax.div(position, 128) * 8
    number = (number + lax.rem(position, 8)).astype(F32)
    is_target = gathered[0][:, 512:513] == number
    target = jnp.sum(jnp.where(is_target, logits, 0.0), axis=1, keepdims=True)
    losses = highest + jnp.log(exp_total) - target
    loss = jnp.sum(losses, axis=0, keepdims=True) / 256
    grad_logits = (exp_logits / exp_total - jnp.where(is_target, 1.0, 0.0)) * (LOSS_SCALE / 256)
    grads = (
        exact_dot(grad_logits, embedded[1]) / SOFTMAX_TEMP,
        exact_dot(grad_logits, embedded[0], TN) / SOFTMAX_TEMP,
    )
    for t in range(2):
        along = jnp.sum(grads[t] * embedded[t], axis=1, keepdims=True)
        per_token = inverse[t] * (grads[t] - embedded[t] * along) / counts[t]
        for r in range(2):
            part = per_token[r * 128 : (r + 1) * 128]
            for i in range(512 // WIDE):
                total[UNITS - 4 + 2 * r + t, i * 128 : (i + 1) * 128] = part[
                    :, i * WIDE : (i + 1) * WIDE
                ]
            rounded_grads[r, t] = per_token[r * 128 : (r + 1) * 128].astype(BF)
    save_grads = pltpu.make_async_copy(rounded_grads, rows_grad_hbm, store_sem.at[6])
    save_grads.start()
    own_parts = []
    for r in range(2):
        spot = UNITS - 4 + 2 * r + place.tower
        lanes = [total[spot, tile(place.rows + 16 * i, 8)] for i in range(512 // WIDE)]
        own_parts.append(jnp.concatenate(lanes, 1))
    own = jnp.concatenate(own_parts, 0)
    pieces = split_three(own)
    own_low = pieces[0]
    own_split = jnp.concatenate([*pieces, jnp.zeros((80, 512), BF)], 0)

    def back_hidden(c):
        lanes = slice(c * 512, (c + 1) * 512)
        row_part = dot(own_low, outer_w[lanes, :], NT).astype(BF)
        row_part = jnp.concatenate([row_part, jnp.zeros((112, 512), BF)], 0)

        def mask(i, carry):
            rows = tile(i, 256)
            spread = dot(expand[rows, :], row_part)
            hidden[rows, lanes] = jnp.where(hidden[rows, lanes] > 0, spread, 0.0).astype(BF)
            return carry

        lax.fori_loop(0, 4, mask, 0)
        for half in range(2):
            part = 2 * c + half
            columns = slice(part * 256, (part + 1) * 256)
            sums.fill(part, dot(normed_two_t[...], hidden[:, columns]))
        sums.after(c, 2 * c, 2 * c + 1)

    def back_middle(i, carry):
        rows = tile(i, 256)
        grad_normed = dot(hidden[rows, :], inner_w[...], NT)
        mid = middle[rows, :]
        scale = lax.rsqrt(jnp.mean(mid * mid, axis=1, keepdims=True) + EPSILON)
        small_ref[1:2, :] += jnp.sum(grad_normed * mid * scale, axis=0, keepdims=True)
        gained = grad_normed * gain_two_ref[...]
        mean = jnp.mean(gained * mid, axis=1, keepdims=True)
        grad_mid = dot(expand[rows, :], own_split) + scale * (gained - mid * scale * scale * mean)
        middle[rows, :] = grad_mid
        rounded = grad_mid.astype(BF)
        mixed[rows, :] = rounded
        grad_mixed[rows, :] = dot(rounded, output_w[...], NT).astype(BF)
        return carry

    for c in range(4):
        back_hidden(c)
    for i in range(2):
        lax.fori_loop(2 * i, 2 * i + 2, back_middle, 0)
        sums.after(4 + 2 * i)
        sums.after(5 + 2 * i)
    for half in range(2):
        sums.fill(8 + half, dot(mixed_t[...], mixed[:, half * 256 : (half + 1) * 256]))
    widen_hidden(1, 0, start=False)
    widen_hidden(1, 1, start=True)
    sums.after(8, 8, 9)

    for i in range(4):
        store_rows(grad_query, layer_hbm, i, 2 + i).wait()
    bias[...] = jnp.zeros_like(bias)

    def attend_back(g, b, r, carry):
        own, near, _, offset = window(r, b)
        lanes = slice(g * 256, (g + 1) * 256)
        grad_stack = stack_heads(grad_mixed[own, lanes])
        grad_soft = dot(grad_stack, values[near, lanes], NT)
        weight = soft(r, b, g)[...]
        parts = []
        for h in range(4):
            rows = slice(h * 128, (h + 1) * 128)
            soft_part = weight[rows].astype(F32)
            grad_part = grad_soft[rows]
            along = jnp.sum(soft_part * grad_part, axis=1, keepdims=True)
            part = (soft_part * (grad_part - along)).astype(BF)
            bias[g * 4 + h, :, offset] += part.astype(F32)
            parts.append(part)
        stacked = jnp.concatenate(parts, 0)
        grad_query[own, lanes] = pick_heads(dot(stacked, keys[near, lanes])).astype(BF)
        key_total[near, :] += dot(stacked, stack_heads(queries[own, lanes]), TN)
        value_total[near, :] += dot(weight, grad_stack, TN)
        return carry

    for g in range(2):
        lanes = slice(g * 256, (g + 1) * 256)
        key_total[...] = jnp.zeros_like(key_total)
        value_total[...] = jnp.zeros_like(value_total)
        for b in range(4):
            lax.fori_loop(0, 2, functools.partial(attend_back, g, b), 0)
            sums.after(9 + 7 * g + b)
        part, piece = 10 + 3 * g, 13 + 7 * g
        sums.fill(part, dot(normed_one_t[...], grad_query[:, lanes]))
        sums.after(piece, part)
        grad_key[:, lanes] = key_total[...].astype(BF)
        sums.fill(part + 1, dot(normed_one_t[...], grad_key[:, lanes]))
        sums.after(piece + 1, part + 1)
        grad_value[:, lanes] = value_total[...].astype(BF)
        sums.fill(part + 2, dot(normed_one_t[...], grad_value[:, lanes]))
        sums.after(piece + 2, part + 2)
        if g == 0:
            widen_hidden(0, 1, start=False)
            swap_hidden(0, start=True)
    widen_hidden(1, 1, start=False)
    swap_hidden(0, start=False)
    swap_hidden(1, start=True)

    def back_tokens(i, carry):
        rows = tile(i, 256)
        grad_normed = (
            dot(grad_query[rows, :], query_w[...], NT)
            + dot(grad_key[rows, :], key_w[...], NT)
            + dot(grad_value[rows, :], value_w[...], NT)
        )
        x = tokens[rows, :].astype(F32)
        scale = lax.rsqrt(jnp.mean(x * x, axis=1, keepdims=True) + EPSILON)
        small_ref[0:1, :] += jnp.sum(grad_normed * x * scale, axis=0, keepdims=True)
        gained = grad_normed * gain_one_ref[...]
        mean = jnp.mean(gained * x, axis=1, keepdims=True)
        grad = middle[rows, :] + scale * (gained - x * scale * scale * mean)
        normed_one[rows, :] = grad.astype(BF)
        return carry

    for i in range(2):
        lax.fori_loop(2 * i, 2 * i + 2, back_tokens, 0)
        for j in (2 * i, 2 * i + 1):
            store_rows(normed_one, token_grad_hbm, j, 2 + j).start()
            sums.after(23 + j)
    mirror = (
        lax.broadcasted_iota(jnp.int32, (128, 128), 0)
        + lax.broadcasted_iota(jnp.int32, (128, 128), 1)
    )
    mirror = jnp.where(mirror == 127, 1.0, 0.0)
    diagonals = []
    for h in range(8):
        turned = exact_dot(mirror, bias[h])
        wide = jnp.concatenate([turned, jnp.zeros((128, FAR - NEAR), F32)], 1)
        wide = pltpu.roll(wide, 0, 1, stride=1, stride_axis=0)
        diagonals.append(jnp.sum(wide, axis=0, keepdims=True))
    buckets = exact_dot(jnp.concatenate(diagonals, 0), bucket_onehot(place_row - 255), NT)
    small_ref[8:16, :] = jnp.concatenate([buckets, jnp.zeros((8, 480), F32)], 1)
    sums.after(27)
    small_ref[6:7, :] = jnp.broadcast_to(loss, (1, 512))
    swap_hidden(1, start=False)
    save_grads.wait()
    for i in range(4):
        store_rows(normed_one, token_grad_hbm, i, 2 + i).wait()


def closing_kernel(
    layer_hbm,
    token_grad_hbm,
    sums_hbm,
    hidden_sum_hbm,
    rows_grad_hbm,
    small_ref,
    layer_out,
    token_out,
    gain_one_out,
    query_out,
    key_out,
    value_out,
    output_out,
    position_out,
    gain_two_out,
    inner_out,
    outer_out,
    loss_out,
    square_out,
    hidden_sum,
    rows_grad,
    hidden_low,
    outer_part,
    rows_part,
    units_part,
    load_sem,
    copy_sem,
    store_sem,
):
    pairs = []
    inner_units = 2048 // WIDE
    for unit in range(inner_units):
        pairs.append((units_part.at[unit], inner_out.at[:, pl.ds(unit * WIDE, WIDE)]))
    places = [(output_out, 0), (output_out, 256)]
    places += [(ref, g * 256) for g in range(2) for ref in (query_out, key_out, value_out)]
    for part, (ref, lane) in enumerate(places):
        for i in range(PER_PART):
            lanes = pl.ds(lane + i * WIDE, WIDE)
            pairs.append((units_part.at[inner_units + part * PER_PART + i], ref.at[:, lanes]))
    pairs += [(rows_part.at[0], layer_out), (rows_part.at[1], token_out)]
    copies = [
        pltpu.make_async_copy(source, target, copy_sem.at[i])
        for i, (source, target) in enumerate(pairs)
    ]
    pairs = [(rows_grad_hbm, rows_grad), (hidden_sum_hbm, hidden_sum)]
    pairs += [(sums_hbm.at[unit], units_part.at[unit]) for unit in range(UNITS)]
    pairs += [(layer_hbm, rows_part.at[0]), (token_grad_hbm, rows_part.at[1])]
    loads = [
        pltpu.make_async_copy(source, target, load_sem.at[i])
        for i, (source, target) in enumerate(pairs)
    ]
    for load in loads:
        load.start()
    gain_one_out[...] = small_ref[0, :]
    gain_two_out[...] = small_ref[1, :]
    position_out[...] = small_ref[8:16, 0:32]
    loss_out[0] = jnp.max(small_ref[6:7, :])
    squares = jnp.sum(small_ref[2:5, :], axis=1, keepdims=True)
    valid = jnp.sum(small_ref[5:6, :], axis=1, keepdims=True)
    roots = jnp.sqrt(squares / valid)
    for i in range(3):
        square_out[i] = jnp.max(roots[i : i + 1, :])
    loads[0].wait()
    loads[1].wait()
    hidden_low[...] = hidden_sum[...].reshape(512, 2048).astype(BF)
    grads = rows_grad[...].reshape(512, 512)
    stores = []
    for c in range(4):
        rows = pl.ds(c * 512, 512)
        outer_part[rows] = dot(hidden_low[:, c * 512 : (c + 1) * 512], grads, TN)
        store = pltpu.make_async_copy(outer_part.at[rows], outer_out.at[rows], store_sem.at[c])
        store.start()
        stores.append(store)
        for i in range(UNITS // 4 * c, UNITS // 4 * (c + 1)):
            loads[2 + i].wait()
            copies[i].start()
    for i in (UNITS, UNITS + 1):
        loads[2 + i].wait()
        copies[i].start()
    for copy in copies + stores:
        copy.wait()


def fast_shards(
    tokens,
    segment_ids,
    positives,
    attention_gain,
    query_weight,
    key_weight,
    value_weight,
    output_weight,
    position_table,
    feedforward_gain,
    inner_weight,
    outer_weight,
):
    block_shape = tokens.shape
    anywhere = pl.BlockSpec(memory_space=pl.ANY)
    vmem = pl.BlockSpec(memory_space=pltpu.VMEM)
    smem = pl.BlockSpec(memory_space=pltpu.SMEM)
    shape = jax.ShapeDtypeStruct
    dma = pltpu.SemaphoreType.DMA
    low = functools.partial(pltpu.VMEM, dtype=BF)
    full = functools.partial(pltpu.VMEM, dtype=F32)
    outs = pl.pallas_call(
        layer_kernel,
        out_shape=[
            shape((1024, 512), BF),
            shape((1024, 512), BF),
            shape((UNITS, 512, WIDE), F32),
            shape((2, 2, 4, 2, 2, 8, 2048), F32),
            shape((2, 2, 128, 512), BF),
            shape((16, 512), F32),
        ],
        in_specs=[anywhere, vmem, smem, vmem]
        + [anywhere] * 4
        + [vmem, vmem, anywhere, anywhere],
        out_specs=[anywhere] * 5 + [vmem],
        scratch_shapes=[
            low((1024, 512)),
            low((512, 512)),
            low((512, 512)),
            low((512, 512)),
            low((512, 512)),
            low((512, 2048)),
            low((2048, 512)),
            low((1024, 512)),
            low((1024, 512)),
            low((1024, 512)),
            low((1024, 512)),
            low((2, 2, 2, 512, 384)),
            low((2, 2, 2, 512, 256)),
            low((1024, 512)),
            full((1024, 512)),
            low((1024, 512)),
            low((1024, 2048)),
            full((8, 128, NEAR)),
            full((1024, 128)),
            full((2, 512)),
            full((2, 2, 4, 4, 8, 640)),
            full((2, 8, 2048)),
            low((512, 1024)),
            low((512, 1024)),
            low((512, 1024)),
            low((1024, 512)),
            low((1024, 512)),
            low((1024, 512)),
            low((1024, 512)),
            full((1024, 256)),
            full((1024, 256)),
            full((UNITS, 512, WIDE)),
            full((UNITS, 496, WIDE)),
            low((1024, 128)),
            low((2, 2, 128, 512)),
            full((5, 16, 512)),
            dma((7,)),
            dma((7,)),
            dma((12, UNITS)),
            dma((12, UNITS)),
            dma((UNITS,)),
            dma((2, 7)),
            dma((2, 7)),
            dma((2, 8)),
            dma((2, 8)),
            dma((5,)),
            dma((5,)),
            dma((4, 3)),
            dma((4, 3)),
        ],
        compiler_params=pltpu.CompilerParams(
            collective_id=0, has_side_effects=True, vmem_limit_bytes=63 * 2**20
        ),
    )(
        tokens.reshape(1024, 512),
        segment_ids.reshape(2, 512),
        positives,
        attention_gain.reshape(1, 512),
        query_weight,
        key_weight,
        value_weight,
        output_weight,
        position_table.T,
        feedforward_gain.reshape(1, 512),
        inner_weight,
        outer_weight,
    )
    results = pl.pallas_call(
        closing_kernel,
        out_shape=[
            shape((1024, 512), BF),
            shape((1024, 512), BF),
            shape((512,), F32),
            shape((512, 512), F32),
            shape((512, 512), F32),
            shape((512, 512), F32),
            shape((512, 512), F32),
            shape((8, 32), F32),
            shape((512,), F32),
            shape((512, 2048), F32),
            shape((2048, 512), F32),
            shape((1,), F32),
            shape((3,), F32),
        ],
        in_specs=[anywhere] * 5 + [vmem],
        out_specs=[anywhere, anywhere, vmem]
        + [anywhere] * 4
        + [vmem, vmem, anywhere, anywhere, smem, smem],
        scratch_shapes=[
            full((2, 2, 4, 2, 2, 8, 2048)),
            low((2, 2, 128, 512)),
            low((512, 2048)),
            full((2048, 512)),
            low((2, 1024, 512)),
            full((UNITS, 512, WIDE)),
            dma((UNITS + 4,)),
            dma((UNITS + 2,)),
            dma((4,)),
        ],
        compiler_params=pltpu.CompilerParams(vmem_limit_bytes=60 * 2**20),
    )(*outs)
    layer, token_grad, *rest = results
    return (
        layer.reshape(block_shape),
        token_grad.reshape(block_shape),
        *rest[:5],
        rest[5].T,
        *rest[6:9],
        rest[9].reshape(()),
        rest[10],
    )


def solution(mesh):
    fast = mesh.shape["tower"] == 2 and mesh.shape["rows"] == 16
    return jax.shard_map(
        fast_shards if fast else shards,
        mesh=mesh,
        in_specs=(
            P("tower", "rows", None, None),
            P("tower", "rows", None),
            P("rows"),
            P(),
            P(),
            P(),
            P(),
            P(),
            P(),
            P(),
            P(),
            P(),
        ),
        out_specs=(
            P("tower", "rows", None, None),
            P("tower", "rows", None, None),
            P(),
            P(),
            P(),
            P(),
            P(),
            P(),
            P(),
            P(),
            P(),
            P(),
            P(),
        ),
        check_vma=False,
    )
```

```python
import functools
import math

import jax
import jax.numpy as jnp
import numpy as np
from jax import lax
from jax.experimental import pallas as pl
from jax.experimental.pallas import tpu as pltpu
from jax.sharding import PartitionSpec as P

MAX_DIST = 128
ITEMS_ROW = 8


EPSILON = 1e-06
SOFTMAX_TEMP = 0.01
LOSS_SCALE = 65536.0
MATMUL_PRECISION = lax.Precision.HIGHEST


def from_partner(value, axis, apart):
    mask = 2**apart
    pairs = [(source, source ^ mask) for source in range(lax.axis_size(axis))]
    return lax.ppermute(value, axis, pairs)


def bucket_table(length, bucket_count, far_limit):
    half_count = bucket_count // 2
    exact_count = half_count // 2
    entries = []
    for offset in range(1 - length, length):
        distance = abs(offset)
        if distance < exact_count:
            within = distance
        else:
            within = exact_count + int(
                math.log(distance / exact_count)
                / math.log(far_limit / exact_count)
                * (half_count - exact_count)
            )
            within = min(within, half_count - 1)
        entries.append(within + (half_count if offset > 0 else 0))
    by_offset = np.array(entries, dtype=np.int32)
    index_grid = np.arange(length)[None, :] - np.arange(length)[:, None] + length - 1
    return (by_offset, by_offset[index_grid])


def contract_rows(left_side, right_side):
    return lax.dot_general(
        left_side, right_side, (((0,), (0,)), ((), ())), preferred_element_type=jnp.float32
    )


def times_transpose(left_side, right_side):
    return lax.dot_general(
        left_side, right_side, (((1,), (1,)), ((), ())), preferred_element_type=jnp.float32
    )


def norm_scale(values):
    return lax.rsqrt(jnp.mean(values * values, axis=1, keepdims=True) + EPSILON)


def norm_back(grad_normed, values, scale, gain):
    gained = grad_normed * gain
    return scale * (
        gained - values * scale * scale * jnp.mean(gained * values, axis=1, keepdims=True)
    )


def row_scores(query_part, key_part, segment_row, position_bias, head_count):
    length = query_part.shape[0]
    query_heads = query_part.reshape(length, head_count, -1)
    key_heads = key_part.reshape(length, head_count, -1)
    scores = (
        jnp.einsum("qhd,khd->hqk", query_heads, key_heads, preferred_element_type=jnp.float32)
        + position_bias
    )
    same_item = segment_row[:, None] == segment_row[None, :]
    return jnp.where(same_item[None], scores, -1e30)


def diagonal_sums(square):
    head_count = square.shape[0]
    length = square.shape[1]
    flipped = square[:, :, ::-1]
    padded = jnp.pad(flipped, ((0, 0), (0, 0), (0, length)))
    sheared = padded.reshape(head_count, 2 * length * length)[:, : length * (2 * length - 1)]
    sheared = sheared.reshape(head_count, length, 2 * length - 1)
    return jnp.sum(sheared, axis=1)[:, ::-1]


def shards(
    tokens,
    segment_ids,
    positives,
    attention_gain,
    query_weight,
    key_weight,
    value_weight,
    output_weight,
    position_table,
    feedforward_gain,
    inner_weight,
    outer_weight,
):
    row_count = tokens.shape[1]
    length = tokens.shape[2]
    model_width = tokens.shape[3]
    head_count = position_table.shape[1]
    inner_width = query_weight.shape[1]
    head_size = inner_width // head_count
    token_count = row_count * length
    by_offset, bucket_index = bucket_table(length, position_table.shape[0], MAX_DIST)
    position_bias = jnp.take(position_table.T, jnp.asarray(bucket_index), axis=1)
    inputs = tokens.reshape(token_count, model_width).astype(jnp.float32)
    segments = segment_ids.reshape(row_count, length)
    scale_one = norm_scale(inputs)
    normed_one = (inputs * scale_one * attention_gain).astype(jnp.bfloat16)
    query_rows = jnp.dot(normed_one, query_weight, preferred_element_type=jnp.float32).astype(
        jnp.bfloat16
    )
    key_rows = jnp.dot(normed_one, key_weight, preferred_element_type=jnp.float32).astype(
        jnp.bfloat16
    )
    value_rows = jnp.dot(normed_one, value_weight, preferred_element_type=jnp.float32).astype(
        jnp.bfloat16
    )
    query_blocks = query_rows.reshape(row_count, length, inner_width)
    key_blocks = key_rows.reshape(row_count, length, inner_width)
    value_blocks = value_rows.reshape(row_count, length, inner_width)

    def attend(packed):
        query_part, key_part, value_part, segment_row = packed
        scores = row_scores(query_part, key_part, segment_row, position_bias, head_count)
        highest = jnp.max(scores, axis=2, keepdims=True)
        exp_scores = jnp.exp(scores - highest)
        exp_total = jnp.sum(exp_scores, axis=2, keepdims=True)
        attention_probs = (exp_scores / exp_total).astype(jnp.bfloat16)
        value_heads = value_part.reshape(length, head_count, head_size)
        mixed_heads = jnp.einsum(
            "hqk,khd->qhd", attention_probs, value_heads, preferred_element_type=jnp.float32
        )
        return (
            mixed_heads.reshape(length, inner_width).astype(jnp.bfloat16),
            (highest + jnp.log(exp_total))[:, :, 0],
        )

    mixed_blocks, log_totals = lax.map(attend, (query_blocks, key_blocks, value_blocks, segments))
    mixed_rows = mixed_blocks.reshape(token_count, inner_width)
    branch_one = jnp.dot(mixed_rows, output_weight, preferred_element_type=jnp.float32)
    middle = inputs + branch_one
    scale_two = norm_scale(middle)
    normed_two = (middle * scale_two * feedforward_gain).astype(jnp.bfloat16)
    hidden = jax.nn.relu(
        jnp.dot(normed_two, inner_weight, preferred_element_type=jnp.float32)
    ).astype(jnp.bfloat16)
    branch_two = jnp.dot(hidden, outer_weight, preferred_element_type=jnp.float32)
    result = middle + branch_two
    valid_mask = (segments < ITEMS_ROW).astype(jnp.float32).reshape(token_count, 1)
    stat_terms = jnp.stack(
        [
            jnp.sum(valid_mask * result * result),
            jnp.sum(valid_mask * branch_one * branch_one),
            jnp.sum(valid_mask * branch_two * branch_two),
            jnp.sum(valid_mask),
        ]
    )
    stat_totals = lax.psum(stat_terms, ("tower", "rows"))
    member = (segments[:, None, :] == jnp.arange(ITEMS_ROW)[None, :, None]).astype(jnp.float32)
    item_sizes = jnp.sum(member, axis=2, keepdims=True)
    result_blocks = result.reshape(row_count, length, model_width)
    pooled = (
        jnp.einsum("ris,rsd->rid", member, result_blocks, precision=MATMUL_PRECISION) / item_sizes
    )
    items_here = row_count * ITEMS_ROW
    pooled = pooled.reshape(items_here, model_width)
    inverse_norm = lax.rsqrt(jnp.sum(pooled * pooled, axis=1, keepdims=True) + EPSILON)
    embedded_tokens = pooled * inverse_norm
    tower_index = lax.axis_index("tower")
    is_query = tower_index == 0
    partner = from_partner(embedded_tokens, "tower", 0)
    query_vectors = jnp.where(is_query, embedded_tokens, partner)
    document_vectors = jnp.where(is_query, partner, embedded_tokens)
    gathered_documents = lax.all_gather(document_vectors, "rows", axis=0, tiled=True)
    item_total = gathered_documents.shape[0]
    half_items = items_here // 2
    my_queries = lax.dynamic_slice_in_dim(query_vectors, tower_index * half_items, half_items, 0)
    my_targets = lax.dynamic_slice_in_dim(positives, tower_index * half_items, half_items, 0)
    similarity_scores = (
        lax.dot_general(
            my_queries,
            gathered_documents,
            (((1,), (1,)), ((), ())),
            precision=MATMUL_PRECISION,
            preferred_element_type=jnp.float32,
        )
        / SOFTMAX_TEMP
    )
    highest = jnp.max(similarity_scores, axis=1, keepdims=True)
    exp_logits = jnp.exp(similarity_scores - highest)
    exp_total = jnp.sum(exp_logits, axis=1, keepdims=True)
    log_total = highest[:, 0] + jnp.log(exp_total[:, 0])
    is_target = jnp.arange(item_total)[None, :] == my_targets[:, None]
    target = jnp.sum(jnp.where(is_target, similarity_scores, 0.0), axis=1)
    loss_part = jnp.sum(log_total - target)
    similarity_gradient = (exp_logits / exp_total - is_target.astype(jnp.float32)) * (
        LOSS_SCALE / item_total
    )
    local_gradient = (
        jnp.dot(similarity_gradient, gathered_documents, precision=MATMUL_PRECISION) / SOFTMAX_TEMP
    )
    grad_documents = lax.psum_scatter(
        lax.dot_general(
            similarity_gradient,
            my_queries,
            (((0,), (0,)), ((), ())),
            precision=MATMUL_PRECISION,
            preferred_element_type=jnp.float32,
        )
        / SOFTMAX_TEMP,
        "rows",
        scatter_dimension=0,
        tiled=True,
    )
    partner_mine, partner_documents = from_partner((local_gradient, grad_documents), "tower", 0)
    query_side = jnp.where(
        is_query,
        jnp.concatenate([local_gradient, partner_mine], 0),
        jnp.concatenate([partner_mine, local_gradient], 0),
    )
    own_grad = jnp.where(is_query, query_side, grad_documents + partner_documents)
    inner_along = jnp.sum(own_grad * embedded_tokens, axis=1, keepdims=True)
    grad_pooled = inverse_norm * (own_grad - embedded_tokens * inner_along)
    per_token = grad_pooled.reshape(row_count, ITEMS_ROW, model_width) / item_sizes
    grad_result = jnp.einsum("ris,rid->rsd", member, per_token, precision=MATMUL_PRECISION).reshape(
        token_count, model_width
    )
    grad_branch_two = grad_result.astype(jnp.bfloat16)
    outer_grad = contract_rows(hidden, grad_branch_two)
    grad_hidden = times_transpose(grad_branch_two, outer_weight)
    grad_pre = jnp.where(hidden > 0, grad_hidden, 0.0).astype(jnp.bfloat16)
    inner_grad = contract_rows(normed_two, grad_pre)
    grad_normed_two = times_transpose(grad_pre, inner_weight)
    feedforward_gain_grad = jnp.sum(grad_normed_two * middle * scale_two, axis=0)
    grad_middle = grad_result + norm_back(grad_normed_two, middle, scale_two, feedforward_gain)
    grad_branch_one = grad_middle.astype(jnp.bfloat16)
    output_grad = contract_rows(mixed_rows, grad_branch_one)
    grad_mixed = times_transpose(grad_branch_one, output_weight).astype(jnp.bfloat16)
    grad_mixed_blocks = grad_mixed.reshape(row_count, length, inner_width)

    def attend_back(running, packed):
        query_part, key_part, value_part, segment_row, row_log_total, grad_part = packed
        scores = row_scores(query_part, key_part, segment_row, position_bias, head_count)
        attention_probs = jnp.exp(scores - row_log_total[:, :, None])
        query_heads = query_part.reshape(length, head_count, head_size)
        key_heads = key_part.reshape(length, head_count, head_size)
        value_heads = value_part.reshape(length, head_count, head_size)
        grad_heads = grad_part.reshape(length, head_count, head_size)
        grad_value = jnp.einsum(
            "hqk,qhd->khd",
            attention_probs.astype(jnp.bfloat16),
            grad_heads,
            preferred_element_type=jnp.float32,
        )
        grad_probs = jnp.einsum(
            "qhd,khd->hqk", grad_heads, value_heads, preferred_element_type=jnp.float32
        )
        row_dot = jnp.sum(attention_probs * grad_probs, axis=2, keepdims=True)
        grad_scores = (attention_probs * (grad_probs - row_dot)).astype(jnp.bfloat16)
        grad_query = jnp.einsum(
            "hqk,khd->qhd", grad_scores, key_heads, preferred_element_type=jnp.float32
        )
        grad_key = jnp.einsum(
            "hqk,qhd->khd", grad_scores, query_heads, preferred_element_type=jnp.float32
        )
        outputs = (
            grad_query.reshape(length, inner_width).astype(jnp.bfloat16),
            grad_key.reshape(length, inner_width).astype(jnp.bfloat16),
            grad_value.reshape(length, inner_width).astype(jnp.bfloat16),
        )
        return (running + grad_scores.astype(jnp.float32), outputs)

    score_sum, grad_rows = lax.scan(
        attend_back,
        jnp.zeros((head_count, length, length), jnp.float32),
        (query_blocks, key_blocks, value_blocks, segments, log_totals, grad_mixed_blocks),
    )
    grad_queries = grad_rows[0].reshape(token_count, inner_width)
    grad_keys = grad_rows[1].reshape(token_count, inner_width)
    grad_values = grad_rows[2].reshape(token_count, inner_width)
    query_grad = contract_rows(normed_one, grad_queries)
    key_grad = contract_rows(normed_one, grad_keys)
    value_grad = contract_rows(normed_one, grad_values)
    grad_normed_one = (
        times_transpose(grad_queries, query_weight)
        + times_transpose(grad_keys, key_weight)
        + times_transpose(grad_values, value_weight)
    )
    attention_gain_grad = jnp.sum(grad_normed_one * inputs * scale_one, axis=0)
    token_grad = grad_middle + norm_back(grad_normed_one, inputs, scale_one, attention_gain)
    offset_onehot = jnp.asarray(
        (by_offset[:, None] == np.arange(position_table.shape[0])[None, :]).astype(np.float32)
    )
    position_grad = jnp.dot(diagonal_sums(score_sum), offset_onehot, precision=MATMUL_PRECISION).T
    closing_terms = loss_part[None]
    summed = lax.psum(
        (
            attention_gain_grad,
            query_grad,
            key_grad,
            value_grad,
            output_grad,
            position_grad,
            feedforward_gain_grad,
            inner_grad,
            outer_grad,
            closing_terms,
        ),
        ("tower", "rows"),
    )
    (
        attention_gain_grad,
        query_grad,
        key_grad,
        value_grad,
        output_grad,
        position_grad,
        feedforward_gain_grad,
        inner_grad,
        outer_grad,
        closing_totals,
    ) = summed
    contrastive_loss = closing_totals[0] / item_total
    root_mean_squares = jnp.sqrt(stat_totals[:3] / (stat_totals[3] * model_width))
    block_shape = (1, row_count, length, model_width)
    return (
        result.reshape(block_shape).astype(jnp.bfloat16),
        token_grad.reshape(block_shape).astype(jnp.bfloat16),
        attention_gain_grad,
        query_grad,
        key_grad,
        value_grad,
        output_grad,
        position_grad,
        feedforward_gain_grad,
        inner_grad,
        outer_grad,
        contrastive_loss,
        root_mean_squares,
    )


F32 = jnp.float32
BF = jnp.bfloat16
MESH = pl.DeviceIdType.MESH
NN = (((1,), (0,)), ((), ()))
NT = (((1,), (1,)), ((), ()))
TN = (((0,), (0,)), ((), ()))
WIDE = 128
UNITS = 4096 // WIDE
PER_PART = 256 // WIDE
STEPS_AFTER = (
    (),
    (0, 1, 2, 3,),
    (4, 5, 6, 7,),
    (8, 9, 10, 11, 0, 1,),
    (12, 13, 2, 3, 14, 15,),
    (),
    (0, 1, 4, 5,),
    (2, 3, 6, 7,),
    (8, 9,),
    (4, 5, 10, 11, 16, 17, 18, 19,),
    (6, 7, 12, 13, 8, 14, 15,),
    (0, 1, 2, 3, 9, 10,),
    (11, 12,),
    (13,),
    (14,),
    (20, 15, 21,),
    (0, 1, 2, 3, 4, 5, 22, 23, 24, 25,),
    (16, 17,),
    (0, 6, 1, 7, 8, 9, 10, 11, 2, 18, 13, 12, 19,),
    (3, 4, 5, 14, 15, 16, 17, 20, 21,),
    (),
    (6, 7, 22, 23, 8,),
    (9, 18, 10, 26, 27, 28,),
    (0, 1, 2, 3, 4, 11, 12, 13, 16, 17, 5, 19, 24, 25, 29, 30, 14, 31,),
    (6, 7, 15, 18, 20, 8, 21, 22, 23,),
    (0, 9, 10, 26, 27,),
    (1, 2, 4, 5, 24, 28,),
    (3, 11, 12, 13, 14, 15, 16, 17, 18, 19, 25, 29, 30, 7, 6, 20, 31, 32, 8, 21, 10, 22, 0, 26, 23, 4, 9, 5, 27, 0, 1, 16, 24, 28, 17, 2, 18, 1, 19, 11, 13, 25, 7, 15, 2, 3, 12, 6, 29, 14, 3, 31, 30, 20, 8, 32, 5, 21, 10, 16, 4, 18, 17, 5, 22, 4, 26, 7, 6, 23, 9, 20, 7, 32, 6, 27, 8, 24, 22, 21, 19, 28, 8, 11, 13, 10, 9, 23, 25, 15, 10, 24, 9, 12, 20, 21, 29, 14, 20, 22, 19, 21, 31, 11, 25, 30, 22, 16, 11, 18, 13, 24, 17, 13, 23, 24, 32, 26, 12, 23, 15, 27, 12, 14, 28, 29, 15, 19, 25, 14, 16, 32, 31, 25, 17, 30, 16, 18, 26, 27, 17, 28, 18, 29, 31, 19, 30, 19, 26, 27, 26, 28, 27, 29, 28, 30, 29, 31, 30, 31,),
)
SMALL = UNITS
PIECES = len(STEPS_AFTER)
FAR = 512
NEAR = 384
WINDOWS = ((0, 256, 128), (0, 384, 0), (128, 384, 0), (256, 256, 0))


def dot(a, b, dims=NN):
    return lax.dot_general(a, b, dims, preferred_element_type=F32)


def exact_dot(a, b, dims=NN):
    return lax.dot_general(
        a, b, dims, precision=lax.Precision.HIGHEST, preferred_element_type=F32
    )


def tile(index, size):
    if isinstance(index, int):
        return pl.ds(index * size, size)
    return pl.ds(pl.multiple_of(index * size, size), size)


def far_limits(bucket_count, far_limit):
    half_count = bucket_count // 2
    exact_count = half_count // 2
    limits = []
    reached = exact_count
    for distance in range(exact_count, 512):
        within = exact_count + int(
            math.log(distance / exact_count)
            / math.log(far_limit / exact_count)
            * (half_count - exact_count)
        )
        within = min(within, half_count - 1)
        while reached < within:
            limits.append(distance)
            reached += 1
    return limits


def bucket_onehot(offset):
    distance = jnp.abs(offset)
    far = jnp.full_like(distance, 8)
    for limit in far_limits(32, MAX_DIST):
        far = far + jnp.where(distance >= limit, 1, 0)
    bucket = jnp.where(distance < 8, distance, far) + jnp.where(offset > 0, 16, 0)
    same = bucket == lax.broadcasted_iota(jnp.int32, (32, FAR), 0)
    return jnp.where(same, 1.0, 0.0).astype(F32)


def split_three(value):
    high = value.astype(BF)
    rest = value - high.astype(F32)
    middle = rest.astype(BF)
    return high, middle, (rest - middle.astype(F32)).astype(BF)


class Place:
    def __init__(self):
        self.tower = lax.axis_index("tower")
        self.rows = lax.axis_index("rows")
        self.flat = lax.rem(self.rows, 4)
        self.deep = lax.div(self.rows, 4)
        bits = {
            "x": lax.rem(self.rows, 2),
            "y": lax.rem(lax.div(self.rows, 2), 2),
            "z": lax.rem(lax.div(self.rows, 4), 2),
            "w": lax.div(self.rows, 8),
        }
        steps = {"x": 1, "y": 2, "z": 4, "w": 8}
        self.bit = {"c": self.tower, **bits}
        self.to = {"c": self.device(1 - self.tower, self.rows)}
        for name, step in steps.items():
            self.to[name] = self.device(self.tower, self.rows + step * (1 - 2 * bits[name]))

    def device(self, tower, rows):
        return {"tower": tower, "rows": rows}

    def along_deep(self, step):
        return self.device(self.tower, lax.rem(self.deep + step, 4) * 4 + self.flat)

    def along_flat(self, step):
        return self.device(self.tower, self.deep * 4 + lax.rem(self.flat + step, 4))


def order_of(unit):
    return (("cxzyw", "cyzxw") if 8 * unit < 5 * UNITS else ("cxyZ", "cyxZ"))[unit % 2]


class Sums:
    def __init__(self, place, total, landed, out, small, small_landed, sems):
        self.place, self.total, self.landed, self.out = place, total, landed, out
        self.small, self.small_landed = small, small_landed
        self.send_sem, self.recv_sem, self.out_sem, self.small_send, self.small_recv = sems
        self.plans = {}
        self.stage = {}
        for unit in range(UNITS):
            order = order_of(unit)
            if order not in self.plans:
                self.plans[order] = self.plan(order)

    def plan(self, order):
        place, steps = self.place, []
        base, size, offset, sem = 0, 512, 0, 0
        for name in order:
            ways = 4 if name == "Z" else 2
            size //= ways
            spot = place.deep if name == "Z" else place.bit[name]
            partners = []
            for i in range(1, ways):
                if name == "Z":
                    piece, device = lax.rem(place.deep + i, 4), place.along_deep(i)
                else:
                    piece, device = 1 - spot, place.to[name]
                partners.append((base + piece * size, device, offset, sem))
                offset, sem = offset + size, sem + 1
            base = base + spot * size
            steps.append((size, base, partners))
        return steps

    def remote(self, source, target, index, unit, device):
        return pltpu.make_async_remote_copy(
            src_ref=source,
            dst_ref=target,
            send_sem=self.send_sem.at[index, unit],
            recv_sem=self.recv_sem.at[index, unit],
            device_id=device,
            device_id_type=MESH,
        )

    def depth(self, unit):
        return 5 if unit == SMALL else 2 * len(order_of(unit))

    def rows(self, start, size):
        return pl.ds(pl.multiple_of(start, size), size)

    def keep(self, unit):
        size, base, _ = self.plans[order_of(unit)][-1]
        rows = self.rows(base, size)
        return pltpu.make_async_copy(
            self.total.at[unit, rows], self.out.at[unit, rows], self.out_sem.at[unit]
        )

    def copies(self, stage, unit):
        if unit == SMALL:
            return [
                pltpu.make_async_remote_copy(
                    src_ref=self.small,
                    dst_ref=self.small_landed.at[stage],
                    send_sem=self.small_send.at[stage],
                    recv_sem=self.small_recv.at[stage],
                    device_id=self.place.to["cxyzw"[stage]],
                    device_id_type=MESH,
                )
            ]
        plan = self.plans[order_of(unit)]
        if stage < len(plan):
            size, _, partners = plan[stage]
            return [
                self.remote(
                    self.total.at[unit, self.rows(start, size)],
                    self.landed.at[unit, pl.ds(offset, size)],
                    sem,
                    unit,
                    device,
                )
                for start, device, offset, sem in partners
            ]
        back = 2 * len(plan) - 1 - stage
        size, base, partners = plan[back]
        rows = self.rows(base, size)
        source = self.total if stage == len(plan) else self.out
        return [
            self.remote(source.at[unit, rows], self.out.at[unit, rows], 6 + sem, unit, device)
            for _, device, _, sem in partners
        ]

    def step(self, unit):
        stage = self.stage.get(unit, -1)
        plan = None if unit == SMALL else self.plans[order_of(unit)]
        if stage >= 0:
            for copy in self.copies(stage, unit):
                copy.wait()
            if unit == SMALL:
                self.small[...] += self.small_landed[stage]
            elif stage < len(plan):
                size, base, partners = plan[stage]
                parts = [self.landed[unit, pl.ds(p[2], size), :] for p in partners]
                self.total[unit, self.rows(base, size), :] += sum(parts[1:], parts[0])
            elif stage == len(plan):
                self.keep(unit).wait()
        stage += 1
        self.stage[unit] = stage
        if stage < self.depth(unit):
            for copy in self.copies(stage, unit):
                copy.start()
            if plan is not None and stage == len(plan):
                self.keep(unit).start()

    def fill(self, part, value):
        for i in range(PER_PART):
            self.total[part * PER_PART + i] = value[:, i * WIDE : (i + 1) * WIDE]

    def after(self, piece, *parts):
        for part in parts:
            for i in range(PER_PART):
                self.step(part * PER_PART + i)
        if piece == PIECES - 1:
            self.step(SMALL)
        for unit in STEPS_AFTER[piece]:
            self.step(unit)


class Spread:
    def __init__(self, place, blocks, send_sem, recv_sem):
        self.place, self.blocks = place, blocks
        self.send_sem, self.recv_sem = send_sem, recv_sem

    def copy(self, row, index, where, device):
        ref = self.blocks.at[where]
        return pltpu.make_async_remote_copy(
            src_ref=ref,
            dst_ref=ref,
            send_sem=self.send_sem.at[row, index],
            recv_sem=self.recv_sem.at[row, index],
            device_id=device,
            device_id_type=MESH,
        )

    def one(self, row, i):
        place = self.place
        where = (row, place.tower, place.deep, place.flat)
        return self.copy(row, i, where, place.along_deep(i + 1))

    def copies(self, row, stage):
        place = self.place
        if stage == 0:
            return [self.one(row, i) for i in range(3)]
        if stage == 1:
            where = (row, place.tower, slice(None), place.flat)
            return [self.copy(row, 3 + i, where, place.along_flat(i + 1)) for i in range(3)]
        return [self.copy(row, 6, (row, place.tower), place.to["c"])]

    def start(self, row, stage):
        for copy in self.copies(row, stage):
            copy.start()

    def wait(self, row, stage):
        for copy in self.copies(row, stage):
            copy.wait()


def layer_kernel(
    tokens_hbm,
    segment_ref,
    positive_ref,
    gain_one_ref,
    query_hbm,
    key_hbm,
    value_hbm,
    output_hbm,
    table_ref,
    gain_two_ref,
    inner_hbm,
    outer_hbm,
    layer_hbm,
    token_grad_hbm,
    sums_hbm,
    hidden_sum_hbm,
    rows_grad_hbm,
    small_ref,
    tokens,
    query_w,
    key_w,
    value_w,
    output_w,
    inner_w,
    outer_w,
    normed_one,
    queries,
    keys,
    values,
    probs,
    side_probs,
    mixed,
    middle,
    normed_two,
    hidden,
    bias,
    segment_column,
    segment_row,
    pooled_all,
    hidden_sum,
    normed_one_t,
    normed_two_t,
    mixed_t,
    grad_mixed,
    grad_query,
    grad_key,
    grad_value,
    key_total,
    value_total,
    total,
    landed,
    expand,
    rounded_grads,
    small_landed,
    load_sem,
    store_sem,
    sum_send,
    sum_recv,
    sum_out,
    pool_send,
    pool_recv,
    hidden_send,
    hidden_recv,
    small_send,
    small_recv,
    relay_send,
    relay_recv,
):
    place = Place()
    barrier = pltpu.get_barrier_semaphore()
    partners = [place.to["c"]]
    partners += [place.along_deep(i) for i in (1, 2, 3)]
    partners += [place.along_flat(i) for i in (1, 2, 3)]
    for partner in partners:
        pl.semaphore_signal(barrier, inc=1, device_id=partner, device_id_type=MESH)

    loads = [
        pltpu.make_async_copy(source, target, load_sem.at[i])
        for i, (source, target) in enumerate(
            (
                (tokens_hbm, tokens),
                (query_hbm, query_w),
                (key_hbm, key_w),
                (value_hbm, value_w),
                (output_hbm, output_w),
                (inner_hbm, inner_w),
                (outer_hbm, outer_w),
            )
        )
    ]
    for load in loads:
        load.start()

    segment_row[...] = segment_ref[...].astype(F32)
    for i in range(8):
        row = segment_row[i // 4 : i // 4 + 1, (i % 4) * 128 : (i % 4) * 128 + 128]
        segment_column[i * 128 : (i + 1) * 128, :] = jnp.broadcast_to(row, (128, 128)).T
    place_row = lax.broadcasted_iota(jnp.int32, (32, FAR), 1)
    offsets = jnp.where(place_row >= NEAR, place_row - FAR, place_row) - 128
    by_place = exact_dot(table_ref[...], bucket_onehot(offsets))
    for h in range(8):
        spread = jnp.broadcast_to(by_place[h : h + 1], (128, FAR))
        bias[h] = pltpu.roll(spread, 0, 1, stride=1, stride_axis=0)[:, :NEAR]
    pooling = Spread(place, pooled_all, pool_send, pool_recv)
    sums = Sums(
        place,
        total,
        landed,
        sums_hbm,
        small_ref,
        small_landed,
        (sum_send, sum_recv, sum_out, small_send, small_recv),
    )

    def hidden_slot(row):
        return hidden_sum_hbm.at[row, place.tower, place.deep, place.bit["y"], place.bit["x"]]

    def save_hidden(row):
        return pltpu.make_async_copy(hidden_sum.at[row], hidden_slot(row), store_sem.at[row])

    def hidden_copy(source, target, row, index, device):
        return pltpu.make_async_remote_copy(
            src_ref=source,
            dst_ref=target,
            send_sem=hidden_send.at[row, index],
            recv_sem=hidden_recv.at[row, index],
            device_id=device,
            device_id_type=MESH,
        )

    def go(copies, start):
        for copy in copies:
            if start:
                copy.start()
            else:
                copy.wait()

    def deepen_hidden(row, start):
        source = hidden_sum.at[row]
        target = hidden_slot(row)
        copies = [
            hidden_copy(source, target, row, i - 1, place.along_deep(i)) for i in (1, 2, 3)
        ]
        go(copies, start)

    def widen_hidden(row, step, start):
        ref = hidden_sum_hbm.at[row, place.tower]
        y, x = place.bit["y"], place.bit["x"]
        left, right = pl.ds(0, 1024), pl.ds(1024, 1024)
        if step == 0:
            parts = (ref.at[:, y, x, :, left], "x"), (ref.at[:, y, x, :, right], "y")
        else:
            parts = (ref.at[:, y, :, :, left], "y"), (ref.at[:, :, x, :, right], "x")
        copies = [
            hidden_copy(part, part, row, 3 + 2 * step + i, place.to[name])
            for i, (part, name) in enumerate(parts)
        ]
        go(copies, start)

    def swap_hidden(row, start):
        ref = hidden_sum_hbm.at[row, place.tower]
        go([hidden_copy(ref, ref, row, 7, place.to["c"])], start)

    def relay(step, start):
        ref = pooled_all.at[1, place.tower, lax.rem(place.deep + 4 - step, 4), place.flat]
        copies = [
            pltpu.make_async_remote_copy(
                src_ref=ref,
                dst_ref=ref,
                send_sem=relay_send.at[step, i - 1],
                recv_sem=relay_recv.at[step, i - 1],
                device_id=place.along_flat(i),
                device_id_type=MESH,
            )
            for i in (1, 2, 3)
        ]
        go(copies, start)

    head_lane = lax.broadcasted_iota(jnp.int32, (1, 256), 1) // 64
    head_mask = [jnp.where(head_lane == h, 1.0, 0.0) for h in range(4)]
    head_mask_low = [mask.astype(BF) for mask in head_mask]

    def stack_heads(part):
        return jnp.concatenate([part * mask for mask in head_mask_low], 0)

    def pick_heads(part):
        return sum(part[h * 128 : (h + 1) * 128] * head_mask[h] for h in range(4))

    def project(i, carry):
        rows = tile(i, 256)
        x = tokens[rows, :].astype(F32)
        scale = lax.rsqrt(jnp.mean(x * x, axis=1, keepdims=True) + EPSILON)
        normed = (x * scale * gain_one_ref[...]).astype(BF)
        normed_one[rows, :] = normed
        queries[rows, :] = dot(normed, query_w[...]).astype(BF)
        keys[rows, :] = dot(normed, key_w[...]).astype(BF)
        values[rows, :] = dot(normed, value_w[...]).astype(BF)
        return carry

    def window(r, b):
        start, width, offset = WINDOWS[b]
        base = r * 512
        own = pl.ds(pl.multiple_of(base + b * 128, 128), 128)
        near = pl.ds(pl.multiple_of(base + start, 128), width)
        return own, near, slice(start, start + width), slice(offset, offset + width)

    def soft(r, b, g):
        if b in (0, 3):
            return side_probs.at[r, b // 3, g]
        return probs.at[r, b - 1, g]

    def attend(b, r, carry):
        own, near, near_row, offset = window(r, b)
        column = segment_column[own, :]
        row = segment_row[pl.ds(r, 1), near_row]
        same = jnp.concatenate([column] * (WINDOWS[b][1] // 128), 1) == row
        for g in range(2):
            lanes = slice(g * 256, (g + 1) * 256)
            scores = dot(stack_heads(queries[own, lanes]), keys[near, lanes], NT)
            parts = []
            for h in range(4):
                part = scores[h * 128 : (h + 1) * 128] + bias[g * 4 + h, :, offset]
                part = jnp.where(same, part, -1e30)
                highest = jnp.max(part, axis=1, keepdims=True)
                exp_part = jnp.exp(part - highest)
                exp_total = jnp.sum(exp_part, axis=1, keepdims=True)
                parts.append((exp_part * (1.0 / exp_total)).astype(BF))
            stacked = jnp.concatenate(parts, 0)
            soft(r, b, g)[...] = stacked
            mixed[own, lanes] = pick_heads(dot(stacked, values[near, lanes])).astype(BF)
        return carry

    def feed(i, carry):
        rows = tile(i, 256)
        branch = dot(mixed[rows, :], output_w[...])
        mid = tokens[rows, :].astype(F32) + branch
        middle[rows, :] = mid
        scale = lax.rsqrt(jnp.mean(mid * mid, axis=1, keepdims=True) + EPSILON)
        normed = (mid * scale * gain_two_ref[...]).astype(BF)
        normed_two[rows, :] = normed
        for c in range(4):
            lanes = slice(c * 512, (c + 1) * 512)
            hidden[rows, lanes] = jnp.maximum(dot(normed, inner_w[:, lanes]), 0.0).astype(BF)
        return carry

    def pool(r):
        rows = tile(r, 512)
        number = lax.broadcasted_iota(jnp.int32, (8, 512), 0).astype(F32)
        member = jnp.where(segment_row[pl.ds(r, 1), :] == number, 1.0, 0.0)
        member_low = jnp.concatenate([member, jnp.zeros_like(member)], 0).astype(BF)
        count = jnp.sum(member, axis=1, keepdims=True)
        hidden_part = dot(member_low, hidden[rows, :])[:8]
        hidden_sum[r] = hidden_part
        middle_part = sum(dot(member_low, piece) for piece in split_three(middle[rows, :]))[:8]
        pieces = split_three(hidden_part)
        stacked = jnp.concatenate([*pieces, jnp.zeros_like(pieces[0])], 0)
        branch = dot(stacked, outer_w[...])
        pooled = (middle_part + (branch[0:8] + branch[8:16] + branch[16:24])) / count
        sublane = lax.broadcasted_iota(jnp.int32, (8, 128), 0)
        ids = jnp.zeros((8, 128), F32)
        for s in range(8):
            ids = jnp.where(sublane == s, positive_ref[r * 8 + s].astype(F32), ids)
        lanes = lax.broadcasted_iota(jnp.int32, (8, 128), 1)
        extra = jnp.where(lanes == 0, ids, count)
        pooled_all[r, place.tower, place.deep, place.flat] = jnp.concatenate([pooled, extra], 1)

    small_ref[...] = jnp.zeros_like(small_ref)
    in_item = jnp.where(segment_row[...] < ITEMS_ROW, 512.0, 0.0)
    small_ref[5:6, :] = jnp.sum(in_item, axis=0, keepdims=True)
    for i in range(4):
        loads[i].wait()
    pl.semaphore_wait(barrier, len(partners))

    def forward(r, carry):
        first, second = r == 0, r == 1
        lax.fori_loop(2 * r, 2 * r + 2, project, 0)
        attend(0, r, 0)
        attend(1, r, 0)

        attend(2, r, 0)
        attend(3, r, 0)

        @pl.when(first)
        def _():
            for i in (4, 5):
                loads[i].wait()

        @pl.when(second)
        def _():
            pooling.wait(0, 0)
            pooling.start(0, 1)

        lax.fori_loop(2 * r, 2 * r + 2, feed, 0)

        @pl.when(first)
        def _():
            loads[6].wait()

        pool(r)
        pooling.start(r, 0)

        @pl.when(second)
        def _():
            relay(0, start=True)
            save_hidden(0).wait()
            deepen_hidden(0, start=False)
            widen_hidden(0, 0, start=True)

        deepen_hidden(r, start=True)
        save_hidden(r).start()
        return carry

    lax.fori_loop(0, 2, forward, 0)

    def store_rows(source, target, i, index):
        rows = tile(i, 256)
        return pltpu.make_async_copy(source.at[rows], target.at[rows], store_sem.at[index])

    def close(i, carry):
        rows = tile(i, 256)
        branch = dot(hidden[rows, :], outer_w[...])
        mid = middle[rows, :]
        first = mid - tokens[rows, :].astype(F32)
        result = mid + branch
        grad_query[rows, :] = result.astype(BF)
        valid = jnp.where(segment_column[rows, 0:1] < ITEMS_ROW, 1.0, 0.0)
        small_ref[2:3, :] += jnp.sum(valid * result * result, axis=0, keepdims=True)
        small_ref[3:4, :] += jnp.sum(valid * first * first, axis=0, keepdims=True)
        small_ref[4:5, :] += jnp.sum(valid * branch * branch, axis=0, keepdims=True)
        return carry

    def turn(i, carry):
        rows = tile(i, 128)
        normed_two_t[:, rows] = normed_two[rows, :].T
        mixed_t[:, rows] = mixed[rows, :].T
        normed_one_t[:, rows] = normed_one[rows, :].T
        return carry

    lax.fori_loop(0, 3, close, 0)
    for step in (1, 2, 3):
        if step == 3:
            lax.fori_loop(3, 4, close, 0)
        pooling.one(1, step - 1).wait()
        relay(step, start=True)
    pooling.wait(0, 1)
    pooling.start(0, 2)
    for i in range(4):
        store_rows(grad_query, layer_hbm, i, 2 + i).start()
    save_hidden(1).wait()
    lax.fori_loop(0, 8, turn, 0)
    widen_hidden(0, 0, start=False)
    widen_hidden(0, 1, start=True)
    lane = lax.broadcasted_iota(jnp.int32, (1, 128), 1)
    item = segment_column[...] + jnp.where(
        lax.broadcasted_iota(jnp.int32, (1024, 128), 0) >= 512, 8.0, 0.0
    )
    item = jnp.where(segment_column[...] < ITEMS_ROW, item, -1.0)
    slot = jnp.where(lane < 48, lax.rem(lane, 16), -2).astype(F32)
    expand[...] = jnp.where(item == slot, 1.0, 0.0).astype(BF)
    for step in range(4):
        relay(step, start=False)
    pooling.start(1, 2)
    deepen_hidden(1, start=False)
    widen_hidden(1, 0, start=True)
    pooling.wait(0, 2)
    pooling.wait(1, 2)

    gathered = [
        jnp.concatenate([pooled_all[r, t].reshape(128, 640) for r in range(2)], 0)
        for t in range(2)
    ]
    vectors, inverse, counts, embedded = [], [], [], []
    for t in range(2):
        vector = gathered[t][:, :512]
        scale = lax.rsqrt(jnp.sum(vector * vector, axis=1, keepdims=True) + EPSILON)
        vectors.append(vector)
        inverse.append(scale)
        embedded.append(vector * scale)
        counts.append(gathered[t][:, 513:514])
    logits = exact_dot(embedded[0], embedded[1], NT) / SOFTMAX_TEMP
    highest = jnp.max(logits, axis=1, keepdims=True)
    exp_logits = jnp.exp(logits - highest)
    exp_total = jnp.sum(exp_logits, axis=1, keepdims=True)
    position = lax.broadcasted_iota(jnp.int32, (256, 256), 1)
    number = lax.rem(lax.div(position, 8), 16) * 16 + lax.div(position, 128) * 8
    number = (number + lax.rem(position, 8)).astype(F32)
    is_target = gathered[0][:, 512:513] == number
    target = jnp.sum(jnp.where(is_target, logits, 0.0), axis=1, keepdims=True)
    losses = highest + jnp.log(exp_total) - target
    loss = jnp.sum(losses, axis=0, keepdims=True) / 256
    grad_logits = (exp_logits / exp_total - jnp.where(is_target, 1.0, 0.0)) * (LOSS_SCALE / 256)
    grads = (
        exact_dot(grad_logits, embedded[1]) / SOFTMAX_TEMP,
        exact_dot(grad_logits, embedded[0], TN) / SOFTMAX_TEMP,
    )
    for t in range(2):
        along = jnp.sum(grads[t] * embedded[t], axis=1, keepdims=True)
        per_token = inverse[t] * (grads[t] - embedded[t] * along) / counts[t]
        for r in range(2):
            part = per_token[r * 128 : (r + 1) * 128]
            for i in range(512 // WIDE):
                total[UNITS - 4 + 2 * r + t, i * 128 : (i + 1) * 128] = part[
                    :, i * WIDE : (i + 1) * WIDE
                ]
            rounded_grads[r, t] = per_token[r * 128 : (r + 1) * 128].astype(BF)
    save_grads = pltpu.make_async_copy(rounded_grads, rows_grad_hbm, store_sem.at[6])
    save_grads.start()
    own_parts = []
    for r in range(2):
        spot = UNITS - 4 + 2 * r + place.tower
        lanes = [total[spot, tile(place.rows + 16 * i, 8)] for i in range(512 // WIDE)]
        own_parts.append(jnp.concatenate(lanes, 1))
    own = jnp.concatenate(own_parts, 0)
    pieces = split_three(own)
    own_low = pieces[0]
    own_split = jnp.concatenate([*pieces, jnp.zeros((80, 512), BF)], 0)

    def back_hidden(c):
        lanes = slice(c * 512, (c + 1) * 512)
        row_part = dot(own_low, outer_w[lanes, :], NT).astype(BF)
        row_part = jnp.concatenate([row_part, jnp.zeros((112, 512), BF)], 0)

        def mask(i, carry):
            rows = tile(i, 256)
            spread = dot(expand[rows, :], row_part)
            hidden[rows, lanes] = jnp.where(hidden[rows, lanes] > 0, spread, 0.0).astype(BF)
            return carry

        lax.fori_loop(0, 4, mask, 0)
        for half in range(2):
            part = 2 * c + half
            columns = slice(part * 256, (part + 1) * 256)
            sums.fill(part, dot(normed_two_t[...], hidden[:, columns]))
        sums.after(c, 2 * c, 2 * c + 1)

    def back_middle(i, carry):
        rows = tile(i, 256)
        grad_normed = dot(hidden[rows, :], inner_w[...], NT)
        mid = middle[rows, :]
        scale = lax.rsqrt(jnp.mean(mid * mid, axis=1, keepdims=True) + EPSILON)
        small_ref[1:2, :] += jnp.sum(grad_normed * mid * scale, axis=0, keepdims=True)
        gained = grad_normed * gain_two_ref[...]
        mean = jnp.mean(gained * mid, axis=1, keepdims=True)
        grad_mid = dot(expand[rows, :], own_split) + scale * (gained - mid * scale * scale * mean)
        middle[rows, :] = grad_mid
        rounded = grad_mid.astype(BF)
        mixed[rows, :] = rounded
        grad_mixed[rows, :] = dot(rounded, output_w[...], NT).astype(BF)
        return carry

    for c in range(4):
        back_hidden(c)
    for i in range(2):
        lax.fori_loop(2 * i, 2 * i + 2, back_middle, 0)
        sums.after(4 + 2 * i)
        sums.after(5 + 2 * i)
    for half in range(2):
        sums.fill(8 + half, dot(mixed_t[...], mixed[:, half * 256 : (half + 1) * 256]))
    widen_hidden(1, 0, start=False)
    widen_hidden(1, 1, start=True)
    sums.after(8, 8, 9)

    for i in range(4):
        store_rows(grad_query, layer_hbm, i, 2 + i).wait()
    bias[...] = jnp.zeros_like(bias)

    def attend_back(g, b, r, carry):
        own, near, _, offset = window(r, b)
        lanes = slice(g * 256, (g + 1) * 256)
        grad_stack = stack_heads(grad_mixed[own, lanes])
        grad_soft = dot(grad_stack, values[near, lanes], NT)
        weight = soft(r, b, g)[...]
        parts = []
        for h in range(4):
            rows = slice(h * 128, (h + 1) * 128)
            soft_part = weight[rows].astype(F32)
            grad_part = grad_soft[rows]
            along = jnp.sum(soft_part * grad_part, axis=1, keepdims=True)
            part = (soft_part * (grad_part - along)).astype(BF)
            bias[g * 4 + h, :, offset] += part.astype(F32)
            parts.append(part)
        stacked = jnp.concatenate(parts, 0)
        grad_query[own, lanes] = pick_heads(dot(stacked, keys[near, lanes])).astype(BF)
        key_total[near, :] += dot(stacked, stack_heads(queries[own, lanes]), TN)
        value_total[near, :] += dot(weight, grad_stack, TN)
        return carry

    for g in range(2):
        lanes = slice(g * 256, (g + 1) * 256)
        key_total[...] = jnp.zeros_like(key_total)
        value_total[...] = jnp.zeros_like(value_total)
        for b in range(4):
            lax.fori_loop(0, 2, functools.partial(attend_back, g, b), 0)
            sums.after(9 + 7 * g + b)
        part, piece = 10 + 3 * g, 13 + 7 * g
        sums.fill(part, dot(normed_one_t[...], grad_query[:, lanes]))
        sums.after(piece, part)
        grad_key[:, lanes] = key_total[...].astype(BF)
        sums.fill(part + 1, dot(normed_one_t[...], grad_key[:, lanes]))
        sums.after(piece + 1, part + 1)
        grad_value[:, lanes] = value_total[...].astype(BF)
        sums.fill(part + 2, dot(normed_one_t[...], grad_value[:, lanes]))
        sums.after(piece + 2, part + 2)
        if g == 0:
            widen_hidden(0, 1, start=False)
            swap_hidden(0, start=True)
    widen_hidden(1, 1, start=False)
    swap_hidden(0, start=False)
    swap_hidden(1, start=True)

    def back_tokens(i, carry):
        rows = tile(i, 256)
        grad_normed = (
            dot(grad_query[rows, :], query_w[...], NT)
            + dot(grad_key[rows, :], key_w[...], NT)
            + dot(grad_value[rows, :], value_w[...], NT)
        )
        x = tokens[rows, :].astype(F32)
        scale = lax.rsqrt(jnp.mean(x * x, axis=1, keepdims=True) + EPSILON)
        small_ref[0:1, :] += jnp.sum(grad_normed * x * scale, axis=0, keepdims=True)
        gained = grad_normed * gain_one_ref[...]
        mean = jnp.mean(gained * x, axis=1, keepdims=True)
        grad = middle[rows, :] + scale * (gained - x * scale * scale * mean)
        normed_one[rows, :] = grad.astype(BF)
        return carry

    for i in range(2):
        lax.fori_loop(2 * i, 2 * i + 2, back_tokens, 0)
        for j in (2 * i, 2 * i + 1):
            store_rows(normed_one, token_grad_hbm, j, 2 + j).start()
            sums.after(23 + j)
    mirror = (
        lax.broadcasted_iota(jnp.int32, (128, 128), 0)
        + lax.broadcasted_iota(jnp.int32, (128, 128), 1)
    )
    mirror = jnp.where(mirror == 127, 1.0, 0.0)
    diagonals = []
    for h in range(8):
        turned = exact_dot(mirror, bias[h])
        wide = jnp.concatenate([turned, jnp.zeros((128, FAR - NEAR), F32)], 1)
        wide = pltpu.roll(wide, 0, 1, stride=1, stride_axis=0)
        diagonals.append(jnp.sum(wide, axis=0, keepdims=True))
    buckets = exact_dot(jnp.concatenate(diagonals, 0), bucket_onehot(place_row - 255), NT)
    small_ref[8:16, :] = jnp.concatenate([buckets, jnp.zeros((8, 480), F32)], 1)
    sums.after(27)
    small_ref[6:7, :] = jnp.broadcast_to(loss, (1, 512))
    swap_hidden(1, start=False)
    save_grads.wait()
    for i in range(4):
        store_rows(normed_one, token_grad_hbm, i, 2 + i).wait()


def closing_kernel(
    layer_hbm,
    token_grad_hbm,
    sums_hbm,
    hidden_sum_hbm,
    rows_grad_hbm,
    small_ref,
    layer_out,
    token_out,
    gain_one_out,
    query_out,
    key_out,
    value_out,
    output_out,
    position_out,
    gain_two_out,
    inner_out,
    outer_out,
    loss_out,
    square_out,
    hidden_sum,
    rows_grad,
    hidden_low,
    outer_part,
    rows_part,
    units_part,
    load_sem,
    copy_sem,
    store_sem,
):
    pairs = []
    inner_units = 2048 // WIDE
    for unit in range(inner_units):
        pairs.append((units_part.at[unit], inner_out.at[:, pl.ds(unit * WIDE, WIDE)]))
    places = [(output_out, 0), (output_out, 256)]
    places += [(ref, g * 256) for g in range(2) for ref in (query_out, key_out, value_out)]
    for part, (ref, lane) in enumerate(places):
        for i in range(PER_PART):
            lanes = pl.ds(lane + i * WIDE, WIDE)
            pairs.append((units_part.at[inner_units + part * PER_PART + i], ref.at[:, lanes]))
    pairs += [(rows_part.at[0], layer_out), (rows_part.at[1], token_out)]
    copies = [
        pltpu.make_async_copy(source, target, copy_sem.at[i])
        for i, (source, target) in enumerate(pairs)
    ]
    pairs = [(rows_grad_hbm, rows_grad), (hidden_sum_hbm, hidden_sum)]
    pairs += [(sums_hbm.at[unit], units_part.at[unit]) for unit in range(UNITS)]
    pairs += [(layer_hbm, rows_part.at[0]), (token_grad_hbm, rows_part.at[1])]
    loads = [
        pltpu.make_async_copy(source, target, load_sem.at[i])
        for i, (source, target) in enumerate(pairs)
    ]
    quarter = UNITS // 4
    early = loads[2 : 2 + quarter]
    for load in early + loads[:2] + loads[2 + quarter :]:
        load.start()
    gain_one_out[...] = small_ref[0, :]
    gain_two_out[...] = small_ref[1, :]
    position_out[...] = small_ref[8:16, 0:32]
    loss_out[0] = jnp.max(small_ref[6:7, :])
    squares = jnp.sum(small_ref[2:5, :], axis=1, keepdims=True)
    valid = jnp.sum(small_ref[5:6, :], axis=1, keepdims=True)
    roots = jnp.sqrt(squares / valid)
    for i in range(3):
        square_out[i] = jnp.max(roots[i : i + 1, :])
    for i in range(quarter):
        loads[2 + i].wait()
        copies[i].start()
    loads[0].wait()
    loads[1].wait()
    hidden_low[...] = hidden_sum[...].reshape(512, 2048).astype(BF)
    grads = rows_grad[...].reshape(512, 512)
    stores = []
    for c in range(4):
        rows = pl.ds(c * 512, 512)
        outer_part[rows] = dot(hidden_low[:, c * 512 : (c + 1) * 512], grads, TN)
        store = pltpu.make_async_copy(outer_part.at[rows], outer_out.at[rows], store_sem.at[c])
        store.start()
        stores.append(store)
        for i in range(quarter * (c + 1), min(quarter * (c + 2), UNITS)):
            loads[2 + i].wait()
            copies[i].start()
    for i in (UNITS, UNITS + 1):
        loads[2 + i].wait()
        copies[i].start()
    for copy in copies + stores:
        copy.wait()


def fast_shards(
    tokens,
    segment_ids,
    positives,
    attention_gain,
    query_weight,
    key_weight,
    value_weight,
    output_weight,
    position_table,
    feedforward_gain,
    inner_weight,
    outer_weight,
):
    block_shape = tokens.shape
    anywhere = pl.BlockSpec(memory_space=pl.ANY)
    vmem = pl.BlockSpec(memory_space=pltpu.VMEM)
    smem = pl.BlockSpec(memory_space=pltpu.SMEM)
    shape = jax.ShapeDtypeStruct
    dma = pltpu.SemaphoreType.DMA
    low = functools.partial(pltpu.VMEM, dtype=BF)
    full = functools.partial(pltpu.VMEM, dtype=F32)
    outs = pl.pallas_call(
        layer_kernel,
        out_shape=[
            shape((1024, 512), BF),
            shape((1024, 512), BF),
            shape((UNITS, 512, WIDE), F32),
            shape((2, 2, 4, 2, 2, 8, 2048), F32),
            shape((2, 2, 128, 512), BF),
            shape((16, 512), F32),
        ],
        in_specs=[anywhere, vmem, smem, vmem]
        + [anywhere] * 4
        + [vmem, vmem, anywhere, anywhere],
        out_specs=[anywhere] * 5 + [vmem],
        scratch_shapes=[
            low((1024, 512)),
            low((512, 512)),
            low((512, 512)),
            low((512, 512)),
            low((512, 512)),
            low((512, 2048)),
            low((2048, 512)),
            low((1024, 512)),
            low((1024, 512)),
            low((1024, 512)),
            low((1024, 512)),
            low((2, 2, 2, 512, 384)),
            low((2, 2, 2, 512, 256)),
            low((1024, 512)),
            full((1024, 512)),
            low((1024, 512)),
            low((1024, 2048)),
            full((8, 128, NEAR)),
            full((1024, 128)),
            full((2, 512)),
            full((2, 2, 4, 4, 8, 640)),
            full((2, 8, 2048)),
            low((512, 1024)),
            low((512, 1024)),
            low((512, 1024)),
            low((1024, 512)),
            low((1024, 512)),
            low((1024, 512)),
            low((1024, 512)),
            full((1024, 256)),
            full((1024, 256)),
            full((UNITS, 512, WIDE)),
            full((UNITS, 496, WIDE)),
            low((1024, 128)),
            low((2, 2, 128, 512)),
            full((5, 16, 512)),
            dma((7,)),
            dma((7,)),
            dma((12, UNITS)),
            dma((12, UNITS)),
            dma((UNITS,)),
            dma((2, 7)),
            dma((2, 7)),
            dma((2, 8)),
            dma((2, 8)),
            dma((5,)),
            dma((5,)),
            dma((4, 3)),
            dma((4, 3)),
        ],
        compiler_params=pltpu.CompilerParams(
            collective_id=0, has_side_effects=True, vmem_limit_bytes=63 * 2**20
        ),
    )(
        tokens.reshape(1024, 512),
        segment_ids.reshape(2, 512),
        positives,
        attention_gain.reshape(1, 512),
        query_weight,
        key_weight,
        value_weight,
        output_weight,
        position_table.T,
        feedforward_gain.reshape(1, 512),
        inner_weight,
        outer_weight,
    )
    results = pl.pallas_call(
        closing_kernel,
        out_shape=[
            shape((1024, 512), BF),
            shape((1024, 512), BF),
            shape((512,), F32),
            shape((512, 512), F32),
            shape((512, 512), F32),
            shape((512, 512), F32),
            shape((512, 512), F32),
            shape((8, 32), F32),
            shape((512,), F32),
            shape((512, 2048), F32),
            shape((2048, 512), F32),
            shape((1,), F32),
            shape((3,), F32),
        ],
        in_specs=[anywhere] * 5 + [vmem],
        out_specs=[anywhere, anywhere, vmem]
        + [anywhere] * 4
        + [vmem, vmem, anywhere, anywhere, smem, smem],
        scratch_shapes=[
            full((2, 2, 4, 2, 2, 8, 2048)),
            low((2, 2, 128, 512)),
            low((512, 2048)),
            full((2048, 512)),
            low((2, 1024, 512)),
            full((UNITS, 512, WIDE)),
            dma((UNITS + 4,)),
            dma((UNITS + 2,)),
            dma((4,)),
        ],
        compiler_params=pltpu.CompilerParams(vmem_limit_bytes=60 * 2**20),
    )(*outs)
    layer, token_grad, *rest = results
    return (
        layer.reshape(block_shape),
        token_grad.reshape(block_shape),
        *rest[:5],
        rest[5].T,
        *rest[6:9],
        rest[9].reshape(()),
        rest[10],
    )


def solution(mesh):
    fast = mesh.shape["tower"] == 2 and mesh.shape["rows"] == 16
    return jax.shard_map(
        fast_shards if fast else shards,
        mesh=mesh,
        in_specs=(
            P("tower", "rows", None, None),
            P("tower", "rows", None),
            P("rows"),
            P(),
            P(),
            P(),
            P(),
            P(),
            P(),
            P(),
            P(),
            P(),
        ),
        out_specs=(
            P("tower", "rows", None, None),
            P("tower", "rows", None, None),
            P(),
            P(),
            P(),
            P(),
            P(),
            P(),
            P(),
            P(),
            P(),
            P(),
            P(),
        ),
        check_vma=False,
    )
```
